32 devices in a mesh: mp: 4 (over x, core), dp: 8 (over z, y).
Axes of the slice: x: 2, y: 2, z: 4, core: 2. Of those that a mesh axis runs over, the one named last changes fastest.
Arguments:
- targets: bfloat16 [32, 256, 768], P('dp'), may hold values from -6 to 6
- memory: bfloat16 [32, 1024, 768], P('dp'), may hold values from -6 to 6
- cotangent: bfloat16 [32, 256, 768], P('dp'), may hold values from -6 to 6
- target_len: int32 [32], P('dp'), may hold values from 32 to 256, as said below
- memory_len: int32 [32], P('dp'), may hold values from 128 to 1024, as said below
- query_self: bfloat16 [768, 768], P(None, 'mp'), may hold values from -0.0546875 to 0.0546875
- key_self: bfloat16 [768, 768], P(None, 'mp'), may hold values from -0.21875 to 0.21875
- value_self: bfloat16 [768, 768], P(None, 'mp'), may hold values from -0.21875 to 0.21875
- out_self: bfloat16 [768, 768], P('mp'), may hold values from -1.75 to 1.75
- query_cross: bfloat16 [768, 768], P(None, 'mp'), may hold values from -0.0546875 to 0.0546875
- key_cross: bfloat16 [768, 768], P(None, 'mp'), may hold values from -0.21875 to 0.21875
- value_cross: bfloat16 [768, 768], P(None, 'mp'), may hold values from -0.21875 to 0.21875
- out_cross: bfloat16 [768, 768], P('mp'), may hold values from -1.75 to 1.75
- gate_proj: bfloat16 [768, 2048], P(None, 'mp'), may hold values from -0.21875 to 0.21875
- up_proj: bfloat16 [768, 2048], P(None, 'mp'), may hold values from -0.21875 to 0.21875
- down_proj: bfloat16 [2048, 768], P('mp'), may hold values from -0.1875 to 0.1875
- gain_self: float32 [768], replicated, may hold values from 0.5 to 1.5
- gain_cross: float32 [768], replicated, may hold values from 0.5 to 1.5
- gain_ffn: float32 [768], replicated, may hold values from 0.5 to 1.5
- pos_bias: float32 [32, 12], P(None, 'mp'), may hold values from -4 to 4
Outputs:
- output: bfloat16 [32, 256, 768], P('dp', 'mp')
- grad_targets: bfloat16 [32, 256, 768], P('dp', 'mp')
- grad_memory: bfloat16 [32, 1024, 768], P('dp', 'mp')
- grad_query_self: float32 [768, 768], P('dp', 'mp')
- grad_key_self: float32 [768, 768], P('dp', 'mp')
- grad_value_self: float32 [768, 768], P('dp', 'mp')
- grad_out_self: float32 [768, 768], P('mp', 'dp')
- grad_query_cross: float32 [768, 768], P('dp', 'mp')
- grad_key_cross: float32 [768, 768], P('dp', 'mp')
- grad_value_cross: float32 [768, 768], P('dp', 'mp')
- grad_out_cross: float32 [768, 768], P('mp', 'dp')
- grad_gate: float32 [768, 2048], P('dp', 'mp')
- grad_up: float32 [768, 2048], P('dp', 'mp')
- grad_down: float32 [2048, 768], P('mp', 'dp')
- grad_gain_self: float32 [768], P('dp')
- grad_gain_cross: float32 [768], P('dp')
- grad_gain_ffn: float32 [768], P('dp')
- grad_pos_bias: float32 [32, 12], P(None, 'mp')
The draws below stay inside these ranges and needn't reach their ends.
Inputs may be any that keep to these rules, and one draw needn't show every extreme that they name: `target_len`: some sequence has exactly 256 target positions and another exactly 32, in every draw. `memory_len`: some sequence has exactly 1024 memory slots and another exactly 128, in every draw.
All inputs are finite; a program needn't handle non-finite values.
Results may differ from the reference program's by a relative error of at most 0.025.
The reference program's roundings to bfloat16 on the way count: a program that leaves them out, or rounds other values in their place, can miss the bound.
Values may be sent and summed in bfloat16 or wider, within the bound.
A program may use at most 192 MiB of HBM per device.

```python
import jax
import jax.numpy as jnp
import numpy as np
from jax import lax

D = 768
HEADS = 12
HEAD_DIM = 64
FF = 2048
BUCKETS = 32
MAX_DIST = 128
TGT = 256
MEM = 1024
SEQ_DEV = 4
SEQS = 32
INNER = 768


def bounded_lengths(key, number, largest):
    lengths = jax.random.randint(key, (number,), largest // 8, largest + 1)
    long_slot = jax.random.randint(jax.random.fold_in(key, 1), (), 0, number)
    short_slot = (long_slot + 1 + jax.random.randint(jax.random.fold_in(key, 2), (), 0, number - 1)) % number
    slots = jnp.arange(number)
    lengths = jnp.where(slots == long_slot, largest, lengths)
    return jnp.where(slots == short_slot, largest // 8, lengths).astype(jnp.int32)


def draw_target_len(key, part):
    key = jax.random.fold_in(key, 11)
    return bounded_lengths(key, SEQS, TGT)


def draw_memory_len(key, part):
    key = jax.random.fold_in(key, 23)
    return bounded_lengths(key, SEQS, MEM)


def block_levels(rng, dims, split, low, top_value):
    loudness, own = 1.0, jax.random.fold_in(rng, 6)
    for axis_at, parts in split:
        heights = jnp.exp(jax.random.uniform(jax.random.fold_in(own, axis_at), (parts,), jnp.float32, low / len(split), top_value / len(split)))
        loudness = loudness * jnp.repeat(heights, dims[axis_at] // parts).reshape([-1 if axis == axis_at else 1 for axis in range(len(dims))])
    return loudness


def normal_values(own_key, dims, deviation, limit, shards=(), kind=jnp.bfloat16):
    values = deviation * jax.random.normal(own_key, dims, jnp.float32)
    if shards:
        values = values * block_levels(own_key, dims, shards, -0.22, 0.18)
    return jnp.clip(values, -limit, limit).astype(kind)


def setup_inputs(seed: int = 0) -> dict:
    key_list = jax.random.split(jax.random.key(seed), 21)
    targets = normal_values(key_list[0], (SEQS, TGT, D), 1.0, 6.0, ((0, 8),))
    memory = normal_values(key_list[1], (SEQS, MEM, D), 1.0, 6.0, ((0, 8),))
    cotangent = normal_values(key_list[2], (SEQS, TGT, D), 1.0, 6.0, ((0, 8),))
    target_len = draw_target_len(jax.random.fold_in(key_list[20], 71), 0)
    memory_len = draw_memory_len(jax.random.fold_in(key_list[20], 71), 0)
    query_self = normal_values(key_list[5], (D, INNER), (16 * D) ** -0.5, 0.0546875, ((1, 4),))
    key_self = normal_values(key_list[6], (D, INNER), D ** -0.5, 0.21875, ((1, 4),))
    value_self = normal_values(key_list[7], (D, INNER), D ** -0.5, 0.21875, ((1, 4),))
    out_self = normal_values(key_list[8], (INNER, D), (max(INNER // 64, 1)) ** -0.5, 1.75, ((0, 4),))
    query_cross = normal_values(key_list[9], (D, INNER), (16 * D) ** -0.5, 0.0546875, ((1, 4),))
    key_cross = normal_values(key_list[10], (D, INNER), D ** -0.5, 0.21875, ((1, 4),))
    value_cross = normal_values(key_list[11], (D, INNER), D ** -0.5, 0.21875, ((1, 4),))
    out_cross = normal_values(key_list[12], (INNER, D), (max(INNER // 64, 1)) ** -0.5, 1.75, ((0, 4),))
    gate_proj = normal_values(key_list[13], (D, FF), D ** -0.5, 0.21875, ((1, 4),))
    up_proj = normal_values(key_list[14], (D, FF), D ** -0.5, 0.21875, ((1, 4),))
    down_proj = normal_values(key_list[15], (FF, D), (FF // 2) ** -0.5, 0.1875, ((0, 4),))
    gain_self = jnp.clip(1.0 + 0.1 * jax.random.normal(key_list[16], (D,), jnp.float32), 0.5, 1.5)
    gain_cross = jnp.clip(1.0 + 0.1 * jax.random.normal(key_list[17], (D,), jnp.float32), 0.5, 1.5)
    gain_ffn = jnp.clip(1.0 + 0.1 * jax.random.normal(key_list[18], (D,), jnp.float32), 0.5, 1.5)
    pos_bias = normal_values(key_list[19], (BUCKETS, HEADS), 1.0, 4.0, ((1, 4),), jnp.float32)
    return dict(targets=targets, memory=memory, cotangent=cotangent, target_len=target_len, memory_len=memory_len, query_self=query_self, key_self=key_self, value_self=value_self, out_self=out_self, query_cross=query_cross, key_cross=key_cross, value_cross=value_cross, out_cross=out_cross, gate_proj=gate_proj, up_proj=up_proj, down_proj=down_proj, gain_self=gain_self, gain_cross=gain_cross, gain_ffn=gain_ffn, pos_bias=pos_bias)


EPS = 1e-06
NEG = -1000000000.0

@jax.custom_vjp
def low(v):
    return lax.optimization_barrier(v.astype(jnp.bfloat16)).astype(jnp.float32)

@jax.custom_vjp
def low_back(v):
    return v

def low_keep(v):
    return (low(v), None)

def low_pass(kept, grad):
    return (grad,)

def back_keep(v):
    return (v, None)

def back_low(kept, grad):
    return (low(grad),)
low.defvjp(low_keep, low_pass)
low_back.defvjp(back_keep, back_low)

def bucket_table(length):
    distance = np.maximum(np.arange(length)[:, None] - np.arange(length)[None, :], 0)
    exact = BUCKETS // 2
    scaled = exact + (np.log(np.maximum(distance, 1) / exact) / np.log(MAX_DIST / exact) * (BUCKETS - exact)).astype(np.int32)
    return np.where(distance < exact, distance, np.minimum(scaled, BUCKETS - 1)).astype(np.int32)

def matmul(inputs, weight):
    return jnp.einsum('bld,df->blf', inputs, weight, precision=lax.Precision.HIGHEST)

def rms_norm(resid, gain):
    return resid * lax.rsqrt(lax.optimization_barrier(jnp.mean(resid * resid, -1, keepdims=True)) + EPS) * gain

def rounded(value):
    return low(low_back(value))

def attention(queries, keys, values, score_bias, valid):
    scores = low_back(jnp.einsum('bihe,bjhe->bhij', queries, keys, precision=lax.Precision.HIGHEST) + score_bias)
    scores = jnp.where(valid, scores, NEG)
    attn_probs = low(jax.nn.softmax(scores, axis=-1))
    return jnp.einsum('bhij,bjhe->bihe', attn_probs, values, precision=lax.Precision.HIGHEST)

def layer(weights, resid0, memory, target_len, memory_len):
    query_self, key_self, value_self, out_self, query_cross, key_cross, value_cross, out_cross, gate_proj, up_proj, down_proj, gain_self, gain_cross, gain_ffn, pos_bias = weights
    length = resid0.shape[1]
    heads = query_self.shape[1] // HEAD_DIM

    def split_heads(value):
        return value.reshape(value.shape[0], value.shape[1], heads, HEAD_DIM)

    def merge_heads(value):
        return value.reshape(value.shape[0], value.shape[1], heads * HEAD_DIM)
    positions = jnp.arange(length)
    self_valid = ((positions[None, :] <= positions[:, None])[None] & (positions[None, None, :] < target_len[:, None, None]))[:, None]
    mem_positions = jnp.arange(memory.shape[1])
    cross_valid = (mem_positions[None, :] < memory_len[:, None])[:, None, None, :]
    score_bias = pos_bias[jnp.asarray(bucket_table(length))].transpose(2, 0, 1)[None]
    normed = low(rms_norm(resid0, gain_self))
    queries = split_heads(rounded(matmul(normed, query_self)))
    keys = split_heads(rounded(matmul(normed, key_self)))
    values = split_heads(rounded(matmul(normed, value_self)))
    mixed = low(low_back(merge_heads(attention(queries, keys, values, score_bias, self_valid))))
    resid1 = resid0 + low_back(matmul(mixed, out_self))
    normed_two = low(rms_norm(resid1, gain_cross))
    queries_two = split_heads(rounded(matmul(normed_two, query_cross)))
    mem_keys = split_heads(rounded(matmul(memory, key_cross)))
    mem_values = split_heads(rounded(matmul(memory, value_cross)))
    mixed_two = low(low_back(merge_heads(attention(queries_two, mem_keys, mem_values, 0.0, cross_valid))))
    resid2 = resid1 + low_back(matmul(mixed_two, out_cross))
    normed_three = low(rms_norm(resid2, gain_ffn))
    gate_pre = low_back(matmul(normed_three, gate_proj))
    up_pre = low_back(matmul(normed_three, up_proj))
    hidden = low(jax.nn.gelu(gate_pre, approximate=True) * up_pre)
    return resid2 + low_back(matmul(hidden, down_proj))

def reference(targets, memory, cotangent, target_len, memory_len, query_self, key_self, value_self, out_self, query_cross, key_cross, value_cross, out_cross, gate_proj, up_proj, down_proj, gain_self, gain_cross, gain_ffn, pos_bias):
    weights = tuple((item.astype(jnp.float32) for item in (query_self, key_self, value_self, out_self, query_cross, key_cross, value_cross, out_cross, gate_proj, up_proj, down_proj, gain_self, gain_cross, gain_ffn, pos_bias)))
    groups = targets.shape[0] // SEQ_DEV

    def regroup(value):
        return value.reshape((groups, SEQ_DEV) + value.shape[1:])
    batches = (regroup(targets), regroup(memory), regroup(cotangent), regroup(target_len), regroup(memory_len))

    def step(totals, batch):
        tgt_rows, mem_rows, cot_rows, tgt_lens, mem_lens = batch

        def forward(weight_list, resid, mem_in):
            return layer(weight_list, resid, mem_in, tgt_lens, mem_lens)
        result, pull = jax.vjp(forward, weights, tgt_rows.astype(jnp.float32), mem_rows.astype(jnp.float32))
        grad_weights, grad_rows, grad_mem = pull(cot_rows.astype(jnp.float32))
        totals = jax.tree.map(lambda earlier, added: earlier + added, totals, grad_weights)
        return (totals, (result.astype(jnp.bfloat16), grad_rows.astype(jnp.bfloat16), grad_mem.astype(jnp.bfloat16)))
    start = jax.tree.map(jnp.zeros_like, weights)
    totals, (outputs, grad_rows, grad_mem) = lax.scan(step, start, batches)
    return (outputs.reshape(targets.shape), grad_rows.reshape(targets.shape), grad_mem.reshape(memory.shape), totals[0], totals[1], totals[2], totals[3], totals[4], totals[5], totals[6], totals[7], totals[8], totals[9], totals[10], totals[11], totals[12], totals[13], totals[14])
```

```python
import jax
import jax.numpy as jnp
import numpy as np
from jax import lax
from jax.sharding import PartitionSpec as P

HEAD_DIM = 64
BUCKETS = 32
MAX_DIST = 128


EPS = 1e-06
NEG = -1000000000.0


def bucket_table(length):
    distance = np.maximum(np.arange(length)[:, None] - np.arange(length)[None, :], 0)
    exact = BUCKETS // 2
    scaled = exact + (
        np.log(np.maximum(distance, 1) / exact) / np.log(MAX_DIST / exact) * (BUCKETS - exact)
    ).astype(np.int32)
    return np.where(distance < exact, distance, np.minimum(scaled, BUCKETS - 1)).astype(np.int32)


def project(inputs, weight):
    return jnp.einsum("bld,df->blf", inputs, weight, preferred_element_type=jnp.float32)


def back_project(gradient, weight):
    return jnp.einsum("blf,df->bld", gradient, weight, preferred_element_type=jnp.float32)


def weight_grad(inputs, gradient):
    return jnp.einsum("bld,blf->df", inputs, gradient, preferred_element_type=jnp.float32)


def norm_forward(resid, gain):
    inv_rms = lax.rsqrt(jnp.mean(resid * resid, -1, keepdims=True) + EPS)
    return (resid * inv_rms * gain, inv_rms)


def norm_backward(resid, inv_rms, gain, grad_normed):
    unit_rows = resid * inv_rms
    grad_gain = jnp.sum(grad_normed * unit_rows, axis=(0, 1))
    weighted = grad_normed * gain
    grad_resid = inv_rms * (
        weighted - unit_rows * jnp.mean(weighted * unit_rows, -1, keepdims=True)
    )
    return (grad_resid, grad_gain)


def scores_of(queries, keys, score_bias, valid):
    scores = (
        jnp.einsum("bihe,bjhe->bhij", queries, keys, preferred_element_type=jnp.float32)
        + score_bias
    )
    return jnp.where(valid, scores, NEG)


def attend(queries, keys, values, score_bias, valid):
    scores = scores_of(queries, keys, score_bias, valid)
    row_max = jnp.max(scores, -1, keepdims=True)
    log_total = row_max + jnp.log(jnp.sum(jnp.exp(scores - row_max), -1, keepdims=True))
    attn_probs = jnp.exp(scores - log_total).astype(jnp.bfloat16)
    mixed = jnp.einsum("bhij,bjhe->bihe", attn_probs, values, preferred_element_type=jnp.float32)
    return (mixed, log_total)


def attend_back(queries, keys, values, score_bias, valid, log_total, grad_mixed):
    attn_probs = jnp.exp(scores_of(queries, keys, score_bias, valid) - log_total)
    grad_values = jnp.einsum(
        "bhij,bihe->bjhe",
        attn_probs.astype(jnp.bfloat16),
        grad_mixed,
        preferred_element_type=jnp.float32,
    )
    grad_probs = jnp.einsum(
        "bihe,bjhe->bhij", grad_mixed, values, preferred_element_type=jnp.float32
    )
    grad_scores = attn_probs * (grad_probs - jnp.sum(attn_probs * grad_probs, -1, keepdims=True))
    grad_low = grad_scores.astype(jnp.bfloat16)
    grad_queries = jnp.einsum("bhij,bjhe->bihe", grad_low, keys, preferred_element_type=jnp.float32)
    grad_keys = jnp.einsum("bhij,bihe->bjhe", grad_low, queries, preferred_element_type=jnp.float32)
    return (grad_queries, grad_keys, grad_values, grad_low)


def swap(value, axis, bit):
    return lax.ppermute(value, axis, [(i, i ^ bit) for i in range(lax.axis_size(axis))])


def bits_of(axis):
    return [1 << i for i in range(lax.axis_size(axis).bit_length() - 1)]


def split_bits(value, axis, dim):
    steps = len(bits_of(axis))
    shape = value.shape
    return value.reshape(
        shape[:dim] + (2,) * steps + (shape[dim] >> steps,) + shape[dim + 1 :]
    )


def own_bit(axis, bit):
    return (lax.axis_index(axis) & bit) // bit


def halve(value, axis, bit, dim):
    mine = own_bit(axis, bit)
    kept = lax.dynamic_index_in_dim(value, mine, dim, keepdims=False)
    sent = lax.dynamic_index_in_dim(value, 1 - mine, dim, keepdims=False)
    arrived = swap(sent.astype(jnp.bfloat16), axis, bit)
    return kept + arrived.astype(jnp.float32)


def reduce_scatter(value, axis, dim):
    bits = bits_of(axis)
    value = split_bits(value, axis, dim)
    for at, bit in enumerate(bits):
        value = halve(value, axis, bit, dim + len(bits) - 1 - at)
    return value


def gather_mp(value):
    value = value[None]
    for bit in reversed(bits_of("mp")):
        other = swap(value, "mp", bit)
        first = own_bit("mp", bit) == 0
        low = jnp.where(first, value, other)
        high = jnp.where(first, other, value)
        value = jnp.stack([low, high], 1 if bit == 1 else 0)
        value = value.reshape((-1,) + value.shape[2:])
    return value


def exchange_mp(value):
    count = lax.axis_size("mp")
    value = split_bits(value, "mp", 0)[None]
    steps = len(bits_of("mp"))
    for at, bit in enumerate(bits_of("mp")):
        dim = steps - at
        mine = own_bit("mp", bit)
        kept = lax.dynamic_index_in_dim(value, mine, dim, keepdims=False)
        sent = lax.dynamic_index_in_dim(value, 1 - mine, dim, keepdims=False)
        arrived = swap(sent, "mp", bit)
        first = mine == 0
        low = jnp.where(first, kept, arrived)
        high = jnp.where(first, arrived, kept)
        value = jnp.stack([low, high], 0)
        value = value.reshape((-1,) + value.shape[2:])
    return value.reshape((count,) + value.shape[1:])


def sum_mp(value):
    for bit in bits_of("mp"):
        value = value + swap(value, "mp", bit)
    return value


def on_device(
    targets,
    memory,
    cotangent,
    target_len,
    memory_len,
    query_self,
    key_self,
    value_self,
    out_self,
    query_cross,
    key_cross,
    value_cross,
    out_cross,
    gate_proj,
    up_proj,
    down_proj,
    gain_self,
    gain_cross,
    gain_ffn,
    pos_bias,
):
    length = targets.shape[1]
    heads_local = query_self.shape[1] // HEAD_DIM
    mp_size = lax.axis_size("mp")
    dp_size = lax.axis_size("dp")
    mp_index = lax.axis_index("mp")
    row_share = length // mp_size
    width = targets.shape[2]

    def split_heads(value):
        return value.reshape(value.shape[0], value.shape[1], -1, HEAD_DIM)

    def merge_heads(value):
        return value.reshape(value.shape[0], value.shape[1], -1)

    def my_rows(value):
        return lax.dynamic_slice_in_dim(value, mp_index * row_share, row_share, 1)

    def mine(value):
        return lax.dynamic_index_in_dim(value, mp_index, 0)

    positions = jnp.arange(length)
    self_valid = (
        (positions[None, :] <= positions[:, None])[None]
        & (positions[None, None, :] < target_len[:, None, None])
    )[:, None]
    mem_positions = jnp.arange(memory.shape[1])
    cross_valid = (mem_positions[None, :] < mine(memory_len)[:, None])[:, None, None, :]
    onehot = (
        jnp.asarray(bucket_table(length)).reshape(-1)[:, None] == jnp.arange(BUCKETS)[None, :]
    ).astype(jnp.float32)
    score_bias = (
        jnp.dot(onehot, pos_bias, precision=lax.Precision.HIGHEST)
        .reshape(length, length, heads_local)
        .transpose(2, 0, 1)[None]
    )
    cross_in = gather_mp(jnp.stack([query_cross, key_cross, value_cross]))
    cross_in = cross_in.transpose(1, 2, 0, 3).reshape(3, width, -1)
    cross_q, cross_k, cross_v = cross_in[0], cross_in[1], cross_in[2]
    cross_o = gather_mp(out_cross).reshape(-1, width)

    resid0 = targets.astype(jnp.float32)
    normed_one, inv_one = norm_forward(resid0, gain_self)
    normed_one = normed_one.astype(jnp.bfloat16)
    queries = split_heads(project(normed_one, query_self).astype(jnp.bfloat16))
    keys = split_heads(project(normed_one, key_self).astype(jnp.bfloat16))
    values = split_heads(project(normed_one, value_self).astype(jnp.bfloat16))
    mixed, log_one = attend(queries, keys, values, score_bias, self_valid)
    mixed = merge_heads(mixed).astype(jnp.bfloat16)
    resid1 = mine(resid0) + reduce_scatter(project(mixed, out_self), "mp", 0)

    mem_own = mine(memory)
    normed_two, inv_two = norm_forward(resid1, gain_cross)
    normed_two = normed_two.astype(jnp.bfloat16)
    queries_two = split_heads(project(normed_two, cross_q).astype(jnp.bfloat16))
    mem_keys = split_heads(project(mem_own, cross_k).astype(jnp.bfloat16))
    mem_values = split_heads(project(mem_own, cross_v).astype(jnp.bfloat16))
    mixed_two, log_two = attend(queries_two, mem_keys, mem_values, 0.0, cross_valid)
    mixed_two = merge_heads(mixed_two).astype(jnp.bfloat16)
    resid2 = resid1 + project(mixed_two, cross_o)
    normed_three, inv_three = norm_forward(resid2, gain_ffn)
    normed_all = gather_mp(normed_three.astype(jnp.bfloat16)[0])

    gate_pre = project(normed_all, gate_proj)
    up_pre = project(normed_all, up_proj)

    def gated(gate_in, up_in):
        return jax.nn.gelu(gate_in, approximate=True) * up_in

    hidden, hidden_pull = jax.vjp(gated, gate_pre, up_pre)
    hidden = hidden.astype(jnp.bfloat16)
    grad_gate_pre, grad_up_pre = hidden_pull(back_project(cotangent, down_proj))
    grad_gate_pre = grad_gate_pre.astype(jnp.bfloat16)
    grad_up_pre = grad_up_pre.astype(jnp.bfloat16)
    grad_normed = reduce_scatter(
        back_project(grad_gate_pre, gate_proj) + back_project(grad_up_pre, up_proj), "mp", 0
    )
    result = project(hidden, down_proj)
    own = (jnp.arange(targets.shape[0]) == mp_index)[:, None, None]
    result = result + jnp.where(own, resid2, 0.0)
    output = reduce_scatter(result, "mp", 1).astype(jnp.bfloat16)
    ffn_grads = jnp.concatenate(
        [
            weight_grad(normed_all, grad_gate_pre),
            weight_grad(normed_all, grad_up_pre),
            weight_grad(cotangent, hidden),
        ],
        1,
    )
    ffn_grads = reduce_scatter(ffn_grads, "dp", 0)
    grad_resid, grad_gain_ffn = norm_backward(resid2, inv_three, gain_ffn, grad_normed)
    grad_two = mine(cotangent).astype(jnp.float32) + grad_resid

    branch_two = grad_two.astype(jnp.bfloat16)
    grad_mixed_two = split_heads(back_project(branch_two, cross_o).astype(jnp.bfloat16))
    grad_q_two, grad_mem_keys, grad_mem_values, _ = attend_back(
        queries_two, mem_keys, mem_values, 0.0, cross_valid, log_two, grad_mixed_two
    )
    grad_q_two = merge_heads(grad_q_two).astype(jnp.bfloat16)
    grad_normed = back_project(grad_q_two, cross_q)
    grad_resid, grad_gain_cross = norm_backward(resid1, inv_two, gain_cross, grad_normed)
    grad_one = grad_two + grad_resid
    branch_one = gather_mp(grad_one.astype(jnp.bfloat16)[0])
    grad_mem_keys = merge_heads(grad_mem_keys).astype(jnp.bfloat16)
    grad_mem_values = merge_heads(grad_mem_values).astype(jnp.bfloat16)
    mem_grad = back_project(grad_mem_keys, cross_k) + back_project(grad_mem_values, cross_v)
    mem_rows = exchange_mp(mem_grad[0].astype(jnp.bfloat16))
    cross_grads = jnp.stack(
        [
            weight_grad(normed_two, grad_q_two),
            weight_grad(mem_own, grad_mem_keys),
            weight_grad(mem_own, grad_mem_values),
            weight_grad(branch_two, mixed_two),
        ],
        1,
    )
    cross_grads = reduce_scatter(cross_grads, "mp", 2)
    cross_grads = reduce_scatter(cross_grads, "dp", 0)

    grad_mixed = split_heads(back_project(branch_one, out_self).astype(jnp.bfloat16))
    grad_q_one, grad_k_one, grad_v_one, grad_scores = attend_back(
        queries, keys, values, score_bias, self_valid, log_one, grad_mixed
    )
    grad_q_one = merge_heads(grad_q_one).astype(jnp.bfloat16)
    grad_k_one = merge_heads(grad_k_one).astype(jnp.bfloat16)
    grad_v_one = merge_heads(grad_v_one).astype(jnp.bfloat16)
    score_total = jnp.sum(grad_scores.astype(jnp.float32), 0).reshape(heads_local, length * length)
    bias_local = jnp.dot(score_total, onehot, precision=lax.Precision.HIGHEST).T
    grad_normed = (
        back_project(grad_q_one, query_self)
        + back_project(grad_k_one, key_self)
        + back_project(grad_v_one, value_self)
    )
    gains = jnp.stack(
        [
            jnp.sum(grad_normed * (resid0 * inv_one), axis=(0, 1)),
            grad_gain_cross,
            grad_gain_ffn,
        ]
    )
    gains = sum_mp(gains)
    share = width // dp_size
    bias_columns = jnp.tile(bias_local.reshape(share, -1), (dp_size, 1))
    self_grads = jnp.concatenate(
        [
            weight_grad(normed_one, grad_q_one),
            weight_grad(normed_one, grad_k_one),
            weight_grad(normed_one, grad_v_one),
            weight_grad(branch_one, mixed),
            gains.T,
            bias_columns,
        ],
        1,
    )
    self_grads = reduce_scatter(self_grads, "dp", 0)
    grad_normed = reduce_scatter(grad_normed, "mp", 1)
    grad_resid, _ = norm_backward(my_rows(resid0), my_rows(inv_one), gain_self, grad_normed)
    grad_targets = (my_rows(branch_one).astype(jnp.float32) + grad_resid).astype(jnp.bfloat16)

    part = query_self.shape[1]
    units = gate_proj.shape[1]
    gains_at = 4 * part
    return (
        output,
        grad_targets,
        mem_rows,
        self_grads[:, :part],
        self_grads[:, part : 2 * part],
        self_grads[:, 2 * part : 3 * part],
        self_grads[:, 3 * part : 4 * part].T,
        cross_grads[:, 0],
        cross_grads[:, 1],
        cross_grads[:, 2],
        cross_grads[:, 3].T,
        ffn_grads[:, :units],
        ffn_grads[:, units : 2 * units],
        ffn_grads[:, 2 * units :].T,
        self_grads[:, gains_at],
        self_grads[:, gains_at + 1],
        self_grads[:, gains_at + 2],
        self_grads[:, gains_at + 3 :].reshape(bias_local.shape),
    )


def solution(mesh):
    return jax.shard_map(
        on_device,
        mesh=mesh,
        in_specs=(
            P("dp", None, None),
            P("dp", None, None),
            P("dp", None, None),
            P("dp"),
            P("dp"),
            P(None, "mp"),
            P(None, "mp"),
            P(None, "mp"),
            P("mp", None),
            P(None, "mp"),
            P(None, "mp"),
            P(None, "mp"),
            P("mp", None),
            P(None, "mp"),
            P(None, "mp"),
            P("mp", None),
            P(),
            P(),
            P(),
            P(None, "mp"),
        ),
        out_specs=(
            P("dp", "mp", None),
            P("dp", "mp", None),
            P("dp", "mp", None),
            P("dp", "mp"),
            P("dp", "mp"),
            P("dp", "mp"),
            P("mp", "dp"),
            P("dp", "mp"),
            P("dp", "mp"),
            P("dp", "mp"),
            P("mp", "dp"),
            P("dp", "mp"),
            P("dp", "mp"),
            P("mp", "dp"),
            P("dp"),
            P("dp"),
            P("dp"),
            P(None, "mp"),
        ),
        check_vma=False,
    )
```

```python
import jax
import jax.numpy as jnp
import numpy as np
from jax import lax
from jax.experimental import pallas as pl
from jax.experimental.pallas import tpu as pltpu
from jax.sharding import PartitionSpec as P

HEAD_DIM = 64
BUCKETS = 32
MAX_DIST = 128


EPS = 1e-06
NEG = -1000000000.0


def bucket_table(length):
    distance = np.maximum(np.arange(length)[:, None] - np.arange(length)[None, :], 0)
    exact = BUCKETS // 2
    scaled = exact + (
        np.log(np.maximum(distance, 1) / exact) / np.log(MAX_DIST / exact) * (BUCKETS - exact)
    ).astype(np.int32)
    return np.where(distance < exact, distance, np.minimum(scaled, BUCKETS - 1)).astype(np.int32)


F32 = jnp.float32
BF16 = jnp.bfloat16
CHUNK = 256
COPIES = 64


def dot(left, right, left_dim, right_dim):
    return lax.dot_general(
        left, right, (((left_dim,), (right_dim,)), ((), ())), preferred_element_type=F32
    )


def dot_nn(left, right):
    return dot(left, right, 1, 0)


def dot_nt(left, right):
    return dot(left, right, 1, 1)


def dot_tn(left, right):
    return dot(left, right, 0, 0)


def unit_rows(resid):
    inv = lax.rsqrt(jnp.mean(resid * resid, -1, keepdims=True) + EPS)
    return inv, resid * inv


def norm_back(resid, gain, grad):
    inv, unit = unit_rows(resid)
    weighted = grad * gain
    grad_resid = inv * (weighted - unit * jnp.mean(weighted * unit, -1, keepdims=True))
    return grad_resid, jnp.sum(grad * unit, 0, keepdims=True)


def layer_kernel(
    tlen_ref, mlen_ref, x0_ref, wq_ref, wk_ref, wv_ref, wo_ref, gains_ref, dist_ref,
    mem_hbm, cot_hbm, xq_hbm, xk_hbm, xv_hbm, xo_hbm, wg_hbm, wu_hbm, wd_hbm,
    out_ref, gt_ref, gm_ref, gf_ref, gx_ref, gs_ref, small_ref,
    q1, k1, v1, e1, r1, u1, o1, bias,
    part_send, part_recv, dn_recv, acc,
    mem, cot, wg, wu, wd, cross_w,
    x1, x2, n2, q2, kv2, e2, r2, u2, o2,
    n3, units, rows_low, rows_recv, rows_send_x, rows_recv_x,
    c2, turned, c1, f_low, f_recv0, f_recv1, f_recv2,
    x_recv0, x_recv1, x_recv2, x_send3, x_recv3,
    s_low, s_recv0, s_recv1, s_recv2, small, small_recv,
    local_sem, send_sem, recv_sem,
):
    me = lax.axis_index("mp")
    core, chip = lax.rem(me, 2), lax.div(me, 2)
    other_core, other_chip = 1 - core, 1 - chip
    by_core = 2 * chip + other_core
    by_x = 2 * other_chip + core
    across = 2 * other_chip + other_core
    at_dp = lax.axis_index("dp")
    bit_y, bit_z1, bit_z2 = lax.rem(at_dp, 2), lax.rem(lax.div(at_dp, 2), 2), lax.div(at_dp, 4)
    by_y = at_dp + 1 - 2 * bit_y
    by_z1 = at_dp + 2 - 4 * bit_z1
    by_z2 = at_dp + 4 - 8 * bit_z2
    to_core, to_x, to_across = {"mp": by_core}, {"mp": by_x}, {"mp": across}
    to_y, to_z1, to_z2 = {"dp": by_y}, {"dp": by_z1}, {"dp": by_z2}

    seqs, length, width = x0_ref.shape
    part = wq_ref.shape[1]
    heads = part // HEAD_DIM
    slots = mem.shape[0]
    blocks = cross_w.shape[0]
    share = width // 8
    quarter = length // blocks

    sent = {}

    def remote(i, src, dst, device):
        return pltpu.make_async_remote_copy(
            src_ref=src, dst_ref=dst, send_sem=send_sem.at[i], recv_sem=recv_sem.at[i],
            device_id=device, device_id_type=pl.DeviceIdType.MESH,
        )

    def send(i, src, dst, device):
        copy = remote(i, src, dst, device)
        copy.start()
        sent[i] = copy

    def left(*names):
        for name in names:
            sent.pop(name).wait_send()

    def arrived(i, dst, device):
        remote(i, dst, dst, device).wait_recv()

    barrier = pltpu.get_barrier_semaphore()
    partners = (to_core, to_x, to_across, to_y, to_z1, to_z2)
    for device in partners:
        pl.semaphore_signal(barrier, inc=1, device_id=device, device_id_type=pl.DeviceIdType.MESH)

    loads = [
        pltpu.make_async_copy(xo_hbm, cross_w.at[me, 3 * part : 4 * part], local_sem.at[3]),
        pltpu.make_async_copy(mem_hbm.at[me], mem, local_sem.at[4]),
        pltpu.make_async_copy(cot_hbm, cot, local_sem.at[5]),
        pltpu.make_async_copy(wg_hbm, wg, local_sem.at[6]),
        pltpu.make_async_copy(wu_hbm, wu, local_sem.at[7]),
        pltpu.make_async_copy(wd_hbm, wd, local_sem.at[8]),
    ]
    staged = [
        pltpu.make_async_copy(
            source.at[i * CHUNK : (i + 1) * CHUNK], stage.at[i], local_sem.at[10 + 3 * j + i]
        )
        for j, (source, stage) in enumerate(((xk_hbm, k1), (xv_hbm, v1), (xq_hbm, q1)))
        for i in range(width // CHUNK)
    ]
    for load in staged + loads:
        load.start()

    key_at = lax.broadcasted_iota(jnp.int32, (length, length), 0)
    query_at = lax.broadcasted_iota(jnp.int32, (length, length), 1)
    for h in range(heads):
        spread = jnp.broadcast_to(dist_ref[h : h + 1, :], (length, length))
        shifted = pltpu.roll(spread, 0, 1, stride=1, stride_axis=0)
        bias[h] = jnp.where(key_at <= query_at, shifted, NEG)

    for load in staged:
        load.wait()
    for j, stage in enumerate((k1, v1, q1)):
        for i in range(width // CHUNK):
            cols = slice(i * CHUNK, (i + 1) * CHUNK)
            cross_w[me, j * part : (j + 1) * part, cols] = stage[i].T
    loads[0].wait()
    pl.semaphore_wait(barrier, len(partners))

    lows, highs = slice(0, 2 * part), slice(2 * part, 4 * part)
    send(0, cross_w.at[me, lows], cross_w.at[me, lows], to_x)
    send(1, cross_w.at[me, lows], cross_w.at[me, lows], to_core)
    send(2, cross_w.at[me, highs], cross_w.at[me, highs], to_x)
    send(3, cross_w.at[me, highs], cross_w.at[me, highs], to_core)

    def self_one(t, carry):
        flip_x, flip_core = 1 - lax.div(t, 2), 1 - lax.rem(t, 2)
        at_x = chip + flip_x - 2 * chip * flip_x
        at_core = core + flip_core - 2 * core * flip_core
        s = 2 * at_x + at_core
        resid = x0_ref[s].astype(F32)
        _, unit = unit_rows(resid)
        n = (unit * gains_ref[0:1, :]).astype(BF16)
        q = dot_nn(n, wq_ref[...]).astype(BF16)
        k = dot_nn(n, wk_ref[...]).astype(BF16)
        v = dot_nn(n, wv_ref[...]).astype(BF16)
        q1[s], k1[s], v1[s] = q, k, v
        mixed = []
        for h in range(heads):
            cols = slice(h * HEAD_DIM, (h + 1) * HEAD_DIM)
            scores = dot_nt(k[:, cols], q[:, cols]) + bias[h]
            scores = jnp.where(key_at < tlen_ref[s], scores, NEG)
            e = jnp.exp(scores - jnp.max(scores, 0, keepdims=True))
            r = 1.0 / jnp.sum(e, 0, keepdims=True)
            e = e.astype(BF16)
            e1[s, h] = e
            r1[s, h] = r
            u = dot_tn(v[:, cols], e)
            u1[s, h] = u
            mixed.append(u * r)
        o = jnp.concatenate(mixed, 0).T.astype(BF16)
        o1[s] = o
        value = dot_nn(o, wo_ref[...])

        @pl.when(t == 0)
        def _():
            part_send[0] = value.astype(BF16)
            remote(4, part_send.at[0], part_recv.at[0], to_core).start()

        @pl.when(t == 1)
        def _():
            arrived(4, part_recv.at[0], to_core)
            part_send[1] = (value + part_recv[0].astype(F32)).astype(BF16)
            remote(5, part_send.at[1], part_recv.at[1], to_x).start()

        @pl.when(t == 2)
        def _():
            part_send[2] = value.astype(BF16)
            remote(6, part_send.at[2], part_recv.at[2], to_core).start()

        @pl.when(t == 3)
        def _():
            x1[...] = resid + value

        return carry

    lax.fori_loop(0, seqs, self_one, 0)
    sent[4] = remote(4, part_send.at[0], part_recv.at[0], to_core)
    sent[5] = remote(5, part_send.at[1], part_recv.at[1], to_x)
    sent[6] = remote(6, part_send.at[2], part_recv.at[2], to_core)

    arrived(0, cross_w.at[by_x, lows], to_x)
    send(7, cross_w.at[by_x, lows], cross_w.at[by_x, lows], to_core)
    arrived(1, cross_w.at[by_core, lows], to_core)
    arrived(7, cross_w.at[across, lows], to_core)
    loads[1].wait()

    def keys_values(b, carry):
        for at in range(0, slots, CHUNK):
            rows = slice(at, at + CHUNK)
            kv2[b, rows, :] = dot_nt(mem[rows, :], cross_w[b, lows, :]).astype(BF16)
        return carry

    lax.fori_loop(0, blocks, keys_values, 0)
    arrived(2, cross_w.at[by_x, highs], to_x)
    send(8, cross_w.at[by_x, highs], cross_w.at[by_x, highs], to_core)
    arrived(3, cross_w.at[by_core, highs], to_core)
    arrived(6, part_recv.at[2], to_core)
    arrived(5, part_recv.at[1], to_x)

    def enter_cross(i, carry):
        rows = pl.ds(pl.multiple_of(i * quarter, quarter), quarter)
        resid = x1[rows, :] + part_recv[1, rows, :].astype(F32) + part_recv[2, rows, :].astype(F32)
        x1[rows, :] = resid
        x2[rows, :] = resid
        n2[rows, :] = (unit_rows(resid)[1] * gains_ref[1:2, :]).astype(BF16)
        return carry

    lax.fori_loop(0, blocks, enter_cross, 0)
    arrived(8, cross_w.at[across, highs], to_core)
    slot_at = lax.broadcasted_iota(jnp.int32, (CHUNK, length), 0)

    def cross_one(b, carry):
        q = dot_nt(n2[...], cross_w[b, 2 * part : 3 * part, :]).astype(BF16)
        q2[b] = q
        mixed = []
        for h in range(heads):
            cols = slice(h * HEAD_DIM, (h + 1) * HEAD_DIM)
            cols_v = slice(part + h * HEAD_DIM, part + (h + 1) * HEAD_DIM)

            def scores_at(at):
                scores = dot_nt(kv2[b, at : at + CHUNK, cols], q[:, cols])
                return jnp.where(slot_at < mlen_ref[me] - at, scores, NEG)

            top = jnp.full((1, length), NEG, F32)
            for at in range(0, slots, CHUNK):
                top = jnp.maximum(top, jnp.max(scores_at(at), 0, keepdims=True))
            total = jnp.zeros((1, length), F32)
            u = jnp.zeros((HEAD_DIM, length), F32)
            for at in range(0, slots, CHUNK):
                rows = slice(at, at + CHUNK)
                e = jnp.exp(scores_at(at) - top)
                total = total + jnp.sum(e, 0, keepdims=True)
                e = e.astype(BF16)
                e2[b * heads + h, rows, :] = e
                u = u + dot_tn(kv2[b, rows, cols_v], e)
            r = 1.0 / total
            r2[b * heads + h] = r
            u2[b * heads + h] = u
            mixed.append(u * r)
        o = jnp.concatenate(mixed, 0).T.astype(BF16)
        o2[b] = o
        x2[...] += dot_nn(o, cross_w[b, 3 * part : 4 * part, :])
        return carry

    lax.fori_loop(0, blocks, cross_one, 0)

    def enter_ffn(i, carry):
        rows = pl.ds(pl.multiple_of(i * quarter, quarter), quarter)
        n3[me, rows, :] = (unit_rows(x2[rows, :])[1] * gains_ref[2:3, :]).astype(BF16)
        return carry

    lax.fori_loop(0, blocks, enter_ffn, 0)
    send(9, n3.at[me], n3.at[me], to_x)
    send(10, n3.at[me], n3.at[me], to_core)
    for load in loads[2:]:
        load.wait()
    left(4, 5, 6)
    scale, cubic = 0.7978845608028654, 0.044715

    def ffn_one(t, carry):
        flip_x, flip_core = lax.div(t, 2), lax.rem(t, 2)
        at_x = chip + flip_x - 2 * chip * flip_x
        at_core = core + flip_core - 2 * core * flip_core
        s = 2 * at_x + at_core

        @pl.when(t == 1)
        def _():
            arrived(10, n3.at[by_core], to_core)

        @pl.when(t == 2)
        def _():
            arrived(9, n3.at[by_x], to_x)
            remote(11, n3.at[by_x], n3.at[by_x], to_core).start()

        @pl.when(t == 3)
        def _():
            arrived(11, n3.at[across], to_core)

        n, c = n3[s], cot[s]
        rows = pl.ds(pl.multiple_of(s * length, length), length)
        for at in range(0, wg.shape[1], CHUNK):
            cols = slice(at, at + CHUNK)
            a = dot_nn(n, wg[:, cols])
            b = dot_nn(n, wu[:, cols])
            dh = dot_nt(c, wd[cols, :])
            square = a * a
            slope = jnp.tanh(scale * (a + cubic * (a * square)))
            half = 0.5 * (1.0 + slope)
            gelu = a * half
            rise = half + 0.5 * a * (1.0 - slope * slope) * (scale * (1.0 + 3.0 * cubic * square))
            units[0, rows, cols] = (dh * b * rise).astype(BF16)
            units[1, rows, cols] = (dh * gelu).astype(BF16)
            units[2, rows, cols] = (gelu * b).astype(BF16)
        dn = dot_nt(units[0, rows, :], wg[...]) + dot_nt(units[1, rows, :], wu[...])

        @pl.when(t == 0)
        def _():
            acc[...] = dn

        @pl.when(t == 1)
        def _():
            part_send[0] = dn.astype(BF16)
            remote(12, part_send.at[0], dn_recv.at[0], to_core).start()

        @pl.when(t == 2)
        def _():
            part_send[2] = dn.astype(BF16)

        @pl.when(t == 3)
        def _():
            part_send[1] = dn.astype(BF16)
            remote(13, part_send.at[1], dn_recv.at[1], to_core).start()

        own = jnp.where(t == 0, 1.0, 0.0)
        result = dot_nn(units[2, rows, :], wd[...]) + own * x2[...]
        for i in range(blocks):
            rows_low[i % 2, i // 2, s] = result[i * quarter : (i + 1) * quarter].astype(BF16)
        return carry

    lax.fori_loop(0, seqs, ffn_one, 0)
    sent[11] = remote(11, n3.at[by_x], n3.at[by_x], to_core)
    arrived(13, dn_recv.at[1], to_core)
    part_send[2] = (part_send[2].astype(F32) + dn_recv[1].astype(F32)).astype(BF16)
    send(14, part_send.at[2], dn_recv.at[2], to_x)
    sent[12] = remote(12, part_send.at[0], dn_recv.at[0], to_core)
    sent[13] = remote(13, part_send.at[1], dn_recv.at[1], to_core)
    send(15, rows_low.at[other_core], rows_recv, to_core)

    def turn(slot, value, first_col, order):
        value = value.T
        for j in range(8):
            y, z1, z2 = j % 2, j // 2 % 2, j // 4
            at = (4 * y + 2 * z1 + z2) if order == "y" else (4 * z1 + 2 * y + z2)
            cols = slice(first_col, first_col + value.shape[1])
            turned[slot, at * share : (at + 1) * share, cols] = value[j * share : (j + 1) * share]

    for s in range(seqs):
        turn(0, n3[s], s * length, "y")
        turn(1, cot[s], s * length, "y")

    half_rows = 4 * share

    def half_at(bit):
        return pl.ds(pl.multiple_of(bit * half_rows, half_rows), half_rows)

    for keep in (False, True):
        for i in range(3):
            rows = half_at(bit_y if keep else 1 - bit_y)
            f_low[i, rows, :] = dot_nn(turned[i // 2, rows, :], units[i]).astype(BF16)
            if not keep:
                send(16 + i, f_low.at[i, rows], f_recv0.at[i], to_y)

    arrived(15, rows_recv, to_core)
    rows_send_x[...] = (
        rows_low[core, other_chip].astype(F32) + rows_recv[other_chip].astype(F32)
    ).astype(BF16)
    send(19, rows_send_x, rows_recv_x, to_x)

    arrived(12, dn_recv.at[0], to_core)
    arrived(14, dn_recv.at[2], to_x)
    small[...] = jnp.zeros_like(small)

    def enter_back(i, carry):
        rows = pl.ds(pl.multiple_of(i * quarter, quarter), quarter)
        dn3 = acc[rows, :] + dn_recv[0, rows, :].astype(F32) + dn_recv[2, rows, :].astype(F32)
        grad, gain_ffn = norm_back(x2[rows, :], gains_ref[2:3, :], dn3)
        dx2 = cot[me, rows, :].astype(F32) + grad
        acc[rows, :] = dx2
        c2[rows, :] = dx2.astype(BF16)
        small[0, 2:3, :] += gain_ffn
        return carry

    lax.fori_loop(0, blocks, enter_back, 0)

    def cross_back(b, carry):
        do = dot_nt(cross_w[b, 3 * part : 4 * part, :], c2[...])
        q = q2[b]
        dqs = []
        for h in range(heads):
            cols = slice(h * HEAD_DIM, (h + 1) * HEAD_DIM)
            cols_v = slice(part + h * HEAD_DIM, part + (h + 1) * HEAD_DIM)
            r = r2[b * heads + h]
            low = (do[cols] * r).astype(BF16)
            delta = r * jnp.sum(low.astype(F32) * u2[b * heads + h], 0, keepdims=True)
            dq = jnp.zeros((HEAD_DIM, length), F32)
            for at in range(0, slots, CHUNK):
                rows = slice(at, at + CHUNK)
                e = e2[b * heads + h, rows, :]
                dp = dot_nn(kv2[b, rows, cols_v], low)
                ds = (e.astype(F32) * (dp - delta)).astype(BF16)
                dq = dq + dot_tn(kv2[b, rows, cols], ds)
                kv2[b, rows, cols_v] = dot_nt(e, low).astype(BF16)
                kv2[b, rows, cols] = dot_nn(ds, q[:, cols]).astype(BF16)
            dqs.append(dq)
        q2[b] = jnp.concatenate(dqs, 0).T.astype(BF16)
        return carry

    lax.fori_loop(0, blocks, cross_back, 0)
    dn2 = dot_nn(q2[0], cross_w[0, 2 * part : 3 * part, :])
    for b in range(1, blocks):
        dn2 = dn2 + dot_nn(q2[b], cross_w[b, 2 * part : 3 * part, :])
    x2[...] = dn2

    def leave_cross(i, carry):
        rows = pl.ds(pl.multiple_of(i * quarter, quarter), quarter)
        grad, gain_cross = norm_back(x1[rows, :], gains_ref[1:2, :], x2[rows, :])
        c1[me, rows, :] = (acc[rows, :] + grad).astype(BF16)
        small[0, 1:2, :] += gain_cross
        return carry

    lax.fori_loop(0, blocks, leave_cross, 0)
    arrived(19, rows_recv_x, to_x)
    out_ref[...] = (
        rows_low[core, chip].astype(F32)
        + rows_recv[chip].astype(F32)
        + rows_recv_x[...].astype(F32)
    ).astype(BF16)
    left(15, 19)
    send(20, c1.at[me], c1.at[me], to_x)
    send(21, c1.at[me], c1.at[me], to_core)

    def add_rows(ref, start, count, recv, recv_start):
        at = pl.ds(pl.multiple_of(start, share), count)
        from_at = pl.ds(pl.multiple_of(recv_start, share), count)
        ref[at, :] = (ref[at, :].astype(F32) + recv[from_at, :].astype(F32)).astype(BF16)

    def pass_on(ref, base, count, recv, bit, i, recv_next, device):
        away, kept = (1 - bit) * count, bit * count
        add_rows(ref, base + away, count, recv, away)
        rows = pl.ds(pl.multiple_of(base + away, share), count)
        send(i, ref.at[rows], recv_next, device)
        add_rows(ref, base + kept, count, recv, kept)
        return base + kept

    f_base = [None] * 3
    for i in range(3):
        arrived(16 + i, f_recv0.at[i], to_y)
        f_base[i] = pass_on(
            f_low.at[i], bit_y * half_rows, 2 * share, f_recv0.at[i], bit_z1, 22 + i, f_recv1.at[i], to_z1
        )

    left(9, 10, 11)

    def memory_grad(target):
        rows = pl.ds(pl.multiple_of(target * CHUNK, CHUNK), CHUNK)
        total = None
        for b in range(blocks):
            term = dot_nn(kv2[b, rows, :], cross_w[b, lows, :])
            total = term if total is None else total + term
        n3[target] = total.astype(BF16)

    memory_grad(by_x)
    send(25, n3.at[by_x], gm_ref.at[me], to_x)
    memory_grad(across)
    send(26, n3.at[across], gm_ref.at[me], to_across)
    memory_grad(by_core)
    send(27, n3.at[by_core], gm_ref.at[me], to_core)
    memory_grad(me)
    own_rows = pltpu.make_async_copy(n3.at[me], gm_ref.at[me], local_sem.at[9])
    own_rows.start()

    turn(0, mem[...], 0, "z1")
    turn(1, n2[...], 0, "z1")
    turn(1, c2[...], length, "z1")
    arrived(21, c1.at[by_core], to_core)

    def cross_grads(b):
        for at in range(0, width, half_rows):
            rows = slice(at, at + half_rows)
            kv = dot_nn(turned[0, rows, :], kv2[b]).astype(BF16)
            q = dot_nn(turned[1, rows, 0:length], q2[b]).astype(BF16)
            o = dot_nn(turned[1, rows, length : 2 * length], o2[b]).astype(BF16)
            e2[3 * b, rows, :] = kv[:, 0:256]
            e2[3 * b + 1, rows, 0:128] = kv[:, 256:384]
            e2[3 * b + 1, rows, 128:256] = q[:, 0:128]
            e2[3 * b + 2, rows, 0:64] = q[:, 128:192]
            e2[3 * b + 2, rows, 64:256] = o

    for i in range(2):
        b = 2 * i + other_core
        cross_grads(b)
        for j in range(3):
            send(
                28 + 3 * i + j,
                e2.at[3 * b + j, 0:width],
                units.at[j, 0:width, 256 * i : 256 * (i + 1)],
                to_core,
            )
    arrived(20, c1.at[by_x], to_x)
    send(34, c1.at[by_x], c1.at[by_x], to_core)
    for i in range(2):
        cross_grads(2 * i + core)
    for i in range(2):
        b = 2 * i + core
        for j in range(3):
            arrived(28 + 3 * i + j, units.at[j, 0:width, 256 * i : 256 * (i + 1)], to_core)
            landed = units.at[j, 0:width, 256 * i : 256 * (i + 1)]
            mine = e2.at[3 * b + j, 0:width]
            add_rows(mine, (1 - bit_z1) * half_rows, half_rows, landed, (1 - bit_z1) * half_rows)
        send(
            35 + i,
            e2.at[pl.ds(3 * b, 3), half_at(1 - bit_z1)],
            x_recv0.at[i],
            to_z1,
        )
        for j in range(3):
            landed = units.at[j, 0:width, 256 * i : 256 * (i + 1)]
            mine = e2.at[3 * b + j, 0:width]
            add_rows(mine, bit_z1 * half_rows, half_rows, landed, bit_z1 * half_rows)

    bias[...] = jnp.zeros_like(bias)

    def self_back(t, carry):
        flip_x, flip_core = lax.div(t, 2), lax.rem(t, 2)
        at_x = chip + flip_x - 2 * chip * flip_x
        at_core = core + flip_core - 2 * core * flip_core
        s = 2 * at_x + at_core

        @pl.when(t == 3)
        def _():
            arrived(34, c1.at[across], to_core)

        do = dot_nt(wo_ref[...], c1[s])
        dqs = []
        for h in range(heads):
            cols = slice(h * HEAD_DIM, (h + 1) * HEAD_DIM)
            r = r1[s, h]
            low = (do[cols] * r).astype(BF16)
            delta = r * jnp.sum(low.astype(F32) * u1[s, h], 0, keepdims=True)
            e = e1[s, h]
            dp = dot_nn(v1[s, :, cols], low)
            ds = (e.astype(F32) * (dp - delta)).astype(BF16)
            bias[h] += ds.astype(F32)
            dqs.append(dot_tn(k1[s, :, cols], ds))
            v1[s, :, cols] = dot_nt(e, low).astype(BF16)
            k1[s, :, cols] = dot_nn(ds, q1[s, :, cols]).astype(BF16)
        q1[s] = jnp.concatenate(dqs, 0).T.astype(BF16)
        dn = dot_nt(q1[s], wq_ref[...]) + dot_nt(k1[s], wk_ref[...]) + dot_nt(v1[s], wv_ref[...])
        acc[...] = dn
        for i in range(blocks):
            rows = slice(i * quarter, (i + 1) * quarter)
            unit = unit_rows(x0_ref[s, rows, :].astype(F32))[1]
            small[0, 0:1, :] += jnp.sum(acc[rows, :] * unit, 0, keepdims=True)
            rows_low[i % 2, i // 2, s] = acc[rows, :].astype(BF16)
        return carry

    lax.fori_loop(0, seqs, self_back, 0)
    send(37, rows_low.at[other_core], rows_recv, to_core)
    send(38, small.at[0], small_recv.at[0], to_core)

    for s in range(seqs):
        _, unit = unit_rows(x0_ref[s].astype(F32))
        turn(0, (unit * gains_ref[0:1, :]).astype(BF16), s * length, "y")
        turn(1, c1[s], s * length, "y")
    for keep in (False, True):
        rows = half_at(bit_y if keep else 1 - bit_y)
        for i, ref in enumerate((k1, v1, q1, o1)):
            right = ref[...].reshape(seqs * length, part)
            value = dot_nn(turned[1 if i == 3 else 0, rows, :], right).astype(BF16)
            s_low[rows, i * part : (i + 1) * part] = value
        if not keep:
            send(39, s_low.at[rows], s_recv0, to_y)

    arrived(37, rows_recv, to_core)
    rows_send_x[...] = (
        rows_low[core, other_chip].astype(F32) + rows_recv[other_chip].astype(F32)
    ).astype(BF16)
    send(40, rows_send_x, rows_recv_x, to_x)
    arrived(38, small_recv.at[0], to_core)
    small[1, 0:8] = small[0] + small_recv[0]
    send(41, small.at[1], small_recv.at[1], to_x)
    for h in range(heads):
        total = bias[h]
        step = 1
        while step < length:
            total = jnp.where((key_at & step) != 0, pltpu.roll(total, length - step, 1), total)
            step *= 2
        small[3, h : h + 1, 0:length] = jnp.sum(total, 0, keepdims=True)
    arrived(41, small_recv.at[1], to_x)
    small[2] = small[1] + small_recv[1]
    send(42, small.at[pl.ds(2, 2)], small_recv.at[pl.ds(2, 2)], to_y)

    x_base = [None] * 2
    for i in range(3):
        arrived(22 + i, f_recv1.at[i], to_z1)
        f_base[i] = pass_on(
            f_low.at[i], f_base[i], share, f_recv1.at[i], bit_z2, 47 + i, f_recv2.at[i], to_z2
        )
    for i in range(2):
        b = 2 * i + core
        arrived(35 + i, x_recv0.at[i], to_z1)
        base = bit_z1 * half_rows
        away, kept = base + (1 - bit_y) * 2 * share, base + bit_y * 2 * share
        for j in range(3):
            add_rows(e2.at[3 * b + j], away, 2 * share, x_recv0.at[i, j], (1 - bit_y) * 2 * share)
        send(
            50 + i,
            e2.at[pl.ds(3 * b, 3), pl.ds(pl.multiple_of(away, share), 2 * share)],
            x_recv1.at[i],
            to_y,
        )
        for j in range(3):
            add_rows(e2.at[3 * b + j], kept, 2 * share, x_recv0.at[i, j], bit_y * 2 * share)
        x_base[i] = kept

    arrived(42, small_recv.at[pl.ds(2, 2)], to_y)
    small[4:6] = small[2:4] + small_recv[2:4]
    send(44, small.at[pl.ds(4, 2)], small_recv.at[pl.ds(4, 2)], to_z1)
    arrived(39, s_recv0, to_y)
    s_base = pass_on(s_low, bit_y * half_rows, 2 * share, s_recv0, bit_z1, 52, s_recv1, to_z1)

    for i in range(2):
        b = 2 * i + core
        arrived(50 + i, x_recv1.at[i], to_y)
        away, kept = x_base[i] + (1 - bit_z2) * share, x_base[i] + bit_z2 * share
        for j in range(3):
            add_rows(e2.at[3 * b + j], away, share, x_recv1.at[i, j], (1 - bit_z2) * share)
        send(
            53 + i,
            e2.at[pl.ds(3 * b, 3), pl.ds(pl.multiple_of(away, share), share)],
            x_recv2.at[i],
            to_z2,
        )
        for j in range(3):
            add_rows(e2.at[3 * b + j], kept, share, x_recv1.at[i, j], bit_z2 * share)
        x_base[i] = kept

    base = x_base[0]

    def cross_sum(at):
        rows = pl.ds(pl.multiple_of(base, share), share)
        return [
            e2[3 * (2 * at + core) + j, rows, :].astype(F32) + x_recv2[at, j].astype(F32)
            for j in range(3)
        ]

    arrived(40, rows_recv_x, to_x)
    my_rows = pl.ds(pl.multiple_of(me * quarter, quarter), quarter)
    for s in range(seqs):
        dn = (
            rows_low[core, chip, s].astype(F32)
            + rows_recv[chip, s].astype(F32)
            + rows_recv_x[s].astype(F32)
        )
        grad, _ = norm_back(x0_ref[s, my_rows, :].astype(F32), gains_ref[0:1, :], dn)
        gt_ref[s] = (c1[s, my_rows, :].astype(F32) + grad).astype(BF16)

    arrived(44, small_recv.at[pl.ds(4, 2)], to_z1)
    small[6:8] = small[4:6] + small_recv[4:6]
    send(46, small.at[pl.ds(6, 2)], small_recv.at[pl.ds(6, 2)], to_z2)
    arrived(52, s_recv1, to_z1)
    s_base = pass_on(s_low, s_base, share, s_recv1, bit_z2, 55, s_recv2, to_z2)
    for i in range(2):
        arrived(53 + i, x_recv2.at[i], to_z2)
    for j, value in enumerate(cross_sum(other_chip)):
        x_send3[j] = value.astype(BF16)
    send(56, x_send3, x_recv3, to_x)
    for i in range(3):
        arrived(47 + i, f_recv2.at[i], to_z2)
        rows = pl.ds(pl.multiple_of(f_base[i], share), share)
        gf_ref[i] = f_low[i, rows, :].astype(F32) + f_recv2[i].astype(F32)
    arrived(46, small_recv.at[pl.ds(6, 2)], to_z2)
    small_ref[...] = small[6:8] + small_recv[6:8]
    arrived(55, s_recv2, to_z2)
    rows = pl.ds(pl.multiple_of(s_base, share), share)
    gs_ref[...] = s_low[rows, :].astype(F32) + s_recv2[...].astype(F32)
    arrived(56, x_recv3, to_x)
    for j, value in enumerate(cross_sum(chip)):
        gx_ref[j] = value + x_recv3[j].astype(F32)
    arrived(25, gm_ref.at[by_x], to_x)
    arrived(26, gm_ref.at[across], to_across)
    arrived(27, gm_ref.at[by_core], to_core)
    own_rows.wait()
    for copy in sent.values():
        copy.wait_send()


def finish_kernel(
    gf_ref, gx_ref, gs_ref, small_ref, onehot_ref, out_ref, gt_ref, gm_ref,
    out_o, gt_o, gm_o, sq_o, sk_o, sv_o, so_o, cq_o, ck_o, cv_o, co_o, gg_o, gu_o, gd_o,
    gains_o, bias_o,
):
    part = sq_o.shape[1]
    out_o[...], gt_o[...], gm_o[...] = out_ref[...], gt_ref[...], gm_ref[...]
    gg_o[...], gu_o[...], gd_o[...] = gf_ref[0], gf_ref[1], gf_ref[2].T
    whole = jnp.concatenate([gx_ref[0], gx_ref[1], gx_ref[2]], 1)
    for value, refs in ((whole, (ck_o, cv_o, cq_o, co_o)), (gs_ref[...], (sk_o, sv_o, sq_o, so_o))):
        for i in range(3):
            refs[i][...] = value[:, i * part : (i + 1) * part]
        refs[3][...] = value[:, 3 * part :].T
    gains_o[...] = small_ref[0]
    bias_o[...] = lax.dot_general(
        onehot_ref[...], small_ref[1, :, 0 : onehot_ref.shape[0]], (((0,), (1,)), ((), ())),
        precision=lax.Precision.HIGHEST, preferred_element_type=F32,
    )


VMEM = pl.BlockSpec(memory_space=pltpu.VMEM)
SMEM = pl.BlockSpec(memory_space=pltpu.SMEM)
ANY = pl.BlockSpec(memory_space=pl.ANY)


def on_device(
    targets,
    memory,
    cotangent,
    target_len,
    memory_len,
    query_self,
    key_self,
    value_self,
    out_self,
    query_cross,
    key_cross,
    value_cross,
    out_cross,
    gate_proj,
    up_proj,
    down_proj,
    gain_self,
    gain_cross,
    gain_ffn,
    pos_bias,
):
    seqs, length, width = targets.shape
    slots = memory.shape[1]
    part = query_self.shape[1]
    units = gate_proj.shape[1]
    heads = part // HEAD_DIM
    blocks = lax.axis_size("mp")
    dp_size = lax.axis_size("dp")
    share = width // dp_size
    quarter = length // blocks
    head_all = heads * blocks

    onehot = jnp.asarray(
        (bucket_table(length)[:, 0][:, None] == np.arange(BUCKETS)[None, :]).astype(np.float32)
    )
    dist = jnp.dot(onehot, pos_bias, precision=lax.Precision.HIGHEST).T
    gains = jnp.stack([gain_self, gain_cross, gain_ffn])

    def low(*shape):
        return pltpu.VMEM(shape, BF16)

    def full(*shape):
        return pltpu.VMEM(shape, F32)

    def sums(count, columns):
        return [low(count, 4 * share, columns), low(count, 2 * share, columns), low(count, share, columns)]

    scratch = [
        low(seqs, length, part), low(seqs, length, part), low(seqs, length, part),
        low(seqs, heads, length, length), full(seqs, heads, 1, length),
        full(seqs, heads, HEAD_DIM, length), low(seqs, length, part), full(heads, length, length),
        low(3, length, width), low(3, length, width), low(3, length, width),
        full(length, width),
        low(slots, width), low(seqs, length, width),
        low(width, units), low(width, units), low(units, width), low(blocks, 4 * part, width),
        full(length, width), full(length, width), low(length, width), low(blocks, length, part),
        low(blocks, slots, 2 * part), low(head_all, slots, length), full(head_all, 1, length),
        full(head_all, HEAD_DIM, length), low(blocks, length, part),
        low(seqs, length, width), low(3, seqs * length, units),
        low(2, 2, seqs, quarter, width), low(2, seqs, quarter, width),
        low(seqs, quarter, width), low(seqs, quarter, width),
        low(length, width), low(2, width, seqs * length), low(seqs, length, width),
        low(3, width, units), *sums(3, units),
        low(2, 3, 4 * share, 256), low(2, 3, 2 * share, 256), low(2, 3, share, 256),
        low(3, share, 256), low(3, share, 256),
        low(width, width), low(4 * share, width), low(2 * share, width), low(share, width),
        full(8, 8, width), full(8, 8, width),
        pltpu.SemaphoreType.DMA((19,)),
        pltpu.SemaphoreType.DMA((COPIES,)),
        pltpu.SemaphoreType.DMA((COPIES,)),
    ]
    struct = jax.ShapeDtypeStruct
    rows = struct((seqs, quarter, width), BF16)
    out, gt, gm, gf, gx, gs, small = pl.pallas_call(
        layer_kernel,
        out_shape=[
            rows,
            rows,
            struct((seqs, slots // blocks, width), BF16),
            struct((3, share, units), F32),
            struct((3, share, 256), F32),
            struct((share, width), F32),
            struct((2, 8, width), F32),
        ],
        in_specs=[SMEM] * 2 + [VMEM] * 7 + [ANY] * 9,
        out_specs=[VMEM, VMEM, ANY, VMEM, VMEM, VMEM, VMEM],
        scratch_shapes=scratch,
        compiler_params=pltpu.CompilerParams(
            collective_id=0, has_side_effects=True, vmem_limit_bytes=63 * 2**20
        ),
        cost_estimate=pl.CostEstimate(flops=24 * 10**9, bytes_accessed=2**24, transcendentals=0),
        name="layer",
    )(
        target_len, memory_len, targets, query_self, key_self, value_self, out_self, gains, dist,
        memory, cotangent, query_cross, key_cross, value_cross, out_cross,
        gate_proj, up_proj, down_proj,
    )
    square = struct((share, part), F32)
    turned = struct((part, share), F32)
    (
        out, gt, gm, sq, sk, sv, so, cq, ck, cv, co, gg, gu, gd, gains, bias,
    ) = pl.pallas_call(
        finish_kernel,
        out_shape=[
            rows, rows, struct((seqs, slots // blocks, width), BF16),
            square, square, square, turned, square, square, square, turned,
            struct((share, units), F32), struct((share, units), F32), struct((units, share), F32),
            struct((8, width), F32), struct((BUCKETS, 8), F32),
        ],
        in_specs=[VMEM] * 8,
        out_specs=[VMEM] * 16,
        compiler_params=pltpu.CompilerParams(vmem_limit_bytes=32 * 2**20),
        name="finish",
    )(gf, gx, gs, small, onehot, out, gt, gm)
    gains = lax.dynamic_slice_in_dim(gains[:3], lax.axis_index("dp") * share, share, 1)
    return (
        out, gt, gm, sq, sk, sv, so, cq, ck, cv, co, gg, gu, gd,
        gains[0], gains[1], gains[2], bias[:, :heads],
    )


def project(inputs, weight):
    return jnp.einsum("bld,df->blf", inputs, weight, preferred_element_type=jnp.float32)


def back_project(gradient, weight):
    return jnp.einsum("blf,df->bld", gradient, weight, preferred_element_type=jnp.float32)


def weight_grad(inputs, gradient):
    return jnp.einsum("bld,blf->df", inputs, gradient, preferred_element_type=jnp.float32)


def norm_forward(resid, gain):
    inv_rms = lax.rsqrt(jnp.mean(resid * resid, -1, keepdims=True) + EPS)
    return (resid * inv_rms * gain, inv_rms)


def norm_backward(resid, inv_rms, gain, grad_normed):
    unit_rows = resid * inv_rms
    grad_gain = jnp.sum(grad_normed * unit_rows, axis=(0, 1))
    weighted = grad_normed * gain
    grad_resid = inv_rms * (
        weighted - unit_rows * jnp.mean(weighted * unit_rows, -1, keepdims=True)
    )
    return (grad_resid, grad_gain)


def scores_of(queries, keys, score_bias, valid):
    scores = (
        jnp.einsum("bihe,bjhe->bhij", queries, keys, preferred_element_type=jnp.float32)
        + score_bias
    )
    return jnp.where(valid, scores, NEG)


def attend(queries, keys, values, score_bias, valid):
    scores = scores_of(queries, keys, score_bias, valid)
    row_max = jnp.max(scores, -1, keepdims=True)
    log_total = row_max + jnp.log(jnp.sum(jnp.exp(scores - row_max), -1, keepdims=True))
    attn_probs = jnp.exp(scores - log_total).astype(jnp.bfloat16)
    mixed = jnp.einsum("bhij,bjhe->bihe", attn_probs, values, preferred_element_type=jnp.float32)
    return (mixed, log_total)


def attend_back(queries, keys, values, score_bias, valid, log_total, grad_mixed):
    attn_probs = jnp.exp(scores_of(queries, keys, score_bias, valid) - log_total)
    grad_values = jnp.einsum(
        "bhij,bihe->bjhe",
        attn_probs.astype(jnp.bfloat16),
        grad_mixed,
        preferred_element_type=jnp.float32,
    )
    grad_probs = jnp.einsum(
        "bihe,bjhe->bhij", grad_mixed, values, preferred_element_type=jnp.float32
    )
    grad_scores = attn_probs * (grad_probs - jnp.sum(attn_probs * grad_probs, -1, keepdims=True))
    grad_low = grad_scores.astype(jnp.bfloat16)
    grad_queries = jnp.einsum("bhij,bjhe->bihe", grad_low, keys, preferred_element_type=jnp.float32)
    grad_keys = jnp.einsum("bhij,bihe->bjhe", grad_low, queries, preferred_element_type=jnp.float32)
    return (grad_queries, grad_keys, grad_values, grad_low)


def swap(value, axis, bit):
    return lax.ppermute(value, axis, [(i, i ^ bit) for i in range(lax.axis_size(axis))])


def bits_of(axis):
    return [1 << i for i in range(lax.axis_size(axis).bit_length() - 1)]


def split_bits(value, axis, dim):
    steps = len(bits_of(axis))
    shape = value.shape
    return value.reshape(
        shape[:dim] + (2,) * steps + (shape[dim] >> steps,) + shape[dim + 1 :]
    )


def own_bit(axis, bit):
    return (lax.axis_index(axis) & bit) // bit


def halve(value, axis, bit, dim):
    mine = own_bit(axis, bit)
    kept = lax.dynamic_index_in_dim(value, mine, dim, keepdims=False)
    sent = lax.dynamic_index_in_dim(value, 1 - mine, dim, keepdims=False)
    arrived = swap(sent.astype(jnp.bfloat16), axis, bit)
    return kept + arrived.astype(jnp.float32)


def reduce_scatter(value, axis, dim):
    bits = bits_of(axis)
    value = split_bits(value, axis, dim)
    for at, bit in enumerate(bits):
        value = halve(value, axis, bit, dim + len(bits) - 1 - at)
    return value


def gather_mp(value):
    value = value[None]
    for bit in reversed(bits_of("mp")):
        other = swap(value, "mp", bit)
        first = own_bit("mp", bit) == 0
        low = jnp.where(first, value, other)
        high = jnp.where(first, other, value)
        value = jnp.stack([low, high], 1 if bit == 1 else 0)
        value = value.reshape((-1,) + value.shape[2:])
    return value


def exchange_mp(value):
    count = lax.axis_size("mp")
    value = split_bits(value, "mp", 0)[None]
    steps = len(bits_of("mp"))
    for at, bit in enumerate(bits_of("mp")):
        dim = steps - at
        mine = own_bit("mp", bit)
        kept = lax.dynamic_index_in_dim(value, mine, dim, keepdims=False)
        sent = lax.dynamic_index_in_dim(value, 1 - mine, dim, keepdims=False)
        arrived = swap(sent, "mp", bit)
        first = mine == 0
        low = jnp.where(first, kept, arrived)
        high = jnp.where(first, arrived, kept)
        value = jnp.stack([low, high], 0)
        value = value.reshape((-1,) + value.shape[2:])
    return value.reshape((count,) + value.shape[1:])


def sum_mp(value):
    for bit in bits_of("mp"):
        value = value + swap(value, "mp", bit)
    return value


def on_device_permutes(
    targets,
    memory,
    cotangent,
    target_len,
    memory_len,
    query_self,
    key_self,
    value_self,
    out_self,
    query_cross,
    key_cross,
    value_cross,
    out_cross,
    gate_proj,
    up_proj,
    down_proj,
    gain_self,
    gain_cross,
    gain_ffn,
    pos_bias,
):
    length = targets.shape[1]
    heads_local = query_self.shape[1] // HEAD_DIM
    mp_size = lax.axis_size("mp")
    dp_size = lax.axis_size("dp")
    mp_index = lax.axis_index("mp")
    row_share = length // mp_size
    width = targets.shape[2]

    def split_heads(value):
        return value.reshape(value.shape[0], value.shape[1], -1, HEAD_DIM)

    def merge_heads(value):
        return value.reshape(value.shape[0], value.shape[1], -1)

    def my_rows(value):
        return lax.dynamic_slice_in_dim(value, mp_index * row_share, row_share, 1)

    def mine(value):
        return lax.dynamic_index_in_dim(value, mp_index, 0)

    positions = jnp.arange(length)
    self_valid = (
        (positions[None, :] <= positions[:, None])[None]
        & (positions[None, None, :] < target_len[:, None, None])
    )[:, None]
    mem_positions = jnp.arange(memory.shape[1])
    cross_valid = (mem_positions[None, :] < mine(memory_len)[:, None])[:, None, None, :]
    onehot = (
        jnp.asarray(bucket_table(length)).reshape(-1)[:, None] == jnp.arange(BUCKETS)[None, :]
    ).astype(jnp.float32)
    score_bias = (
        jnp.dot(onehot, pos_bias, precision=lax.Precision.HIGHEST)
        .reshape(length, length, heads_local)
        .transpose(2, 0, 1)[None]
    )
    cross_in = gather_mp(jnp.stack([query_cross, key_cross, value_cross]))
    cross_in = cross_in.transpose(1, 2, 0, 3).reshape(3, width, -1)
    cross_q, cross_k, cross_v = cross_in[0], cross_in[1], cross_in[2]
    cross_o = gather_mp(out_cross).reshape(-1, width)

    resid0 = targets.astype(jnp.float32)
    normed_one, inv_one = norm_forward(resid0, gain_self)
    normed_one = normed_one.astype(jnp.bfloat16)
    queries = split_heads(project(normed_one, query_self).astype(jnp.bfloat16))
    keys = split_heads(project(normed_one, key_self).astype(jnp.bfloat16))
    values = split_heads(project(normed_one, value_self).astype(jnp.bfloat16))
    mixed, log_one = attend(queries, keys, values, score_bias, self_valid)
    mixed = merge_heads(mixed).astype(jnp.bfloat16)
    resid1 = mine(resid0) + reduce_scatter(project(mixed, out_self), "mp", 0)

    mem_own = mine(memory)
    normed_two, inv_two = norm_forward(resid1, gain_cross)
    normed_two = normed_two.astype(jnp.bfloat16)
    queries_two = split_heads(project(normed_two, cross_q).astype(jnp.bfloat16))
    mem_keys = split_heads(project(mem_own, cross_k).astype(jnp.bfloat16))
    mem_values = split_heads(project(mem_own, cross_v).astype(jnp.bfloat16))
    mixed_two, log_two = attend(queries_two, mem_keys, mem_values, 0.0, cross_valid)
    mixed_two = merge_heads(mixed_two).astype(jnp.bfloat16)
    resid2 = resid1 + project(mixed_two, cross_o)
    normed_three, inv_three = norm_forward(resid2, gain_ffn)
    normed_all = gather_mp(normed_three.astype(jnp.bfloat16)[0])

    gate_pre = project(normed_all, gate_proj)
    up_pre = project(normed_all, up_proj)

    def gated(gate_in, up_in):
        return jax.nn.gelu(gate_in, approximate=True) * up_in

    hidden, hidden_pull = jax.vjp(gated, gate_pre, up_pre)
    hidden = hidden.astype(jnp.bfloat16)
    grad_gate_pre, grad_up_pre = hidden_pull(back_project(cotangent, down_proj))
    grad_gate_pre = grad_gate_pre.astype(jnp.bfloat16)
    grad_up_pre = grad_up_pre.astype(jnp.bfloat16)
    grad_normed = reduce_scatter(
        back_project(grad_gate_pre, gate_proj) + back_project(grad_up_pre, up_proj), "mp", 0
    )
    result = project(hidden, down_proj)
    own = (jnp.arange(targets.shape[0]) == mp_index)[:, None, None]
    result = result + jnp.where(own, resid2, 0.0)
    output = reduce_scatter(result, "mp", 1).astype(jnp.bfloat16)
    ffn_grads = jnp.concatenate(
        [
            weight_grad(normed_all, grad_gate_pre),
            weight_grad(normed_all, grad_up_pre),
            weight_grad(cotangent, hidden),
        ],
        1,
    )
    ffn_grads = reduce_scatter(ffn_grads, "dp", 0)
    grad_resid, grad_gain_ffn = norm_backward(resid2, inv_three, gain_ffn, grad_normed)
    grad_two = mine(cotangent).astype(jnp.float32) + grad_resid

    branch_two = grad_two.astype(jnp.bfloat16)
    grad_mixed_two = split_heads(back_project(branch_two, cross_o).astype(jnp.bfloat16))
    grad_q_two, grad_mem_keys, grad_mem_values, _ = attend_back(
        queries_two, mem_keys, mem_values, 0.0, cross_valid, log_two, grad_mixed_two
    )
    grad_q_two = merge_heads(grad_q_two).astype(jnp.bfloat16)
    grad_normed = back_project(grad_q_two, cross_q)
    grad_resid, grad_gain_cross = norm_backward(resid1, inv_two, gain_cross, grad_normed)
    grad_one = grad_two + grad_resid
    branch_one = gather_mp(grad_one.astype(jnp.bfloat16)[0])
    grad_mem_keys = merge_heads(grad_mem_keys).astype(jnp.bfloat16)
    grad_mem_values = merge_heads(grad_mem_values).astype(jnp.bfloat16)
    mem_grad = back_project(grad_mem_keys, cross_k) + back_project(grad_mem_values, cross_v)
    mem_rows = exchange_mp(mem_grad[0].astype(jnp.bfloat16))
    cross_grads = jnp.stack(
        [
            weight_grad(normed_two, grad_q_two),
            weight_grad(mem_own, grad_mem_keys),
            weight_grad(mem_own, grad_mem_values),
            weight_grad(branch_two, mixed_two),
        ],
        1,
    )
    cross_grads = reduce_scatter(cross_grads, "mp", 2)
    cross_grads = reduce_scatter(cross_grads, "dp", 0)

    grad_mixed = split_heads(back_project(branch_one, out_self).astype(jnp.bfloat16))
    grad_q_one, grad_k_one, grad_v_one, grad_scores = attend_back(
        queries, keys, values, score_bias, self_valid, log_one, grad_mixed
    )
    grad_q_one = merge_heads(grad_q_one).astype(jnp.bfloat16)
    grad_k_one = merge_heads(grad_k_one).astype(jnp.bfloat16)
    grad_v_one = merge_heads(grad_v_one).astype(jnp.bfloat16)
    score_total = jnp.sum(grad_scores.astype(jnp.float32), 0).reshape(heads_local, length * length)
    bias_local = jnp.dot(score_total, onehot, precision=lax.Precision.HIGHEST).T
    grad_normed = (
        back_project(grad_q_one, query_self)
        + back_project(grad_k_one, key_self)
        + back_project(grad_v_one, value_self)
    )
    gains = jnp.stack(
        [
            jnp.sum(grad_normed * (resid0 * inv_one), axis=(0, 1)),
            grad_gain_cross,
            grad_gain_ffn,
        ]
    )
    gains = sum_mp(gains)
    share = width // dp_size
    bias_columns = jnp.tile(bias_local.reshape(share, -1), (dp_size, 1))
    self_grads = jnp.concatenate(
        [
            weight_grad(normed_one, grad_q_one),
            weight_grad(normed_one, grad_k_one),
            weight_grad(normed_one, grad_v_one),
            weight_grad(branch_one, mixed),
            gains.T,
            bias_columns,
        ],
        1,
    )
    self_grads = reduce_scatter(self_grads, "dp", 0)
    grad_normed = reduce_scatter(grad_normed, "mp", 1)
    grad_resid, _ = norm_backward(my_rows(resid0), my_rows(inv_one), gain_self, grad_normed)
    grad_targets = (my_rows(branch_one).astype(jnp.float32) + grad_resid).astype(jnp.bfloat16)

    part = query_self.shape[1]
    units = gate_proj.shape[1]
    gains_at = 4 * part
    return (
        output,
        grad_targets,
        mem_rows,
        self_grads[:, :part],
        self_grads[:, part : 2 * part],
        self_grads[:, 2 * part : 3 * part],
        self_grads[:, 3 * part : 4 * part].T,
        cross_grads[:, 0],
        cross_grads[:, 1],
        cross_grads[:, 2],
        cross_grads[:, 3].T,
        ffn_grads[:, :units],
        ffn_grads[:, units : 2 * units],
        ffn_grads[:, 2 * units :].T,
        self_grads[:, gains_at],
        self_grads[:, gains_at + 1],
        self_grads[:, gains_at + 2],
        self_grads[:, gains_at + 3 :].reshape(bias_local.shape),
    )


def solution(mesh):
    fits = mesh.shape["dp"] == 8 and mesh.shape["mp"] == 4
    return jax.shard_map(
        on_device if fits else on_device_permutes,
        mesh=mesh,
        in_specs=(
            P("dp", None, None),
            P("dp", None, None),
            P("dp", None, None),
            P("dp"),
            P("dp"),
            P(None, "mp"),
            P(None, "mp"),
            P(None, "mp"),
            P("mp", None),
            P(None, "mp"),
            P(None, "mp"),
            P(None, "mp"),
            P("mp", None),
            P(None, "mp"),
            P(None, "mp"),
            P("mp", None),
            P(),
            P(),
            P(),
            P(None, "mp"),
        ),
        out_specs=(
            P("dp", "mp", None),
            P("dp", "mp", None),
            P("dp", "mp", None),
            P("dp", "mp"),
            P("dp", "mp"),
            P("dp", "mp"),
            P("mp", "dp"),
            P("dp", "mp"),
            P("dp", "mp"),
            P("dp", "mp"),
            P("mp", "dp"),
            P("dp", "mp"),
            P("dp", "mp"),
            P("mp", "dp"),
            P("dp"),
            P("dp"),
            P("dp"),
            P(None, "mp"),
        ),
        check_vma=False,
    )
```

```python
import jax
import jax.numpy as jnp
import numpy as np
from jax import lax
from jax.experimental import pallas as pl
from jax.experimental.pallas import tpu as pltpu
from jax.sharding import PartitionSpec as P

HEAD_DIM = 64
BUCKETS = 32
MAX_DIST = 128


EPS = 1e-06
NEG = -1000000000.0


def bucket_table(length):
    distance = np.maximum(np.arange(length)[:, None] - np.arange(length)[None, :], 0)
    exact = BUCKETS // 2
    scaled = exact + (
        np.log(np.maximum(distance, 1) / exact) / np.log(MAX_DIST / exact) * (BUCKETS - exact)
    ).astype(np.int32)
    return np.where(distance < exact, distance, np.minimum(scaled, BUCKETS - 1)).astype(np.int32)


F32 = jnp.float32
BF16 = jnp.bfloat16
CHUNK = 256
COPIES = 120


def dot(left, right, left_dim, right_dim):
    return lax.dot_general(
        left, right, (((left_dim,), (right_dim,)), ((), ())), preferred_element_type=F32
    )


def dot_nn(left, right):
    return dot(left, right, 1, 0)


def dot_nt(left, right):
    return dot(left, right, 1, 1)


def dot_tn(left, right):
    return dot(left, right, 0, 0)


def unit_rows(resid):
    inv = lax.rsqrt(jnp.mean(resid * resid, -1, keepdims=True) + EPS)
    return inv, resid * inv


def norm_back(resid, gain, grad):
    inv, unit = unit_rows(resid)
    weighted = grad * gain
    grad_resid = inv * (weighted - unit * jnp.mean(weighted * unit, -1, keepdims=True))
    return grad_resid, jnp.sum(grad * unit, 0, keepdims=True)


def bucket_ranges(length):
    of_distance = bucket_table(length)[:, 0]
    ranges = []
    for k in range(BUCKETS):
        inside = np.flatnonzero(of_distance == k)
        ranges.append((int(inside[0]), int(inside[-1]) + 1) if len(inside) else (0, 0))
    return ranges


def place_of(chunk, order):
    y, z1, z2 = chunk % 2, chunk // 2 % 2, chunk // 4
    return 4 * y + 2 * z1 + z2 if order == "y" else 4 * z1 + 2 * y + z2


def layer_kernel(
    tlen_ref, mlen_ref, pos_ref, gain_self_ref, gain_cross_ref, gain_ffn_ref,
    x0_hbm, wq_hbm, wk_hbm, wv_hbm, wo_hbm, mem_hbm, cot_hbm, xq_hbm, xk_hbm, xv_hbm, xo_hbm, wg_hbm, wu_hbm, wd_hbm,
    out_ref, gt_ref, gm_ref, gf_ref, gx_ref, gs_ref, small_ref,
    q1, k1, v1, e1, r1, u1, o1, bias,
    part_send, part_recv, dn_recv, acc,
    x0_ref, wq_ref, wk_ref, wv_ref, wo_ref, mem, cot, wg, wu, wd, cross_w,
    x1, x2, n2, q2, kv2, e2, r2, u2, o2,
    n3, units, rows_low, rows_recv, rows_send_x, rows_recv_x,
    c2, turned, c1, f_low, f_recv0, f_recv1, f_recv2,
    x_recv0, x_recv1, x_recv2, x_send3, x_recv3,
    s_low, s_recv0, s_recv1, s_recv2, small, small_recv,
    local_sem, send_sem, recv_sem,
):
    me = lax.axis_index("mp")
    core, chip = lax.rem(me, 2), lax.div(me, 2)
    other_core, other_chip = 1 - core, 1 - chip
    by_core = 2 * chip + other_core
    by_x = 2 * other_chip + core
    across = 2 * other_chip + other_core
    at_dp = lax.axis_index("dp")
    bit_y, bit_z1, bit_z2 = lax.rem(at_dp, 2), lax.rem(lax.div(at_dp, 2), 2), lax.div(at_dp, 4)
    to_core, to_x, to_across = {"mp": by_core}, {"mp": by_x}, {"mp": across}
    to_y = {"dp": at_dp + 1 - 2 * bit_y}
    to_z1 = {"dp": at_dp + 2 - 4 * bit_z1}
    to_z2 = {"dp": at_dp + 4 - 8 * bit_z2}

    seqs, length, width = x0_ref.shape
    part = wq_ref.shape[0]
    heads = part // HEAD_DIM
    slots = mem.shape[0]
    blocks = cross_w.shape[0]
    share = width // 8
    quarter = length // blocks
    half = length // 2

    gain_self_row, gain_cross_row, gain_ffn_row = (
        ref[...].reshape(1, width) for ref in (gain_self_ref, gain_cross_ref, gain_ffn_ref)
    )
    sent = {}
    names = iter(range(COPIES))

    def fresh(count):
        return [next(names) for _ in range(count)]

    def remote(i, src, dst, device):
        return pltpu.make_async_remote_copy(
            src_ref=src, dst_ref=dst, send_sem=send_sem.at[i], recv_sem=recv_sem.at[i],
            device_id=device, device_id_type=pl.DeviceIdType.MESH,
        )

    def note(i, src, dst, device, waited=False):
        sent[i] = remote(i, src, dst, device)

    def send(i, src, dst, device):
        remote(i, src, dst, device).start()
        note(i, src, dst, device)

    def left(*sends):
        for i in sends:
            sent.pop(i).wait_send()

    def arrived(i, dst, device):
        remote(i, dst, dst, device).wait_recv()

    def add_rows(ref, at, recv, from_at):
        ref[at, :] = (ref[at, :].astype(F32) + recv[from_at, :].astype(F32)).astype(BF16)

    class Sum:
        def __init__(self, low, recvs, order):
            self.low, self.recvs = low, recvs
            bits = (bit_y, bit_z1, bit_z2) if order == "y" else (bit_z1, bit_y, bit_z2)
            self.devices = (to_y, to_z1, to_z2) if order == "y" else (to_z1, to_y, to_z2)
            self.ids = fresh(3)
            self.away, self.kept, self.away_in, self.kept_in = [], [], [], []
            base = 0
            for k, bit in enumerate(bits):
                count = (4 >> k) * share

                def rows(start):
                    return pl.ds(pl.multiple_of(start, share), count)

                self.away.append(rows(base + (1 - bit) * count))
                self.kept.append(rows(base + bit * count))
                self.away_in.append(rows((1 - bit) * count))
                self.kept_in.append(rows(bit * count))
                base = base + bit * count

        def copy(self, k):
            return (self.ids[k], self.low.at[self.away[k]], self.recvs[k], self.devices[k])

        def start(self):
            send(*self.copy(0))

        def start_with(self, landed):
            add_rows(self.low, self.away[0], landed, self.away[0])
            send(*self.copy(0))
            add_rows(self.low, self.kept[0], landed, self.kept[0])

        def step(self, k, in_loop=False):
            recv = self.recvs[k - 1]
            arrived(self.ids[k - 1], recv, self.devices[k - 1])
            add_rows(self.low, self.away[k], recv, self.away_in[k])
            if in_loop:
                remote(*self.copy(k)).start()
            else:
                send(*self.copy(k))
            add_rows(self.low, self.kept[k], recv, self.kept_in[k])

        def total(self):
            arrived(self.ids[2], self.recvs[2], self.devices[2])
            return self.low[self.kept[2], :].astype(F32) + self.recvs[2][...].astype(F32)

    def neighbour(t):
        flip_x, flip_core = lax.div(t, 2), lax.rem(t, 2)
        at_x = chip + flip_x * (other_chip - chip)
        return 2 * at_x + core + flip_core * (other_core - core)

    barrier = pltpu.get_barrier_semaphore()
    partners = (to_core, to_x, to_across, to_y, to_z1, to_z2)
    for device in partners:
        pl.semaphore_signal(barrier, inc=1, device_id=device, device_id_type=pl.DeviceIdType.MESH)

    loads = [
        pltpu.make_async_copy(source, target, local_sem.at[i])
        for i, (source, target) in enumerate((
            (xk_hbm, cross_w.at[me, 0:part]),
            (xv_hbm, cross_w.at[me, part : 2 * part]),
            (xq_hbm, cross_w.at[me, 2 * part : 3 * part]),
            (xo_hbm, cross_w.at[me, 3 * part : 4 * part]),
            (x0_hbm, x0_ref),
            (wq_hbm, wq_ref),
            (wk_hbm, wk_ref),
            (wv_hbm, wv_ref),
            (wo_hbm, wo_ref),
            (mem_hbm.at[me], mem),
            (cot_hbm, cot),
            (wg_hbm, wg),
            (wu_hbm, wu),
            (wd_hbm, wd),
        ))
    ]
    for load in loads[:9]:
        load.start()
    for load in loads[:4]:
        load.wait()
    pl.semaphore_wait(barrier, len(partners))

    def piece(flip_y, flip_z1, p):
        at_y = bit_y + flip_y * (1 - 2 * bit_y)
        at_z1 = bit_z1 + flip_z1 * (1 - 2 * bit_z1)
        start = part * (at_y + 2 * at_z1) + share * p
        return pl.ds(pl.multiple_of(start, share), share)

    lows, highs = slice(0, 2 * part), slice(2 * part, 4 * part)
    w_core, w_x, w_y, w_z1, w_on = fresh(2), fresh(2), fresh(3), fresh(3), fresh(8)

    def weights_on(i, rows, device, in_loop=False):
        copy = (i, cross_w.at[by_x, rows], cross_w.at[by_x, rows], device)
        if in_loop:
            remote(*copy).start()
        else:
            send(*copy)
        return copy

    def weights_from(i, rows, device):
        arrived(i, cross_w.at[by_x, rows], device)

    def weights_from_x(p, in_loop=False):
        rows = piece(0, 0, p)
        weights_from(w_x[p], rows, to_x)
        return [
            weights_on(w_y[p], rows, to_y, in_loop),
            weights_on(w_z1[p], rows, to_z1, in_loop),
            weights_on(w_on[p], rows, to_core, in_loop),
        ]

    def weights_near(p):
        from_y, from_z1 = piece(1, 0, p), piece(0, 1, p)
        weights_from(w_y[p], from_y, to_y)
        if p == 0:
            weights_on(w_z1[2], from_y, to_z1)
        weights_on(w_on[2 + p], from_y, to_core)
        weights_from(w_z1[p], from_z1, to_z1)
        if p == 1:
            weights_on(w_y[2], from_z1, to_y)
        weights_on(w_on[4 + p], from_z1, to_core)

    def weights_far():
        weights_from(w_z1[2], piece(1, 1, 0), to_z1)
        weights_on(w_on[6], piece(1, 1, 0), to_core)
        weights_from(w_y[2], piece(1, 1, 1), to_y)
        weights_on(w_on[7], piece(1, 1, 1), to_core)

    def weights_from_core():
        for i, (flip_y, flip_z1) in enumerate(((0, 0), (1, 0), (0, 1), (1, 1))):
            for p in range(2):
                rows = piece(flip_y, flip_z1, p)
                arrived(w_on[2 * i + p], cross_w.at[across, rows], to_core)

    for p in range(2):
        rows = piece(0, 0, p)
        send(w_x[p], cross_w.at[me, rows], cross_w.at[me, rows], to_x)
    send(w_core[0], cross_w.at[me, lows], cross_w.at[me, lows], to_core)
    send(w_core[1], cross_w.at[me, highs], cross_w.at[me, highs], to_core)
    for load in loads[9:]:
        load.start()

    key_at = lax.broadcasted_iota(jnp.int32, (length, length), 0)
    query_at = lax.broadcasted_iota(jnp.int32, (length, length), 1)
    distance = lax.broadcasted_iota(jnp.int32, (8, length), 1)
    for h in range(heads):
        of_distance = jnp.zeros((8, length), F32)
        for k, (first, last) in enumerate(bucket_ranges(length)):
            inside = (distance >= first) & (distance < last)
            of_distance = jnp.where(inside, pos_ref[h, k], of_distance)
        spread = jnp.broadcast_to(of_distance[0:1], (length, length))
        shifted = pltpu.roll(spread, 0, 1, stride=1, stride_axis=0)
        bias[h] = jnp.where(key_at <= query_at, shifted, NEG)

    for load in loads[4:9]:
        load.wait()

    x1_core0, x1_x, x1_core1 = fresh(3)

    def self_one(t, carry):
        s = neighbour(3 - t)

        @pl.when(t == 3)
        def _():
            weights_from_x(0, True)

        resid = x0_ref[s].astype(F32)
        _, unit = unit_rows(resid)
        n = (unit * gain_self_row).astype(BF16)
        q = dot_nt(n, wq_ref[...]).astype(BF16)
        k = dot_nt(n, wk_ref[...]).astype(BF16)
        v = dot_nt(n, wv_ref[...]).astype(BF16)
        q1[s], k1[s], v1[s] = q, k, v
        mixed = []
        for h in range(heads):
            cols = slice(h * HEAD_DIM, (h + 1) * HEAD_DIM)
            scores = dot_nt(k[:, cols], q[:, cols]) + bias[h]
            scores = jnp.where(key_at < tlen_ref[s], scores, NEG)
            e = jnp.exp(scores - jnp.max(scores, 0, keepdims=True))
            r = 1.0 / jnp.sum(e, 0, keepdims=True)
            e = e.astype(BF16)
            e1[s, h] = e
            r1[s, h] = r
            u = dot_tn(v[:, cols], e)
            u1[s, h] = u
            mixed.append(u * r)
        o = jnp.concatenate(mixed, 0).T.astype(BF16)
        o1[s] = o
        value = dot_nn(o, wo_ref[...])

        @pl.when(t == 0)
        def _():
            part_send[0] = value.astype(BF16)
            remote(x1_core0, part_send.at[0], part_recv.at[0], to_core).start()

        @pl.when(t == 1)
        def _():
            arrived(x1_core0, part_recv.at[0], to_core)
            part_send[1] = (value + part_recv[0].astype(F32)).astype(BF16)
            remote(x1_x, part_send.at[1], part_recv.at[1], to_x).start()

        @pl.when(t == 2)
        def _():
            part_send[2] = value.astype(BF16)
            remote(x1_core1, part_send.at[2], part_recv.at[2], to_core).start()

        @pl.when(t == 3)
        def _():
            x1[...] = resid + value

        return carry

    lax.fori_loop(0, seqs, self_one, 0)
    note(x1_core0, part_send.at[0], part_recv.at[0], to_core, waited=True)
    note(x1_x, part_send.at[1], part_recv.at[1], to_x)
    note(x1_core1, part_send.at[2], part_recv.at[2], to_core)

    first = piece(0, 0, 0)
    for i, device in ((w_y[0], to_y), (w_z1[0], to_z1), (w_on[0], to_core)):
        note(i, cross_w.at[by_x, first], cross_w.at[by_x, first], device)

    def keys_values(b):
        for at in range(0, slots, CHUNK):
            rows = slice(at, at + CHUNK)
            kv2[b, rows, :] = dot_nt(mem[rows, :], cross_w[b, lows, :]).astype(BF16)

    loads[9].wait()
    arrived(w_core[0], cross_w.at[by_core, lows], to_core)

    def near_keys(t, carry):
        keys_values(neighbour(t))
        return carry

    lax.fori_loop(0, 2, near_keys, 0)
    weights_from_x(1)
    weights_near(0)
    arrived(w_core[1], cross_w.at[by_core, highs], to_core)
    weights_near(1)
    arrived(x1_core1, part_recv.at[2], to_core)
    arrived(x1_x, part_recv.at[1], to_x)

    def enter_cross(i, carry):
        rows = pl.ds(pl.multiple_of(i * quarter, quarter), quarter)
        resid = x1[rows, :] + part_recv[1, rows, :].astype(F32) + part_recv[2, rows, :].astype(F32)
        x1[rows, :] = resid
        x2[rows, :] = resid
        n2[rows, :] = (unit_rows(resid)[1] * gain_cross_row).astype(BF16)
        return carry

    lax.fori_loop(0, blocks, enter_cross, 0)
    weights_far()
    slot_at = lax.broadcasted_iota(jnp.int32, (CHUNK, length), 0)

    def cross_one(t, carry):
        b = neighbour(t)

        @pl.when(t == 2)
        def _():
            keys_values(by_x)

        @pl.when(t == 3)
        def _():
            weights_from_core()
            keys_values(across)

        q = dot_nt(n2[...], cross_w[b, 2 * part : 3 * part, :]).astype(BF16)
        q2[b] = q
        mixed = []
        for h in range(heads):
            cols = slice(h * HEAD_DIM, (h + 1) * HEAD_DIM)
            cols_v = slice(part + h * HEAD_DIM, part + (h + 1) * HEAD_DIM)

            def scores_at(at):
                scores = dot_nt(kv2[b, at : at + CHUNK, cols], q[:, cols])
                return jnp.where(slot_at < mlen_ref[me] - at, scores, NEG)

            top = jnp.full((1, length), NEG, F32)
            for at in range(0, slots, CHUNK):
                top = jnp.maximum(top, jnp.max(scores_at(at), 0, keepdims=True))
            total = jnp.zeros((1, length), F32)
            u = jnp.zeros((HEAD_DIM, length), F32)
            for at in range(0, slots, CHUNK):
                rows = slice(at, at + CHUNK)
                e = jnp.exp(scores_at(at) - top)
                total = total + jnp.sum(e, 0, keepdims=True)
                e = e.astype(BF16)
                e2[b * heads + h, rows, :] = e
                u = u + dot_tn(kv2[b, rows, cols_v], e)
            r = 1.0 / total
            r2[b * heads + h] = r
            u2[b * heads + h] = u
            mixed.append(u * r)
        o = jnp.concatenate(mixed, 0).T.astype(BF16)
        o2[b] = o
        x2[...] += dot_nn(o, cross_w[b, 3 * part : 4 * part, :])
        return carry

    lax.fori_loop(0, blocks, cross_one, 0)

    n3_x, n3_core, n3_on = fresh(2), next(names), fresh(2)
    dn_near, dn_core, dn_x = next(names), fresh(2), fresh(2)
    halves = [slice(0, half), slice(half, length)]

    def enter_ffn(i, carry):
        rows = pl.ds(pl.multiple_of(i * quarter, quarter), quarter)
        n3[me, rows, :] = (unit_rows(x2[rows, :])[1] * gain_ffn_row).astype(BF16)
        return carry

    for i in range(2):
        lax.fori_loop(2 * i, 2 * i + 2, enter_ffn, 0)
        send(n3_x[i], n3.at[me, halves[i]], n3.at[me, halves[i]], to_x)
    send(n3_core, n3.at[me], n3.at[me], to_core)
    for load in loads[10:]:
        load.wait()
    left(x1_core0, x1_x, x1_core1)
    scale, cubic = 0.7978845608028654, 0.044715

    def turn(slot, value, first_col, order=None):
        value = value.T
        cols = pl.ds(first_col, value.shape[1])
        if order is None:
            turned[slot, :, cols] = value
            return
        for j in range(8):
            at = place_of(j, order) * share
            turned[slot, at : at + share, cols] = value[j * share : (j + 1) * share]

    def turn_normed(s):
        turn(0, n3[s], pl.multiple_of(s * length, length), "y")

    def pass_dn(i):
        arrived(dn_core[i], dn_recv.at[1, halves[i]], to_core)
        part_send[2, halves[i], :] = (
            part_send[2, halves[i], :].astype(F32) + dn_recv[1, halves[i], :].astype(F32)
        ).astype(BF16)
        remote(dn_x[i], part_send.at[2, halves[i]], dn_recv.at[2, halves[i]], to_x).start()

    def ffn_one(t, carry):
        late, odd = lax.div(t, 2), lax.rem(t, 2)
        at_x = chip + late * (other_chip - chip)
        near_core = (1 - late) * odd
        seq_a = 2 * at_x + core + near_core * (other_core - core)
        seq_b = 2 * at_x + core + (late + near_core) * (other_core - core)
        half_a, half_b = late * odd, 1 - late + late * odd
        in_a = pl.ds(pl.multiple_of(half_a * half, half), half)
        in_b = pl.ds(pl.multiple_of(half_b * half, half), half)
        rows_a = pl.ds(pl.multiple_of(seq_a * length + half_a * half, half), half)
        rows_b = pl.ds(pl.multiple_of(seq_b * length + half_b * half, half), half)

        @pl.when(t == 1)
        def _():
            arrived(n3_core, n3.at[by_core], to_core)

        @pl.when(t == 2)
        def _():
            turn_normed(me)
            turn_normed(by_core)
            arrived(n3_x[0], n3.at[by_x, halves[0]], to_x)
            remote(n3_on[0], n3.at[by_x, halves[0]], n3.at[by_x, halves[0]], to_core).start()
            turn(1, cot[0], 0, "z1")
            turn(1, cot[1], length, "z1")
            arrived(n3_on[0], n3.at[across, halves[0]], to_core)

        @pl.when(t == 3)
        def _():
            pass_dn(0)
            arrived(n3_x[1], n3.at[by_x, halves[1]], to_x)
            remote(n3_on[1], n3.at[by_x, halves[1]], n3.at[by_x, halves[1]], to_core).start()
            turn(1, cot[2], 2 * length, "z1")
            turn(1, cot[3], 3 * length, "z1")
            arrived(n3_on[1], n3.at[across, halves[1]], to_core)

        n = jnp.concatenate([n3[seq_a, in_a, :], n3[seq_b, in_b, :]], 0)
        c = jnp.concatenate([cot[seq_a, in_a, :], cot[seq_b, in_b, :]], 0)
        for at in range(0, wg.shape[1], CHUNK):
            cols = slice(at, at + CHUNK)
            a = dot_nn(n, wg[:, cols])
            b = dot_nn(n, wu[:, cols])
            dh = dot_nt(c, wd[cols, :])
            square = a * a
            slope = jnp.tanh(scale * (a + cubic * (a * square)))
            mid = 0.5 * (1.0 + slope)
            gelu = a * mid
            rise = mid + 0.5 * a * (1.0 - slope * slope) * (scale * (1.0 + 3.0 * cubic * square))
            for i, value in enumerate((dh * b * rise, dh * gelu, gelu * b)):
                value = value.astype(BF16)
                units[i, rows_a, cols] = value[:half]
                units[i, rows_b, cols] = value[half:]

        def both(i):
            return jnp.concatenate([units[i, rows_a, :], units[i, rows_b, :]], 0)

        dn = dot_nt(both(0), wg[...]) + dot_nt(both(1), wu[...])

        @pl.when(t == 0)
        def _():
            acc[...] = dn

        @pl.when(t == 1)
        def _():
            part_send[0] = dn.astype(BF16)
            remote(dn_near, part_send.at[0], dn_recv.at[0], to_core).start()

        for i in range(2):

            @pl.when(t == 2 + i)
            def _(i=i):
                part_send[1, halves[i], :] = dn[half:].astype(BF16)
                remote(
                    dn_core[i], part_send.at[1, halves[i]], dn_recv.at[1, halves[i]], to_core
                ).start()
                part_send[2, halves[i], :] = dn[:half].astype(BF16)

        own = jnp.where(t == 0, 1.0, 0.0)
        result = (dot_nn(both(2), wd[...]) + own * x2[...]).astype(BF16)
        rows_low[0, half_a, seq_a] = result[0:quarter]
        rows_low[1, half_a, seq_a] = result[quarter : 2 * quarter]
        rows_low[0, half_b, seq_b] = result[2 * quarter : 3 * quarter]
        rows_low[1, half_b, seq_b] = result[3 * quarter :]
        return carry

    lax.fori_loop(0, seqs, ffn_one, 0)
    pass_dn(1)
    for i in range(2):
        note(n3_on[i], n3.at[by_x, halves[i]], n3.at[by_x, halves[i]], to_core, waited=True)
        note(
            dn_core[i], part_send.at[1, halves[i]], dn_recv.at[1, halves[i]], to_core, waited=True
        )
        note(dn_x[i], part_send.at[2, halves[i]], dn_recv.at[2, halves[i]], to_x)
    note(dn_near, part_send.at[0], dn_recv.at[0], to_core)
    out_core, out_x = fresh(2)
    send(out_core, rows_low.at[other_core], rows_recv, to_core)
    turn_normed(by_x)
    turn_normed(across)
    orders = ("y", "y", "z1")
    f_sums = [
        Sum(f_low.at[i], [f_recv0.at[i], f_recv1.at[i], f_recv2.at[i]], orders[i]) for i in range(3)
    ]

    def ffn_grad(i, rows):
        f_low[i, rows, :] = dot_nn(turned[i // 2, rows, :], units[i]).astype(BF16)

    for i in (0, 2, 1):
        ffn_grad(i, f_sums[i].away[0])
        f_sums[i].start()
    for i in (0, 2, 1):
        ffn_grad(i, f_sums[i].kept[0])

    arrived(out_core, rows_recv, to_core)
    rows_send_x[...] = (
        rows_low[core, other_chip].astype(F32) + rows_recv[other_chip].astype(F32)
    ).astype(BF16)
    send(out_x, rows_send_x, rows_recv_x, to_x)

    arrived(dn_near, dn_recv.at[0], to_core)
    for i in range(2):
        arrived(dn_x[i], dn_recv.at[2, halves[i]], to_x)
    small[...] = jnp.zeros_like(small)

    def enter_back(i, carry):
        rows = pl.ds(pl.multiple_of(i * quarter, quarter), quarter)
        dn3 = acc[rows, :] + dn_recv[0, rows, :].astype(F32) + dn_recv[2, rows, :].astype(F32)
        grad, gain_ffn = norm_back(x2[rows, :], gain_ffn_row, dn3)
        dx2 = cot[me, rows, :].astype(F32) + grad
        acc[rows, :] = dx2
        c2[rows, :] = dx2.astype(BF16)
        small[0, 2:3, :] += gain_ffn
        return carry

    lax.fori_loop(0, blocks, enter_back, 0)

    def cross_back(b, carry):
        @pl.when(b == 3)
        def _():
            f_sums[0].step(1, True)
            f_sums[2].step(1, True)

        do = dot_nt(cross_w[b, 3 * part : 4 * part, :], c2[...])
        q = q2[b]
        dqs = []
        for h in range(heads):
            cols = slice(h * HEAD_DIM, (h + 1) * HEAD_DIM)
            cols_v = slice(part + h * HEAD_DIM, part + (h + 1) * HEAD_DIM)
            r = r2[b * heads + h]
            low = (do[cols] * r).astype(BF16)
            delta = r * jnp.sum(low.astype(F32) * u2[b * heads + h], 0, keepdims=True)
            dq = jnp.zeros((HEAD_DIM, length), F32)
            for at in range(0, slots, CHUNK):
                rows = slice(at, at + CHUNK)
                e = e2[b * heads + h, rows, :]
                dp = dot_nn(kv2[b, rows, cols_v], low)
                ds = (e.astype(F32) * (dp - delta)).astype(BF16)
                dq = dq + dot_tn(kv2[b, rows, cols], ds)
                kv2[b, rows, cols_v] = dot_nt(e, low).astype(BF16)
                kv2[b, rows, cols] = dot_nn(ds, q[:, cols]).astype(BF16)
            dqs.append(dq)
        q2[b] = jnp.concatenate(dqs, 0).T.astype(BF16)
        return carry

    lax.fori_loop(0, blocks, cross_back, 0)
    for i in (0, 2):
        note(*f_sums[i].copy(1))
    dn2 = dot_nn(q2[0], cross_w[0, 2 * part : 3 * part, :])
    for b in range(1, blocks):
        dn2 = dn2 + dot_nn(q2[b], cross_w[b, 2 * part : 3 * part, :])
    x2[...] = dn2

    def leave_cross(i, carry):
        rows = pl.ds(pl.multiple_of(i * quarter, quarter), quarter)
        grad, gain_cross = norm_back(x1[rows, :], gain_cross_row, x2[rows, :])
        c1[me, rows, :] = (acc[rows, :] + grad).astype(BF16)
        small[0, 1:2, :] += gain_cross
        return carry

    lax.fori_loop(0, blocks, leave_cross, 0)
    arrived(out_x, rows_recv_x, to_x)
    out_ref[...] = (
        rows_low[core, chip].astype(F32)
        + rows_recv[chip].astype(F32)
        + rows_recv_x[...].astype(F32)
    ).astype(BF16)
    left(out_core, out_x)
    c1_x, c1_core, c1_on = fresh(3)
    send(c1_x, c1.at[me], c1.at[me], to_x)
    send(c1_core, c1.at[me], c1.at[me], to_core)
    f_sums[1].step(1)
    turn(0, mem[...], 0)
    turn(1, n2[...], 0)
    turn(1, c2[...], length)

    def put(slabs, first_row, first_col, value):
        at = 0
        while at < value.shape[1]:
            slab, col = divmod(first_col + at, 256)
            count = min(256 - col, value.shape[1] - at)
            for i in range(value.shape[0] // share):
                row = place_of(first_row // share + i, orders[slab]) * share
                slabs[slab][row : row + share, col : col + count] = value[
                    i * share : (i + 1) * share, at : at + count
                ]
            at += count

    def cross_grads(b):
        slabs = [e2.at[3 * b + j] for j in range(3)]
        for at in range(0, width, width // 2):
            rows = slice(at, at + width // 2)
            put(slabs, at, 0, dot_nn(turned[0, rows, :], kv2[b]).astype(BF16))
            put(slabs, at, 2 * part, dot_nn(turned[1, rows, 0:length], q2[b]).astype(BF16))
            put(slabs, at, 3 * part, dot_nn(turned[1, rows, length : 2 * length], o2[b]).astype(BF16))

    def landing(i, j):
        return units.at[j, 0:width, 256 * i : 256 * (i + 1)]

    x_core = [fresh(3) for _ in range(2)]
    for i in range(2):
        b = 2 * i + other_core
        cross_grads(b)
        if i == 0:
            arrived(c1_core, c1.at[by_core], to_core)
        for j in range(3):
            send(x_core[i][j], e2.at[3 * b + j, 0:width], landing(i, j), to_core)
    for i in (0, 2):
        f_sums[i].step(2)
    x_sums = []
    for i in range(2):
        b = 2 * i + core
        cross_grads(b)
        x_sums.append([
            Sum(e2.at[3 * b + j], [x_recv0.at[i, j], x_recv1.at[i, j], x_recv2.at[i, j]], orders[j])
            for j in range(3)
        ])
    for j in (0, 2, 1):
        for i in range(2):
            arrived(x_core[i][j], landing(i, j), to_core)
            x_sums[i][j].start_with(landing(i, j))

    left(*n3_x, n3_core, *n3_on)
    gm_x, gm_across, gm_core = fresh(3)

    def memory_grad(target):
        rows = pl.ds(pl.multiple_of(target * CHUNK, CHUNK), CHUNK)
        for at in range(0, width, CHUNK):
            cols = slice(at, at + CHUNK)
            total = dot_nn(kv2[0, rows, :], cross_w[0, lows, cols])
            for b in range(1, blocks):
                total = total + dot_nn(kv2[b, rows, :], cross_w[b, lows, cols])
            n3[target, :, cols] = total.astype(BF16)

    memory_grad(by_x)
    send(gm_x, n3.at[by_x], gm_ref.at[me], to_x)
    memory_grad(across)
    send(gm_across, n3.at[across], gm_ref.at[me], to_across)

    bias[...] = jnp.zeros_like(bias)

    def self_back(t, carry):
        s = neighbour(t)

        @pl.when(t == 2)
        def _():
            arrived(c1_x, c1.at[by_x], to_x)
            remote(c1_on, c1.at[by_x], c1.at[by_x], to_core).start()
            f_sums[1].step(2, True)

        @pl.when(t == 3)
        def _():
            arrived(c1_on, c1.at[across], to_core)
            for i in range(2):
                x_sums[i][0].step(1, True)
                x_sums[i][2].step(1, True)

        do = dot_nt(wo_ref[...], c1[s])
        dqs = []
        for h in range(heads):
            cols = slice(h * HEAD_DIM, (h + 1) * HEAD_DIM)
            r = r1[s, h]
            low = (do[cols] * r).astype(BF16)
            delta = r * jnp.sum(low.astype(F32) * u1[s, h], 0, keepdims=True)
            e = e1[s, h]
            dp = dot_nn(v1[s, :, cols], low)
            ds = (e.astype(F32) * (dp - delta)).astype(BF16)
            bias[h] += ds.astype(F32)
            dqs.append(dot_tn(k1[s, :, cols], ds))
            v1[s, :, cols] = dot_nt(e, low).astype(BF16)
            k1[s, :, cols] = dot_nn(ds, q1[s, :, cols]).astype(BF16)
        q1[s] = jnp.concatenate(dqs, 0).T.astype(BF16)
        dn = dot_nn(q1[s], wq_ref[...]) + dot_nn(k1[s], wk_ref[...]) + dot_nn(v1[s], wv_ref[...])
        acc[...] = dn
        for i in range(blocks):
            rows = slice(i * quarter, (i + 1) * quarter)
            unit = unit_rows(x0_ref[s, rows, :].astype(F32))[1]
            small[0, 0:1, :] += jnp.sum(acc[rows, :] * unit, 0, keepdims=True)
            rows_low[i % 2, i // 2, s] = acc[rows, :].astype(BF16)
        return carry

    lax.fori_loop(0, seqs, self_back, 0)
    note(c1_on, c1.at[by_x], c1.at[by_x], to_core, waited=True)
    note(*f_sums[1].copy(2))
    for i in range(2):
        note(*x_sums[i][2].copy(1))
        note(*x_sums[i][0].copy(1))
    dn1_core, dn1_x, small_y, small_z1, small_z2 = fresh(5)
    small_mp = fresh(3)
    send(dn1_core, rows_low.at[other_core], rows_recv, to_core)
    for h in range(heads):
        total = bias[h]
        step = 1
        while step < length:
            total = jnp.where((key_at & step) != 0, pltpu.roll(total, length - step, 1), total)
            step *= 2
        small[1, h : h + 1, 0:length] = jnp.sum(total, 0, keepdims=True)
    pairs = [pl.ds(2 * i, 2) for i in range(4)]
    send(small_y, small.at[pairs[0]], small_recv.at[pairs[0]], to_y)

    for s in range(seqs):
        _, unit = unit_rows(x0_ref[s].astype(F32))
        turn(0, (unit * gain_self_row).astype(BF16), s * length)
        turn(1, c1[s], s * length)
    slabs = [s_low.at[j] for j in range(3)]
    s_sums = [
        Sum(s_low.at[j], [s_recv0.at[j], s_recv1.at[j], s_recv2.at[j]], orders[j]) for j in range(3)
    ]
    for i, ref in enumerate((k1, v1, q1, o1)):
        right = ref[...].reshape(seqs * length, part)
        for at in range(0, width, width // 2):
            value = dot_nn(turned[i // 3, at : at + width // 2, :], right).astype(BF16)
            put(slabs, at, i * part, value)
        if i:
            s_sums[i - 1].start()

    arrived(dn1_core, rows_recv, to_core)
    rows_send_x[...] = (
        rows_low[core, other_chip].astype(F32) + rows_recv[other_chip].astype(F32)
    ).astype(BF16)
    send(dn1_x, rows_send_x, rows_recv_x, to_x)

    def pass_small(i, came, device, goes, onward):
        arrived(came, small_recv.at[pairs[i]], device)
        small[pairs[i + 1]] = small[pairs[i]] + small_recv[pairs[i]]
        if goes is not None:
            send(goes, small.at[pairs[i + 1]], small_recv.at[pairs[i + 1]], onward)

    pass_small(0, small_y, to_y, small_z1, to_z1)
    memory_grad(by_core)
    send(gm_core, n3.at[by_core], gm_ref.at[me], to_core)
    memory_grad(me)
    own_rows = pltpu.make_async_copy(n3.at[me], gm_ref.at[me], local_sem.at[15])
    own_rows.start()

    for i in range(2):
        x_sums[i][0].step(2)
    pass_small(1, small_z1, to_z1, small_z2, to_z2)
    for i in range(2):
        x_sums[i][1].step(1)
    s_sums[2].step(1)
    for i in range(2):
        x_sums[i][2].step(2)
    s_sums[0].step(1)
    for i in range(2):
        x_sums[i][1].step(2)
    s_sums[2].step(2)
    s_sums[1].step(1)
    for i in range(3):
        gf_ref[i] = f_sums[i].total()

    arrived(dn1_x, rows_recv_x, to_x)
    my_rows = pl.ds(pl.multiple_of(me * quarter, quarter), quarter)
    for s in range(seqs):
        dn = (
            rows_low[core, chip, s].astype(F32)
            + rows_recv[chip, s].astype(F32)
            + rows_recv_x[s].astype(F32)
        )
        grad, _ = norm_back(x0_ref[s, my_rows, :].astype(F32), gain_self_row, dn)
        gt_ref[s] = (c1[s, my_rows, :].astype(F32) + grad).astype(BF16)
    s_sums[0].step(2)
    s_sums[1].step(2)

    last_x = next(names)
    for i in range(2):
        for j in range(3):
            arrived(x_sums[i][j].ids[2], x_recv2.at[i, j], to_z2)

    def cross_total(at, j):
        rows = x_sums[0][j].kept[2]
        return e2[3 * (2 * at + core) + j, rows, :].astype(F32) + x_recv2[at, j].astype(F32)

    for j in range(3):
        x_send3[j] = cross_total(other_chip, j).astype(BF16)
    send(last_x, x_send3, x_recv3, to_x)
    pass_small(2, small_z2, to_z2, None, None)
    mp_peers = (to_core, to_x, to_across)
    for i, device in enumerate(mp_peers):
        send(small_mp[i], small.at[6], small_recv.at[6 + i], device)
    for j in range(3):
        gs_ref[j] = s_sums[j].total()
    arrived(last_x, x_recv3, to_x)
    for j in range(3):
        gx_ref[j] = cross_total(chip, j) + x_recv3[j].astype(F32)
    for i, device in enumerate(mp_peers):
        arrived(small_mp[i], small_recv.at[6 + i], device)
    small_ref[0] = small[6] + small_recv[6] + small_recv[7] + small_recv[8]
    small_ref[1] = small[7]
    arrived(gm_x, gm_ref.at[by_x], to_x)
    arrived(gm_across, gm_ref.at[across], to_across)
    arrived(gm_core, gm_ref.at[by_core], to_core)
    own_rows.wait()
    for copy in sent.values():
        copy.wait_send()


def finish_kernel(
    gf_ref, gx_ref, gs_ref, small_ref, onehot_ref, out_ref, gt_ref, gm_ref,
    out_o, gt_o, gm_o, sq_o, sk_o, sv_o, so_o, cq_o, ck_o, cv_o, co_o, gg_o, gu_o, gd_o,
    gain_self_o, gain_cross_o, gain_ffn_o, bias_o,
):
    part, share = sq_o.shape[1], sq_o.shape[0]
    width = small_ref.shape[2]
    out_o[...], gt_o[...], gm_o[...] = out_ref[...], gt_ref[...], gm_ref[...]
    gg_o[...], gu_o[...], gd_o[...] = gf_ref[0], gf_ref[1], gf_ref[2]
    for source, refs in ((gx_ref, (ck_o, cv_o, cq_o, co_o)), (gs_ref, (sk_o, sv_o, sq_o, so_o))):
        value = jnp.concatenate([source[0], source[1], source[2]], 1)
        for i in range(3):
            refs[i][...] = value[:, i * part : (i + 1) * part]
        refs[3][...] = value[:, 3 * part :].T
    shift = width - lax.axis_index("dp") * share
    gains = pltpu.roll(small_ref[0], shift, 1)
    for i, ref in enumerate((gain_self_o, gain_cross_o, gain_ffn_o)):
        ref[...] = gains[i : i + 1, 0:share]
    bias_o[...] = lax.dot_general(
        small_ref[1, 0 : bias_o.shape[0], 0 : onehot_ref.shape[0]], onehot_ref[...], (((1,), (0,)), ((), ())),
        precision=lax.Precision.HIGHEST, preferred_element_type=F32,
    )


VMEM = pl.BlockSpec(memory_space=pltpu.VMEM)
SMEM = pl.BlockSpec(memory_space=pltpu.SMEM)
ANY = pl.BlockSpec(memory_space=pl.ANY)


def on_device(
    targets,
    memory,
    cotangent,
    target_len,
    memory_len,
    query_self,
    key_self,
    value_self,
    out_self,
    query_cross,
    key_cross,
    value_cross,
    out_cross,
    gate_proj,
    up_proj,
    down_proj,
    gain_self,
    gain_cross,
    gain_ffn,
    pos_bias,
):
    seqs, length, width = targets.shape
    slots = memory.shape[1]
    part = query_self.shape[1]
    units = gate_proj.shape[1]
    heads = part // HEAD_DIM
    blocks = lax.axis_size("mp")
    dp_size = lax.axis_size("dp")
    share = width // dp_size
    quarter = length // blocks
    head_all = heads * blocks

    onehot = jnp.asarray(
        (bucket_table(length)[:, 0][:, None] == np.arange(BUCKETS)[None, :]).astype(np.float32)
    )
    def low(*shape):
        return pltpu.VMEM(shape, BF16)

    def full(*shape):
        return pltpu.VMEM(shape, F32)

    def sums(count, columns):
        return [low(count, 4 * share, columns), low(count, 2 * share, columns), low(count, share, columns)]

    scratch = [
        low(seqs, length, part), low(seqs, length, part), low(seqs, length, part),
        low(seqs, heads, length, length), full(seqs, heads, 1, length),
        full(seqs, heads, HEAD_DIM, length), low(seqs, length, part), full(heads, length, length),
        low(3, length, width), low(3, length, width), low(3, length, width),
        full(length, width),
        low(seqs, length, width), low(part, width), low(part, width), low(part, width),
        low(part, width), low(slots, width), low(seqs, length, width),
        low(width, units), low(width, units), low(units, width), low(blocks, 4 * part, width),
        full(length, width), full(length, width), low(length, width), low(blocks, length, part),
        low(blocks, slots, 2 * part), low(head_all, slots, length), full(head_all, 1, length),
        full(head_all, HEAD_DIM, length), low(blocks, length, part),
        low(seqs, length, width), low(3, seqs * length, units),
        low(2, 2, seqs, quarter, width), low(2, seqs, quarter, width),
        low(seqs, quarter, width), low(seqs, quarter, width),
        low(length, width), low(2, width, seqs * length), low(seqs, length, width),
        low(3, width, units), *sums(3, units),
        low(2, 3, 4 * share, 256), low(2, 3, 2 * share, 256), low(2, 3, share, 256),
        low(3, share, 256), low(3, share, 256),
        low(3, width, 256), *sums(3, 256),
        full(8, 8, width), full(9, 8, width),
        pltpu.SemaphoreType.DMA((16,)),
        pltpu.SemaphoreType.DMA((COPIES,)),
        pltpu.SemaphoreType.DMA((COPIES,)),
    ]
    struct = jax.ShapeDtypeStruct
    rows = struct((seqs, quarter, width), BF16)
    out, gt, gm, gf, gx, gs, small = pl.pallas_call(
        layer_kernel,
        out_shape=[
            rows,
            rows,
            struct((seqs, slots // blocks, width), BF16),
            struct((3, share, units), F32),
            struct((3, share, 256), F32),
            struct((3, share, 256), F32),
            struct((2, 8, width), F32),
        ],
        in_specs=[SMEM] * 3 + [VMEM] * 3 + [ANY] * 14,
        out_specs=[VMEM, VMEM, ANY, VMEM, VMEM, VMEM, VMEM],
        scratch_shapes=scratch,
        compiler_params=pltpu.CompilerParams(
            collective_id=0, has_side_effects=True, vmem_limit_bytes=63 * 2**20
        ),
        cost_estimate=pl.CostEstimate(flops=24 * 10**9, bytes_accessed=2**24, transcendentals=0),
        name="layer",
    )(
        target_len, memory_len, pos_bias.T,
        gain_self, gain_cross, gain_ffn, targets,
        query_self.T, key_self.T, value_self.T, out_self, memory, cotangent, query_cross.T, key_cross.T, value_cross.T, out_cross,
        gate_proj, up_proj, down_proj,
    )
    square = struct((share, part), F32)
    turned = struct((part, share), F32)
    (
        out, gt, gm, sq, sk, sv, so, cq, ck, cv, co, gg, gu, gd,
        grad_self, grad_cross, grad_ffn, bias,
    ) = pl.pallas_call(
        finish_kernel,
        out_shape=[
            rows, rows, struct((seqs, slots // blocks, width), BF16),
            square, square, square, turned, square, square, square, turned,
            struct((share, units), F32), struct((share, units), F32), struct((share, units), F32),
            struct((1, share), F32), struct((1, share), F32), struct((1, share), F32),
            struct((heads, BUCKETS), F32),
        ],
        in_specs=[VMEM] * 8,
        out_specs=[VMEM] * 18,
        compiler_params=pltpu.CompilerParams(vmem_limit_bytes=62 * 2**20),
        name="finish",
    )(gf, gx, gs, small, onehot, out, gt, gm)
    return (
        out, gt, gm, sq, sk, sv, so, cq, ck, cv, co, gg, gu, gd.T,
        grad_self[0], grad_cross[0], grad_ffn[0], bias.T,
    )


def project(inputs, weight):
    return jnp.einsum("bld,df->blf", inputs, weight, preferred_element_type=jnp.float32)


def back_project(gradient, weight):
    return jnp.einsum("blf,df->bld", gradient, weight, preferred_element_type=jnp.float32)


def weight_grad(inputs, gradient):
    return jnp.einsum("bld,blf->df", inputs, gradient, preferred_element_type=jnp.float32)


def norm_forward(resid, gain):
    inv_rms = lax.rsqrt(jnp.mean(resid * resid, -1, keepdims=True) + EPS)
    return (resid * inv_rms * gain, inv_rms)


def norm_backward(resid, inv_rms, gain, grad_normed):
    unit_rows = resid * inv_rms
    grad_gain = jnp.sum(grad_normed * unit_rows, axis=(0, 1))
    weighted = grad_normed * gain
    grad_resid = inv_rms * (
        weighted - unit_rows * jnp.mean(weighted * unit_rows, -1, keepdims=True)
    )
    return (grad_resid, grad_gain)


def scores_of(queries, keys, score_bias, valid):
    scores = (
        jnp.einsum("bihe,bjhe->bhij", queries, keys, preferred_element_type=jnp.float32)
        + score_bias
    )
    return jnp.where(valid, scores, NEG)


def attend(queries, keys, values, score_bias, valid):
    scores = scores_of(queries, keys, score_bias, valid)
    row_max = jnp.max(scores, -1, keepdims=True)
    log_total = row_max + jnp.log(jnp.sum(jnp.exp(scores - row_max), -1, keepdims=True))
    attn_probs = jnp.exp(scores - log_total).astype(jnp.bfloat16)
    mixed = jnp.einsum("bhij,bjhe->bihe", attn_probs, values, preferred_element_type=jnp.float32)
    return (mixed, log_total)


def attend_back(queries, keys, values, score_bias, valid, log_total, grad_mixed):
    attn_probs = jnp.exp(scores_of(queries, keys, score_bias, valid) - log_total)
    grad_values = jnp.einsum(
        "bhij,bihe->bjhe",
        attn_probs.astype(jnp.bfloat16),
        grad_mixed,
        preferred_element_type=jnp.float32,
    )
    grad_probs = jnp.einsum(
        "bihe,bjhe->bhij", grad_mixed, values, preferred_element_type=jnp.float32
    )
    grad_scores = attn_probs * (grad_probs - jnp.sum(attn_probs * grad_probs, -1, keepdims=True))
    grad_low = grad_scores.astype(jnp.bfloat16)
    grad_queries = jnp.einsum("bhij,bjhe->bihe", grad_low, keys, preferred_element_type=jnp.float32)
    grad_keys = jnp.einsum("bhij,bihe->bjhe", grad_low, queries, preferred_element_type=jnp.float32)
    return (grad_queries, grad_keys, grad_values, grad_low)


def swap(value, axis, bit):
    return lax.ppermute(value, axis, [(i, i ^ bit) for i in range(lax.axis_size(axis))])


def bits_of(axis):
    return [1 << i for i in range(lax.axis_size(axis).bit_length() - 1)]


def split_bits(value, axis, dim):
    steps = len(bits_of(axis))
    shape = value.shape
    return value.reshape(
        shape[:dim] + (2,) * steps + (shape[dim] >> steps,) + shape[dim + 1 :]
    )


def own_bit(axis, bit):
    return (lax.axis_index(axis) & bit) // bit


def halve(value, axis, bit, dim):
    mine = own_bit(axis, bit)
    kept = lax.dynamic_index_in_dim(value, mine, dim, keepdims=False)
    sent = lax.dynamic_index_in_dim(value, 1 - mine, dim, keepdims=False)
    arrived = swap(sent.astype(jnp.bfloat16), axis, bit)
    return kept + arrived.astype(jnp.float32)


def reduce_scatter(value, axis, dim):
    bits = bits_of(axis)
    value = split_bits(value, axis, dim)
    for at, bit in enumerate(bits):
        value = halve(value, axis, bit, dim + len(bits) - 1 - at)
    return value


def gather_mp(value):
    value = value[None]
    for bit in reversed(bits_of("mp")):
        other = swap(value, "mp", bit)
        first = own_bit("mp", bit) == 0
        low = jnp.where(first, value, other)
        high = jnp.where(first, other, value)
        value = jnp.stack([low, high], 1 if bit == 1 else 0)
        value = value.reshape((-1,) + value.shape[2:])
    return value


def exchange_mp(value):
    count = lax.axis_size("mp")
    value = split_bits(value, "mp", 0)[None]
    steps = len(bits_of("mp"))
    for at, bit in enumerate(bits_of("mp")):
        dim = steps - at
        mine = own_bit("mp", bit)
        kept = lax.dynamic_index_in_dim(value, mine, dim, keepdims=False)
        sent = lax.dynamic_index_in_dim(value, 1 - mine, dim, keepdims=False)
        arrived = swap(sent, "mp", bit)
        first = mine == 0
        low = jnp.where(first, kept, arrived)
        high = jnp.where(first, arrived, kept)
        value = jnp.stack([low, high], 0)
        value = value.reshape((-1,) + value.shape[2:])
    return value.reshape((count,) + value.shape[1:])


def sum_mp(value):
    for bit in bits_of("mp"):
        value = value + swap(value, "mp", bit)
    return value


def on_device_permutes(
    targets,
    memory,
    cotangent,
    target_len,
    memory_len,
    query_self,
    key_self,
    value_self,
    out_self,
    query_cross,
    key_cross,
    value_cross,
    out_cross,
    gate_proj,
    up_proj,
    down_proj,
    gain_self,
    gain_cross,
    gain_ffn,
    pos_bias,
):
    length = targets.shape[1]
    heads_local = query_self.shape[1] // HEAD_DIM
    mp_size = lax.axis_size("mp")
    dp_size = lax.axis_size("dp")
    mp_index = lax.axis_index("mp")
    row_share = length // mp_size
    width = targets.shape[2]

    def split_heads(value):
        return value.reshape(value.shape[0], value.shape[1], -1, HEAD_DIM)

    def merge_heads(value):
        return value.reshape(value.shape[0], value.shape[1], -1)

    def my_rows(value):
        return lax.dynamic_slice_in_dim(value, mp_index * row_share, row_share, 1)

    def mine(value):
        return lax.dynamic_index_in_dim(value, mp_index, 0)

    positions = jnp.arange(length)
    self_valid = (
        (positions[None, :] <= positions[:, None])[None]
        & (positions[None, None, :] < target_len[:, None, None])
    )[:, None]
    mem_positions = jnp.arange(memory.shape[1])
    cross_valid = (mem_positions[None, :] < mine(memory_len)[:, None])[:, None, None, :]
    onehot = (
        jnp.asarray(bucket_table(length)).reshape(-1)[:, None] == jnp.arange(BUCKETS)[None, :]
    ).astype(jnp.float32)
    score_bias = (
        jnp.dot(onehot, pos_bias, precision=lax.Precision.HIGHEST)
        .reshape(length, length, heads_local)
        .transpose(2, 0, 1)[None]
    )
    cross_in = gather_mp(jnp.stack([query_cross, key_cross, value_cross]))
    cross_in = cross_in.transpose(1, 2, 0, 3).reshape(3, width, -1)
    cross_q, cross_k, cross_v = cross_in[0], cross_in[1], cross_in[2]
    cross_o = gather_mp(out_cross).reshape(-1, width)

    resid0 = targets.astype(jnp.float32)
    normed_one, inv_one = norm_forward(resid0, gain_self)
    normed_one = normed_one.astype(jnp.bfloat16)
    queries = split_heads(project(normed_one, query_self).astype(jnp.bfloat16))
    keys = split_heads(project(normed_one, key_self).astype(jnp.bfloat16))
    values = split_heads(project(normed_one, value_self).astype(jnp.bfloat16))
    mixed, log_one = attend(queries, keys, values, score_bias, self_valid)
    mixed = merge_heads(mixed).astype(jnp.bfloat16)
    resid1 = mine(resid0) + reduce_scatter(project(mixed, out_self), "mp", 0)

    mem_own = mine(memory)
    normed_two, inv_two = norm_forward(resid1, gain_cross)
    normed_two = normed_two.astype(jnp.bfloat16)
    queries_two = split_heads(project(normed_two, cross_q).astype(jnp.bfloat16))
    mem_keys = split_heads(project(mem_own, cross_k).astype(jnp.bfloat16))
    mem_values = split_heads(project(mem_own, cross_v).astype(jnp.bfloat16))
    mixed_two, log_two = attend(queries_two, mem_keys, mem_values, 0.0, cross_valid)
    mixed_two = merge_heads(mixed_two).astype(jnp.bfloat16)
    resid2 = resid1 + project(mixed_two, cross_o)
    normed_three, inv_three = norm_forward(resid2, gain_ffn)
    normed_all = gather_mp(normed_three.astype(jnp.bfloat16)[0])

    gate_pre = project(normed_all, gate_proj)
    up_pre = project(normed_all, up_proj)

    def gated(gate_in, up_in):
        return jax.nn.gelu(gate_in, approximate=True) * up_in

    hidden, hidden_pull = jax.vjp(gated, gate_pre, up_pre)
    hidden = hidden.astype(jnp.bfloat16)
    grad_gate_pre, grad_up_pre = hidden_pull(back_project(cotangent, down_proj))
    grad_gate_pre = grad_gate_pre.astype(jnp.bfloat16)
    grad_up_pre = grad_up_pre.astype(jnp.bfloat16)
    grad_normed = reduce_scatter(
        back_project(grad_gate_pre, gate_proj) + back_project(grad_up_pre, up_proj), "mp", 0
    )
    result = project(hidden, down_proj)
    own = (jnp.arange(targets.shape[0]) == mp_index)[:, None, None]
    result = result + jnp.where(own, resid2, 0.0)
    output = reduce_scatter(result, "mp", 1).astype(jnp.bfloat16)
    ffn_grads = jnp.concatenate(
        [
            weight_grad(normed_all, grad_gate_pre),
            weight_grad(normed_all, grad_up_pre),
            weight_grad(cotangent, hidden),
        ],
        1,
    )
    ffn_grads = reduce_scatter(ffn_grads, "dp", 0)
    grad_resid, grad_gain_ffn = norm_backward(resid2, inv_three, gain_ffn, grad_normed)
    grad_two = mine(cotangent).astype(jnp.float32) + grad_resid

    branch_two = grad_two.astype(jnp.bfloat16)
    grad_mixed_two = split_heads(back_project(branch_two, cross_o).astype(jnp.bfloat16))
    grad_q_two, grad_mem_keys, grad_mem_values, _ = attend_back(
        queries_two, mem_keys, mem_values, 0.0, cross_valid, log_two, grad_mixed_two
    )
    grad_q_two = merge_heads(grad_q_two).astype(jnp.bfloat16)
    grad_normed = back_project(grad_q_two, cross_q)
    grad_resid, grad_gain_cross = norm_backward(resid1, inv_two, gain_cross, grad_normed)
    grad_one = grad_two + grad_resid
    branch_one = gather_mp(grad_one.astype(jnp.bfloat16)[0])
    grad_mem_keys = merge_heads(grad_mem_keys).astype(jnp.bfloat16)
    grad_mem_values = merge_heads(grad_mem_values).astype(jnp.bfloat16)
    mem_grad = back_project(grad_mem_keys, cross_k) + back_project(grad_mem_values, cross_v)
    mem_rows = exchange_mp(mem_grad[0].astype(jnp.bfloat16))
    cross_grads = jnp.stack(
        [
            weight_grad(normed_two, grad_q_two),
            weight_grad(mem_own, grad_mem_keys),
            weight_grad(mem_own, grad_mem_values),
            weight_grad(branch_two, mixed_two),
        ],
        1,
    )
    cross_grads = reduce_scatter(cross_grads, "mp", 2)
    cross_grads = reduce_scatter(cross_grads, "dp", 0)

    grad_mixed = split_heads(back_project(branch_one, out_self).astype(jnp.bfloat16))
    grad_q_one, grad_k_one, grad_v_one, grad_scores = attend_back(
        queries, keys, values, score_bias, self_valid, log_one, grad_mixed
    )
    grad_q_one = merge_heads(grad_q_one).astype(jnp.bfloat16)
    grad_k_one = merge_heads(grad_k_one).astype(jnp.bfloat16)
    grad_v_one = merge_heads(grad_v_one).astype(jnp.bfloat16)
    score_total = jnp.sum(grad_scores.astype(jnp.float32), 0).reshape(heads_local, length * length)
    bias_local = jnp.dot(score_total, onehot, precision=lax.Precision.HIGHEST).T
    grad_normed = (
        back_project(grad_q_one, query_self)
        + back_project(grad_k_one, key_self)
        + back_project(grad_v_one, value_self)
    )
    gains = jnp.stack(
        [
            jnp.sum(grad_normed * (resid0 * inv_one), axis=(0, 1)),
            grad_gain_cross,
            grad_gain_ffn,
        ]
    )
    gains = sum_mp(gains)
    share = width // dp_size
    bias_columns = jnp.tile(bias_local.reshape(share, -1), (dp_size, 1))
    self_grads = jnp.concatenate(
        [
            weight_grad(normed_one, grad_q_one),
            weight_grad(normed_one, grad_k_one),
            weight_grad(normed_one, grad_v_one),
            weight_grad(branch_one, mixed),
            gains.T,
            bias_columns,
        ],
        1,
    )
    self_grads = reduce_scatter(self_grads, "dp", 0)
    grad_normed = reduce_scatter(grad_normed, "mp", 1)
    grad_resid, _ = norm_backward(my_rows(resid0), my_rows(inv_one), gain_self, grad_normed)
    grad_targets = (my_rows(branch_one).astype(jnp.float32) + grad_resid).astype(jnp.bfloat16)

    part = query_self.shape[1]
    units = gate_proj.shape[1]
    gains_at = 4 * part
    return (
        output,
        grad_targets,
        mem_rows,
        self_grads[:, :part],
        self_grads[:, part : 2 * part],
        self_grads[:, 2 * part : 3 * part],
        self_grads[:, 3 * part : 4 * part].T,
        cross_grads[:, 0],
        cross_grads[:, 1],
        cross_grads[:, 2],
        cross_grads[:, 3].T,
        ffn_grads[:, :units],
        ffn_grads[:, units : 2 * units],
        ffn_grads[:, 2 * units :].T,
        self_grads[:, gains_at],
        self_grads[:, gains_at + 1],
        self_grads[:, gains_at + 2],
        self_grads[:, gains_at + 3 :].reshape(bias_local.shape),
    )


def solution(mesh):
    fits = mesh.shape["dp"] == 8 and mesh.shape["mp"] == 4
    return jax.shard_map(
        on_device if fits else on_device_permutes,
        mesh=mesh,
        in_specs=(
            P("dp", None, None),
            P("dp", None, None),
            P("dp", None, None),
            P("dp"),
            P("dp"),
            P(None, "mp"),
            P(None, "mp"),
            P(None, "mp"),
            P("mp", None),
            P(None, "mp"),
            P(None, "mp"),
            P(None, "mp"),
            P("mp", None),
            P(None, "mp"),
            P(None, "mp"),
            P("mp", None),
            P(),
            P(),
            P(),
            P(None, "mp"),
        ),
        out_specs=(
            P("dp", "mp", None),
            P("dp", "mp", None),
            P("dp", "mp", None),
            P("dp", "mp"),
            P("dp", "mp"),
            P("dp", "mp"),
            P("mp", "dp"),
            P("dp", "mp"),
            P("dp", "mp"),
            P("dp", "mp"),
            P("mp", "dp"),
            P("dp", "mp"),
            P("dp", "mp"),
            P("mp", "dp"),
            P("dp"),
            P("dp"),
            P("dp"),
            P(None, "mp"),
        ),
        check_vma=False,
    )
```

```python
import jax
import jax.numpy as jnp
import numpy as np
from jax import lax
from jax.experimental import pallas as pl
from jax.experimental.pallas import tpu as pltpu
from jax.sharding import PartitionSpec as P

HEAD_DIM = 64
BUCKETS = 32
MAX_DIST = 128


EPS = 1e-06
NEG = -1000000000.0


def bucket_table(length):
    distance = np.maximum(np.arange(length)[:, None] - np.arange(length)[None, :], 0)
    exact = BUCKETS // 2
    scaled = exact + (
        np.log(np.maximum(distance, 1) / exact) / np.log(MAX_DIST / exact) * (BUCKETS - exact)
    ).astype(np.int32)
    return np.where(distance < exact, distance, np.minimum(scaled, BUCKETS - 1)).astype(np.int32)


F32 = jnp.float32
BF16 = jnp.bfloat16
CHUNK = 256
SPAN = 512
COPIES = 128


def dot(left, right, left_dim, right_dim):
    return lax.dot_general(
        left, right, (((left_dim,), (right_dim,)), ((), ())), preferred_element_type=F32
    )


def dot_nn(left, right):
    return dot(left, right, 1, 0)


def dot_nt(left, right):
    return dot(left, right, 1, 1)


def dot_tn(left, right):
    return dot(left, right, 0, 0)


def unit_rows(resid):
    inv = lax.rsqrt(jnp.mean(resid * resid, -1, keepdims=True) + EPS)
    return inv, resid * inv


def norm_back(resid, gain, grad):
    inv, unit = unit_rows(resid)
    weighted = grad * gain
    grad_resid = inv * (weighted - unit * jnp.mean(weighted * unit, -1, keepdims=True))
    return grad_resid, jnp.sum(grad * unit, 0, keepdims=True)


def bucket_ranges(length):
    of_distance = bucket_table(length)[:, 0]
    ranges = []
    for k in range(BUCKETS):
        inside = np.flatnonzero(of_distance == k)
        ranges.append((int(inside[0]), int(inside[-1]) + 1) if len(inside) else (0, 0))
    return ranges


def place_of(chunk, order):
    y, z1, z2 = chunk % 2, chunk // 2 % 2, chunk // 4
    return 4 * y + 2 * z1 + z2 if order == "y" else 4 * z1 + 2 * y + z2


def layer_kernel(
    tlen_ref, mlen_ref, pos_ref, gain_self_ref, gain_cross_ref, gain_ffn_ref,
    x0_hbm, wq_hbm, wk_hbm, wv_hbm, wo_hbm, mem_hbm, cot_hbm, xq_hbm, xk_hbm, xv_hbm, xo_hbm, wg_hbm, wu_hbm, wd_hbm,
    out_ref, gt_ref, gm_ref, gf_ref, gx_ref, gs_ref, small_ref,
    q1, k1, v1, e1, r1, u1, o1, bias,
    part_send, part_recv, dn_recv, acc,
    x0_ref, wq_ref, wk_ref, wv_ref, wo_ref, mem, cot, wg, wu, wd, cross_w,
    x1, x2, n2, q2, kv2, e2, r2, u2, o2,
    n3, units, rows_low, rows_recv, rows_send_x, rows_recv_x,
    c2, turned, c1, f_low, f_recv0, f_recv1, f_recv2,
    x_recv0, x_recv1, x_recv2, x_send3, x_recv3, x_mid,
    s_low, s_recv1, s_recv2, small, small_recv,
    local_sem, send_sem, recv_sem,
):
    me = lax.axis_index("mp")
    core, chip = lax.rem(me, 2), lax.div(me, 2)
    other_core, other_chip = 1 - core, 1 - chip
    by_core = 2 * chip + other_core
    by_x = 2 * other_chip + core
    across = 2 * other_chip + other_core
    at_dp = lax.axis_index("dp")
    bit_y, bit_z1, bit_z2 = lax.rem(at_dp, 2), lax.rem(lax.div(at_dp, 2), 2), lax.div(at_dp, 4)
    to_core, to_x, to_across = {"mp": by_core}, {"mp": by_x}, {"mp": across}
    to_y = {"dp": at_dp + 1 - 2 * bit_y}
    to_z1 = {"dp": at_dp + 2 - 4 * bit_z1}
    to_z2 = {"dp": at_dp + 4 - 8 * bit_z2}

    seqs, length, width = x0_ref.shape
    part = wq_ref.shape[0]
    heads = part // HEAD_DIM
    slots = mem.shape[0]
    blocks = cross_w.shape[0]
    share = width // 8
    quarter = length // blocks

    gain_self_row, gain_cross_row, gain_ffn_row = (
        ref[...].reshape(1, width) for ref in (gain_self_ref, gain_cross_ref, gain_ffn_ref)
    )
    sent = {}
    names = iter(range(COPIES))

    def fresh(count):
        return [next(names) for _ in range(count)]

    def remote(i, src, dst, device):
        return pltpu.make_async_remote_copy(
            src_ref=src, dst_ref=dst, send_sem=send_sem.at[i], recv_sem=recv_sem.at[i],
            device_id=device, device_id_type=pl.DeviceIdType.MESH,
        )

    def note(i, src, dst, device, waited=False):
        sent[i] = remote(i, src, dst, device)

    def send(i, src, dst, device):
        remote(i, src, dst, device).start()
        note(i, src, dst, device)

    def left(*sends):
        for i in sends:
            sent.pop(i).wait_send()

    def arrived(i, dst, device):
        remote(i, dst, dst, device).wait_recv()

    def add_rows(ref, at, recv, from_at):
        ref[at, :] = (ref[at, :].astype(F32) + recv[from_at, :].astype(F32)).astype(BF16)

    class Sum:
        def __init__(self, low, recvs, order):
            self.low, self.recvs = low, recvs
            bits = (bit_y, bit_z1, bit_z2) if order == "y" else (bit_z1, bit_y, bit_z2)
            self.devices = (to_y, to_z1, to_z2) if order == "y" else (to_z1, to_y, to_z2)
            self.ids = fresh(3)
            self.away, self.kept, self.away_in, self.kept_in = [], [], [], []
            base = 0
            for k, bit in enumerate(bits):
                count = (4 >> k) * share

                def rows(start):
                    return pl.ds(pl.multiple_of(start, share), count)

                self.away.append(rows(base + (1 - bit) * count))
                self.kept.append(rows(base + bit * count))
                self.away_in.append(rows((1 - bit) * count))
                self.kept_in.append(rows(bit * count))
                base = base + bit * count

        def copy(self, k):
            return (self.ids[k], self.low.at[self.away[k]], self.recvs[k], self.devices[k])

        def start(self):
            send(*self.copy(0))

        def start_with(self, landed):
            add_rows(self.low, self.away[0], landed, self.away[0])
            send(*self.copy(0))
            add_rows(self.low, self.kept[0], landed, self.kept[0])

        def step(self, k, in_loop=False):
            recv = self.recvs[k - 1]
            arrived(self.ids[k - 1], recv, self.devices[k - 1])
            add_rows(self.low, self.away[k], recv, self.away_in[k])
            if in_loop:
                remote(*self.copy(k)).start()
            else:
                send(*self.copy(k))
            add_rows(self.low, self.kept[k], recv, self.kept_in[k])

        def total(self):
            arrived(self.ids[2], self.recvs[2], self.devices[2])
            return self.low[self.kept[2], :].astype(F32) + self.recvs[2][...].astype(F32)

    def neighbour(t):
        flip_x, flip_core = lax.div(t, 2), lax.rem(t, 2)
        at_x = chip + flip_x * (other_chip - chip)
        return 2 * at_x + core + flip_core * (other_core - core)

    barrier = pltpu.get_barrier_semaphore()
    partners = (to_core, to_x, to_across, to_y, to_z1, to_z2)
    for device in partners:
        pl.semaphore_signal(barrier, inc=1, device_id=device, device_id_type=pl.DeviceIdType.MESH)

    loads = [
        pltpu.make_async_copy(source, target, local_sem.at[i])
        for i, (source, target) in enumerate((
            (xk_hbm, cross_w.at[me, 0:part]),
            (xv_hbm, cross_w.at[me, part : 2 * part]),
            (xq_hbm, cross_w.at[me, 2 * part : 3 * part]),
            (xo_hbm, cross_w.at[me, 3 * part : 4 * part]),
            (x0_hbm, x0_ref),
            (wq_hbm, wq_ref),
            (wk_hbm, wk_ref),
            (wv_hbm, wv_ref),
            (wo_hbm, wo_ref),
            (mem_hbm.at[me], mem),
            (cot_hbm, cot),
            (wg_hbm, wg),
            (wu_hbm, wu),
            (wd_hbm, wd),
        ))
    ]
    for load in loads[:9]:
        load.start()
    for load in loads[:4]:
        load.wait()
    pl.semaphore_wait(barrier, len(partners))

    def piece(flip_y, flip_z1, p):
        at_y = bit_y + flip_y * (1 - 2 * bit_y)
        at_z1 = bit_z1 + flip_z1 * (1 - 2 * bit_z1)
        start = 2 * part * p + share * (at_y + 2 * at_z1)
        return pl.ds(pl.multiple_of(start, share), share)

    lows, highs = slice(0, 2 * part), slice(2 * part, 4 * part)
    w_core, w_x, w_y, w_z1, w_on = fresh(2), fresh(2), fresh(3), fresh(3), fresh(8)

    def weights_on(i, rows, device, in_loop=False):
        copy = (i, cross_w.at[by_x, rows], cross_w.at[by_x, rows], device)
        if in_loop:
            remote(*copy).start()
        else:
            send(*copy)
        return copy

    def weights_from(i, rows, device):
        arrived(i, cross_w.at[by_x, rows], device)

    def weights_from_x(p, in_loop=False):
        rows = piece(0, 0, p)
        weights_from(w_x[p], rows, to_x)
        return [
            weights_on(w_y[p], rows, to_y, in_loop),
            weights_on(w_z1[p], rows, to_z1, in_loop),
            weights_on(w_on[p], rows, to_core, in_loop),
        ]

    def weights_near(p):
        from_y, from_z1 = piece(1, 0, p), piece(0, 1, p)
        weights_from(w_y[p], from_y, to_y)
        if p == 0:
            weights_on(w_z1[2], from_y, to_z1)
        weights_on(w_on[2 + p], from_y, to_core)
        weights_from(w_z1[p], from_z1, to_z1)
        if p == 1:
            weights_on(w_y[2], from_z1, to_y)
        weights_on(w_on[4 + p], from_z1, to_core)

    def weights_far(p):
        i, device = ((w_z1[2], to_z1), (w_y[2], to_y))[p]
        weights_from(i, piece(1, 1, p), device)
        weights_on(w_on[6 + p], piece(1, 1, p), to_core)

    def weights_from_core(p):
        for i, (flip_y, flip_z1) in enumerate(((0, 0), (1, 0), (0, 1), (1, 1))):
            rows = piece(flip_y, flip_z1, p)
            arrived(w_on[2 * i + p], cross_w.at[across, rows], to_core)

    for p in range(2):
        rows = piece(0, 0, p)
        send(w_x[p], cross_w.at[me, rows], cross_w.at[me, rows], to_x)
    send(w_core[0], cross_w.at[me, lows], cross_w.at[me, lows], to_core)
    send(w_core[1], cross_w.at[me, highs], cross_w.at[me, highs], to_core)
    for load in loads[9:]:
        load.start()

    key_at = lax.broadcasted_iota(jnp.int32, (length, length), 0)
    query_at = lax.broadcasted_iota(jnp.int32, (length, length), 1)
    distance = lax.broadcasted_iota(jnp.int32, (8, length), 1)
    for h in range(heads):
        of_distance = jnp.zeros((8, length), F32)
        for k, (first, last) in enumerate(bucket_ranges(length)):
            inside = (distance >= first) & (distance < last)
            of_distance = jnp.where(inside, pos_ref[h, k], of_distance)
        spread = jnp.broadcast_to(of_distance[0:1], (length, length))
        shifted = pltpu.roll(spread, 0, 1, stride=1, stride_axis=0)
        bias[h] = jnp.where(key_at <= query_at, shifted, NEG)

    for load in loads[4:9]:
        load.wait()

    x1_core0, x1_x, x1_core1 = fresh(3)

    def self_one(t, carry):
        s = neighbour(3 - t)

        @pl.when(t == 3)
        def _():
            weights_from_x(0, True)

        resid = x0_ref[s].astype(F32)
        _, unit = unit_rows(resid)
        n = (unit * gain_self_row).astype(BF16)
        q = dot_nt(n, wq_ref[...]).astype(BF16)
        k = dot_nt(n, wk_ref[...]).astype(BF16)
        v = dot_nt(n, wv_ref[...]).astype(BF16)
        q1[s], k1[s], v1[s] = q, k, v
        mixed = []
        for h in range(heads):
            cols = slice(h * HEAD_DIM, (h + 1) * HEAD_DIM)
            scores = dot_nt(k[:, cols], q[:, cols]) + bias[h]
            scores = jnp.where(key_at < tlen_ref[s], scores, NEG)
            e = jnp.exp(scores - jnp.max(scores, 0, keepdims=True))
            r = 1.0 / jnp.sum(e, 0, keepdims=True)
            e = e.astype(BF16)
            e1[s, h] = e
            r1[s, h] = r
            u = dot_tn(v[:, cols], e)
            u1[s, h] = u
            mixed.append(u * r)
        o = jnp.concatenate(mixed, 0).T.astype(BF16)
        o1[s] = o
        value = dot_nn(o, wo_ref[...])

        @pl.when(t == 0)
        def _():
            part_send[0] = value.astype(BF16)
            remote(x1_core0, part_send.at[0], part_recv.at[0], to_core).start()

        @pl.when(t == 1)
        def _():
            arrived(x1_core0, part_recv.at[0], to_core)
            part_send[1] = (value + part_recv[0].astype(F32)).astype(BF16)
            remote(x1_x, part_send.at[1], part_recv.at[1], to_x).start()

        @pl.when(t == 2)
        def _():
            part_send[2] = value.astype(BF16)
            remote(x1_core1, part_send.at[2], part_recv.at[2], to_core).start()

        @pl.when(t == 3)
        def _():
            x1[...] = resid + value

        return carry

    lax.fori_loop(0, seqs, self_one, 0)
    note(x1_core0, part_send.at[0], part_recv.at[0], to_core, waited=True)
    note(x1_x, part_send.at[1], part_recv.at[1], to_x)
    note(x1_core1, part_send.at[2], part_recv.at[2], to_core)

    first = piece(0, 0, 0)
    for i, device in ((w_y[0], to_y), (w_z1[0], to_z1), (w_on[0], to_core)):
        note(i, cross_w.at[by_x, first], cross_w.at[by_x, first], device)

    def keys_values(b):
        for at in range(0, slots, CHUNK):
            rows = slice(at, at + CHUNK)
            kv2[b, rows, :] = dot_nt(mem[rows, :], cross_w[b, lows, :]).astype(BF16)

    loads[9].wait()
    arrived(w_core[0], cross_w.at[by_core, lows], to_core)

    def near_keys(t, carry):
        keys_values(neighbour(t))
        return carry

    lax.fori_loop(0, 2, near_keys, 0)
    weights_from_x(1)
    weights_near(0)
    arrived(w_core[1], cross_w.at[by_core, highs], to_core)
    weights_near(1)
    arrived(x1_core1, part_recv.at[2], to_core)
    arrived(x1_x, part_recv.at[1], to_x)

    def enter_cross(i, carry):
        rows = pl.ds(pl.multiple_of(i * quarter, quarter), quarter)
        resid = x1[rows, :] + part_recv[1, rows, :].astype(F32) + part_recv[2, rows, :].astype(F32)
        x1[rows, :] = resid
        x2[rows, :] = resid
        n2[rows, :] = (unit_rows(resid)[1] * gain_cross_row).astype(BF16)
        return carry

    lax.fori_loop(0, blocks, enter_cross, 0)
    weights_far(0)
    weights_far(1)
    slot_at = lax.broadcasted_iota(jnp.int32, (CHUNK, length), 0)
    spans = range(0, slots, SPAN)

    def cross_one(t, carry):
        b = neighbour(t)

        @pl.when(t == 2)
        def _():
            keys_values(by_x)

        @pl.when(t == 3)
        def _():
            weights_from_core(0)
            weights_from_core(1)
            keys_values(across)

        q = dot_nt(n2[...], cross_w[b, 2 * part : 3 * part, :]).astype(BF16)
        q2[b] = q
        mixed = []
        for h in range(heads):
            cols = slice(h * HEAD_DIM, (h + 1) * HEAD_DIM)
            cols_v = slice(part + h * HEAD_DIM, part + (h + 1) * HEAD_DIM)

            def scores_at(at):
                scores = dot_nt(kv2[b, at : at + CHUNK, cols], q[:, cols])
                return jnp.where(slot_at < mlen_ref[me] - at, scores, NEG)

            top = jnp.full((1, length), NEG, F32)
            for at in range(0, slots, CHUNK):
                top = jnp.maximum(top, jnp.max(scores_at(at), 0, keepdims=True))
            total = jnp.zeros((1, length), F32)
            u = jnp.zeros((HEAD_DIM, length), F32)
            for at in range(0, slots, CHUNK):
                rows = slice(at, at + CHUNK)
                e = jnp.exp(scores_at(at) - top)
                total = total + jnp.sum(e, 0, keepdims=True)
                e = e.astype(BF16)
                e2[b * heads + h, rows, :] = e
                u = u + dot_tn(kv2[b, rows, cols_v], e)
            r = 1.0 / total
            r2[b * heads + h] = r
            u2[b * heads + h] = u
            mixed.append(u * r)
        o = jnp.concatenate(mixed, 0).T.astype(BF16)
        o2[b] = o
        x2[...] += dot_nn(o, cross_w[b, 3 * part : 4 * part, :])
        return carry

    lax.fori_loop(0, blocks, cross_one, 0)

    n3_x, n3_core, n3_on = fresh(blocks), next(names), fresh(blocks)
    dn_near, dn_core, dn_x = next(names), fresh(blocks), fresh(blocks)

    def quarter_at(i):
        return pl.ds(pl.multiple_of(i * quarter, quarter), quarter)

    def n3_to_x(i):
        return (n3_x[0] + i, n3.at[me, quarter_at(i)], n3.at[me, quarter_at(i)], to_x)

    def n3_to_core(i):
        return (n3_on[0] + i, n3.at[by_x, quarter_at(i)], n3.at[by_x, quarter_at(i)], to_core)

    def dn_to_core(i):
        rows = quarter_at(i)
        return (dn_core[0] + i, part_send.at[1, rows], dn_recv.at[1, rows], to_core)

    def dn_to_x(i):
        return (dn_x[0] + i, part_send.at[2, quarter_at(i)], dn_recv.at[2, quarter_at(i)], to_x)

    def enter_ffn(i, carry):
        rows = quarter_at(i)
        n3[me, rows, :] = (unit_rows(x2[rows, :])[1] * gain_ffn_row).astype(BF16)
        remote(*n3_to_x(i)).start()
        return carry

    lax.fori_loop(0, blocks, enter_ffn, 0)
    for i in range(blocks):
        note(*n3_to_x(i), waited=True)
    send(n3_core, n3.at[me], n3.at[me], to_core)
    for load in loads[10:]:
        load.wait()
    left(x1_core0, x1_x, x1_core1)
    scale, cubic = 0.7978845608028654, 0.044715

    def turn(slot, value, first_col, order=None):
        value = value.T
        cols = pl.ds(first_col, value.shape[1])
        if order is None:
            turned[slot, :, cols] = value
            return
        for j in range(8):
            at = place_of(j, order) * share
            turned[slot, at : at + share, cols] = value[j * share : (j + 1) * share]

    def turn_normed(s):
        turn(0, n3[s], pl.multiple_of(s * length, length), "y")

    def ffn_rows(n, c, at_rows):
        count = n.shape[0] // len(at_rows)
        for at in range(0, wg.shape[1], CHUNK):
            cols = slice(at, at + CHUNK)
            a = dot_nn(n, wg[:, cols])
            b = dot_nn(n, wu[:, cols])
            dh = dot_nt(c, wd[cols, :])
            square = a * a
            slope = jnp.tanh(scale * (a + cubic * (a * square)))
            mid = 0.5 * (1.0 + slope)
            gelu = a * mid
            rise = mid + 0.5 * a * (1.0 - slope * slope) * (scale * (1.0 + 3.0 * cubic * square))
            for i, value in enumerate((dh * b * rise, dh * gelu, gelu * b)):
                value = value.astype(BF16)
                for j, rows in enumerate(at_rows):
                    units[i, rows, cols] = value[j * count : (j + 1) * count]

        def whole(i):
            return jnp.concatenate([units[i, rows, :] for rows in at_rows], 0)

        dn = dot_nt(whole(0), wg[...]) + dot_nt(whole(1), wu[...])
        return dn, lambda: dot_nn(whole(2), wd[...])

    def ffn_near(t, carry):
        s = neighbour(t)

        @pl.when(t == 1)
        def _():
            arrived(n3_core, n3.at[by_core], to_core)

        rows = pl.ds(pl.multiple_of(s * length, length), length)
        dn, result = ffn_rows(n3[s], cot[s], [rows])

        @pl.when(t == 0)
        def _():
            acc[...] = dn

        @pl.when(t == 1)
        def _():
            part_send[0] = dn.astype(BF16)
            remote(dn_near, part_send.at[0], dn_recv.at[0], to_core).start()

        own = jnp.where(t == 0, 1.0, 0.0)
        low = (result() + own * x2[...]).astype(BF16)
        for i in range(blocks):
            rows_low[i % 2, i // 2, s] = low[i * quarter : (i + 1) * quarter]
        return carry

    lax.fori_loop(0, 2, ffn_near, 0)
    note(dn_near, part_send.at[0], dn_recv.at[0], to_core)
    turn_normed(me)
    turn_normed(by_core)

    def pass_dn(i):
        rows = quarter_at(i)
        arrived(dn_core[0] + i, dn_recv.at[1, rows], to_core)
        part_send[2, rows, :] = (
            part_send[2, rows, :].astype(F32) + dn_recv[1, rows, :].astype(F32)
        ).astype(BF16)
        remote(*dn_to_x(i)).start()

    def ffn_far(t, carry):
        rows = quarter_at(t)

        @pl.when(t > 0)
        def _():
            pass_dn(t - 1)

        arrived(n3_x[0] + t, n3.at[by_x, rows], to_x)
        remote(*n3_to_core(t)).start()
        turn(1, cot[t], pl.multiple_of(t * length, length), "z1")
        arrived(n3_on[0] + t, n3.at[across, rows], to_core)
        n = jnp.concatenate([n3[by_x, rows, :], n3[across, rows, :]], 0)
        c = jnp.concatenate([cot[by_x, rows, :], cot[across, rows, :]], 0)
        dn, result = ffn_rows(
            n, c, [
                pl.ds(pl.multiple_of(s * length + t * quarter, quarter), quarter)
                for s in (by_x, across)
            ],
        )
        part_send[1, rows, :] = dn[quarter:].astype(BF16)
        remote(*dn_to_core(t)).start()
        part_send[2, rows, :] = dn[:quarter].astype(BF16)
        low = result().astype(BF16)
        rows_low[lax.rem(t, 2), lax.div(t, 2), by_x] = low[:quarter]
        rows_low[lax.rem(t, 2), lax.div(t, 2), across] = low[quarter:]
        return carry

    lax.fori_loop(0, blocks, ffn_far, 0)
    pass_dn(blocks - 1)
    for i in range(blocks):
        note(*n3_to_core(i), waited=True)
        note(*dn_to_core(i), waited=True)
        note(*dn_to_x(i))
    out_core, out_x = fresh(2)
    send(out_core, rows_low.at[other_core], rows_recv, to_core)
    turn_normed(by_x)
    turn_normed(across)
    orders = ("y", "y", "z1")
    f_sums = [
        Sum(f_low.at[i], [f_recv0.at[i], f_recv1.at[i], f_recv2.at[i]], orders[i]) for i in range(3)
    ]

    def ffn_grad(i, rows):
        f_low[i, rows, :] = dot_nn(turned[i // 2, rows, :], units[i]).astype(BF16)

    for i in (0, 2, 1):
        ffn_grad(i, f_sums[i].away[0])
        f_sums[i].start()
    for i in (0, 2, 1):
        ffn_grad(i, f_sums[i].kept[0])

    arrived(out_core, rows_recv, to_core)
    rows_send_x[...] = (
        rows_low[core, other_chip].astype(F32) + rows_recv[other_chip].astype(F32)
    ).astype(BF16)
    send(out_x, rows_send_x, rows_recv_x, to_x)

    arrived(dn_near, dn_recv.at[0], to_core)
    for i in range(blocks):
        arrived(dn_x[i], dn_recv.at[2, quarter_at(i)], to_x)
    small[...] = jnp.zeros_like(small)

    def enter_back(i, carry):
        rows = pl.ds(pl.multiple_of(i * quarter, quarter), quarter)
        dn3 = acc[rows, :] + dn_recv[0, rows, :].astype(F32) + dn_recv[2, rows, :].astype(F32)
        grad, gain_ffn = norm_back(x2[rows, :], gain_ffn_row, dn3)
        dx2 = cot[me, rows, :].astype(F32) + grad
        acc[rows, :] = dx2
        c2[rows, :] = dx2.astype(BF16)
        small[0, 2:3, :] += gain_ffn
        return carry

    lax.fori_loop(0, blocks, enter_back, 0)

    def cross_back(b, carry):
        @pl.when(b == 2)
        def _():
            f_sums[0].step(1, True)

        @pl.when(b == 3)
        def _():
            f_sums[2].step(1, True)

        do = dot_nt(cross_w[b, 3 * part : 4 * part, :], c2[...])
        q = q2[b]
        dqs = []
        for h in range(heads):
            cols = slice(h * HEAD_DIM, (h + 1) * HEAD_DIM)
            cols_v = slice(part + h * HEAD_DIM, part + (h + 1) * HEAD_DIM)
            r = r2[b * heads + h]
            low = (do[cols] * r).astype(BF16)
            delta = r * jnp.sum(low.astype(F32) * u2[b * heads + h], 0, keepdims=True)
            dq = jnp.zeros((HEAD_DIM, length), F32)
            for at in spans:
                rows = slice(at, at + SPAN)
                e = e2[b * heads + h, rows, :]
                dp = dot_nn(kv2[b, rows, cols_v], low)
                ds = e * (dp - delta).astype(BF16)
                dq = dq + dot_tn(kv2[b, rows, cols], ds)
                kv2[b, rows, cols_v] = dot_nt(e, low).astype(BF16)
                kv2[b, rows, cols] = dot_nn(ds, q[:, cols]).astype(BF16)
            dqs.append(dq)
        q2[b] = jnp.concatenate(dqs, 0).T.astype(BF16)
        return carry

    lax.fori_loop(0, blocks, cross_back, 0)
    for i in (0, 2):
        note(*f_sums[i].copy(1))
    dn2 = dot_nn(q2[0], cross_w[0, 2 * part : 3 * part, :])
    for b in range(1, blocks):
        dn2 = dn2 + dot_nn(q2[b], cross_w[b, 2 * part : 3 * part, :])
    x2[...] = dn2

    def leave_cross(i, carry):
        rows = pl.ds(pl.multiple_of(i * quarter, quarter), quarter)
        grad, gain_cross = norm_back(x1[rows, :], gain_cross_row, x2[rows, :])
        c1[me, rows, :] = (acc[rows, :] + grad).astype(BF16)
        small[0, 1:2, :] += gain_cross
        return carry

    lax.fori_loop(0, blocks, leave_cross, 0)
    arrived(out_x, rows_recv_x, to_x)
    out_ref[...] = (
        rows_low[core, chip].astype(F32)
        + rows_recv[chip].astype(F32)
        + rows_recv_x[...].astype(F32)
    ).astype(BF16)
    left(out_core, out_x)
    c1_x, c1_core, c1_on = fresh(3)
    send(c1_x, c1.at[me], c1.at[me], to_x)
    send(c1_core, c1.at[me], c1.at[me], to_core)
    f_sums[1].step(1)
    turn(0, mem[...], 0)
    turn(1, n2[...], 0)
    turn(1, c2[...], length)

    def put(slabs, first_row, first_col, value):
        at = 0
        while at < value.shape[1]:
            slab, col = divmod(first_col + at, 256)
            count = min(256 - col, value.shape[1] - at)
            for i in range(value.shape[0] // share):
                row = place_of(first_row // share + i, orders[slab]) * share
                slabs[slab][row : row + share, col : col + count] = value[
                    i * share : (i + 1) * share, at : at + count
                ]
            at += count

    def cross_grads(b):
        slabs = [e2.at[3 * b + j] for j in range(3)]
        for at in range(0, width, width // 2):
            rows = slice(at, at + width // 2)
            put(slabs, at, 0, dot_nn(turned[0, rows, :], kv2[b]).astype(BF16))
            put(slabs, at, 2 * part, dot_nn(turned[1, rows, 0:length], q2[b]).astype(BF16))
            put(slabs, at, 3 * part, dot_nn(turned[1, rows, length : 2 * length], o2[b]).astype(BF16))

    def landing(i, j):
        return units.at[j, 0:width, 256 * i : 256 * (i + 1)]

    x_core = [fresh(3) for _ in range(2)]
    x_sums = [
        [
            Sum(
                e2.at[3 * (2 * i + core) + j],
                [x_recv0.at[i, j], x_recv1.at[i, j], x_recv2.at[i, j]],
                orders[j],
            )
            for j in range(3)
        ]
        for i in range(2)
    ]
    mid_sum = Sum(
        e2.at[3 * (2 * chip + core) + 1], [x_mid, x_recv1.at[0, 1], x_recv2.at[0, 1]], "y"
    )
    mid_x = fresh(2)
    mid_halves = [slice(0, 4 * share), slice(4 * share, 8 * share)]

    def cross_away(i):
        b = 2 * i + other_core
        cross_grads(b)
        if i == 0:
            arrived(c1_core, c1.at[by_core], to_core)
        for j in range(3):
            send(x_core[i][j], e2.at[3 * b + j, 0:width], landing(i, j), to_core)

    def cross_start(i):
        for j in (0, 2):
            arrived(x_core[i][j], landing(i, j), to_core)
            x_sums[i][j].start_with(landing(i, j))
        arrived(x_core[i][1], landing(i, 1), to_core)
        for rows in mid_halves:
            add_rows(e2.at[3 * (2 * i + core) + 1], rows, landing(i, 1), rows)

    cross_away(0)
    cross_grads(core)
    cross_away(1)
    cross_start(0)
    for i in (0, 2):
        f_sums[i].step(2)
    cross_grads(2 + core)
    cross_start(1)
    for i in range(2):
        send(
            mid_x[i], e2.at[3 * (2 * other_chip + core) + 1, mid_halves[i]], x_recv0.at[i, 1], to_x
        )

    left(*n3_x, n3_core, *n3_on)
    gm_x, gm_across, gm_core = fresh(3)

    def memory_grad(target):
        rows = pl.ds(pl.multiple_of(target * CHUNK, CHUNK), CHUNK)
        for at in range(0, width, CHUNK):
            cols = slice(at, at + CHUNK)
            total = dot_nn(kv2[0, rows, :], cross_w[0, lows, cols])
            for b in range(1, blocks):
                total = total + dot_nn(kv2[b, rows, :], cross_w[b, lows, cols])
            n3[target, :, cols] = total.astype(BF16)

    memory_grad(by_x)
    send(gm_x, n3.at[by_x], gm_ref.at[me], to_x)
    memory_grad(across)
    send(gm_across, n3.at[across], gm_ref.at[me], to_across)

    bias[...] = jnp.zeros_like(bias)

    def self_back(t, carry):
        s = neighbour(t)

        @pl.when(t == 2)
        def _():
            arrived(c1_x, c1.at[by_x], to_x)
            remote(c1_on, c1.at[by_x], c1.at[by_x], to_core).start()
            f_sums[1].step(2, True)
            x_sums[0][0].step(1, True)
            x_sums[0][2].step(1, True)

        @pl.when(t == 3)
        def _():
            arrived(c1_on, c1.at[across], to_core)
            x_sums[1][0].step(1, True)
            x_sums[1][2].step(1, True)

        do = dot_nt(wo_ref[...], c1[s])
        dqs = []
        for h in range(heads):
            cols = slice(h * HEAD_DIM, (h + 1) * HEAD_DIM)
            r = r1[s, h]
            low = (do[cols] * r).astype(BF16)
            delta = r * jnp.sum(low.astype(F32) * u1[s, h], 0, keepdims=True)
            e = e1[s, h]
            dp = dot_nn(v1[s, :, cols], low)
            ds = e * (dp - delta).astype(BF16)
            bias[h] += ds.astype(F32)
            dqs.append(dot_tn(k1[s, :, cols], ds))
            v1[s, :, cols] = dot_nt(e, low).astype(BF16)
            k1[s, :, cols] = dot_nn(ds, q1[s, :, cols]).astype(BF16)
        q1[s] = jnp.concatenate(dqs, 0).T.astype(BF16)
        dn = dot_nn(q1[s], wq_ref[...]) + dot_nn(k1[s], wk_ref[...]) + dot_nn(v1[s], wv_ref[...])
        acc[...] = dn
        for i in range(blocks):
            rows = slice(i * quarter, (i + 1) * quarter)
            unit = unit_rows(x0_ref[s, rows, :].astype(F32))[1]
            small[0, 0:1, :] += jnp.sum(acc[rows, :] * unit, 0, keepdims=True)
            rows_low[i % 2, i // 2, s] = acc[rows, :].astype(BF16)
        return carry

    lax.fori_loop(0, seqs, self_back, 0)
    note(c1_on, c1.at[by_x], c1.at[by_x], to_core, waited=True)
    note(*f_sums[1].copy(2))
    for i in range(2):
        note(*x_sums[i][2].copy(1))
        note(*x_sums[i][0].copy(1))
    dn1_core, dn1_x, small_y, small_z1, small_z2 = fresh(5)
    small_mp = fresh(3)
    send(dn1_core, rows_low.at[other_core], rows_recv, to_core)
    for i in range(2):
        arrived(mid_x[i], x_recv0.at[i, 1], to_x)
        add_rows(e2.at[3 * (2 * chip + core) + 1], mid_halves[i], x_recv0.at[i, 1], slice(None))
    mid_sum.start()
    for h in range(heads):
        total = bias[h]
        step = 1
        while step < length:
            total = jnp.where((key_at & step) != 0, pltpu.roll(total, length - step, 1), total)
            step *= 2
        small[0, 3 + h : 4 + h, 0:length] = jnp.sum(total, 0, keepdims=True)
    send(small_y, small.at[0], small_recv.at[0], to_y)

    for s in range(seqs):
        _, unit = unit_rows(x0_ref[s].astype(F32))
        turn(0, (unit * gain_self_row).astype(BF16), s * length)
        turn(1, c1[s], s * length)
    slabs = [s_low.at[j] for j in range(3)]
    s_sums = [
        Sum(s_low.at[j], [f_recv0.at[j, :, 0:256], s_recv1.at[j], s_recv2.at[j]], orders[j]) for j in range(3)
    ]
    for i, ref in enumerate((k1, v1, q1, o1)):
        right = ref[...].reshape(seqs * length, part)
        for at in range(0, width, width // 2):
            value = dot_nn(turned[i // 3, at : at + width // 2, :], right).astype(BF16)
            put(slabs, at, i * part, value)
        if i:
            s_sums[i - 1].start()
        if i == 2:
            x_sums[0][0].step(2)
            x_sums[1][0].step(2)

    arrived(dn1_core, rows_recv, to_core)
    rows_send_x[...] = (
        rows_low[core, other_chip].astype(F32) + rows_recv[other_chip].astype(F32)
    ).astype(BF16)
    send(dn1_x, rows_send_x, rows_recv_x, to_x)

    def pass_small(i, came, device, goes, onward):
        arrived(came, small_recv.at[i], device)
        small[i + 1] = small[i] + small_recv[i]
        if goes is not None:
            send(goes, small.at[i + 1], small_recv.at[i + 1], onward)

    mid_sum.step(1)
    memory_grad(by_core)
    send(gm_core, n3.at[by_core], gm_ref.at[me], to_core)
    memory_grad(me)
    own_rows = pltpu.make_async_copy(n3.at[me], gm_ref.at[me], local_sem.at[15])
    own_rows.start()
    pass_small(0, small_y, to_y, small_z1, to_z1)

    s_sums[2].step(1)
    for i in range(2):
        x_sums[i][2].step(2)
    mid_sum.step(2)
    s_sums[0].step(1)
    pass_small(1, small_z1, to_z1, small_z2, to_z2)
    s_sums[1].step(1)
    s_sums[2].step(2)
    s_sums[0].step(2)
    for i in range(3):
        gf_ref[i] = f_sums[i].total()

    s_sums[1].step(2)

    last_x = next(names)
    for i in range(2):
        for j in (0, 2):
            arrived(x_sums[i][j].ids[2], x_recv2.at[i, j], to_z2)

    def cross_total(at, j):
        rows = x_sums[0][j].kept[2]
        return e2[3 * (2 * at + core) + j, rows, :].astype(F32) + x_recv2[at, j].astype(F32)

    for i, j in enumerate((0, 2)):
        x_send3[i] = cross_total(other_chip, j).astype(BF16)
    send(last_x, x_send3, x_recv3, to_x)
    pass_small(2, small_z2, to_z2, None, None)
    mp_peers = (to_core, to_x, to_across)
    for i, device in enumerate(mp_peers):
        send(small_mp[i], small.at[3], small_recv.at[3 + i], device)
    arrived(dn1_x, rows_recv_x, to_x)
    my_rows = pl.ds(pl.multiple_of(me * quarter, quarter), quarter)
    for s in range(seqs):
        dn = (
            rows_low[core, chip, s].astype(F32)
            + rows_recv[chip, s].astype(F32)
            + rows_recv_x[s].astype(F32)
        )
        grad, _ = norm_back(x0_ref[s, my_rows, :].astype(F32), gain_self_row, dn)
        gt_ref[s] = (c1[s, my_rows, :].astype(F32) + grad).astype(BF16)
    for j in range(3):
        gs_ref[j] = s_sums[j].total()
    arrived(last_x, x_recv3, to_x)
    for i, j in enumerate((0, 2)):
        gx_ref[j] = cross_total(chip, j) + x_recv3[i].astype(F32)
    gx_ref[1] = mid_sum.total()
    for i, device in enumerate(mp_peers):
        arrived(small_mp[i], small_recv.at[3 + i], device)
    small_ref[0] = small[3] + small_recv[3] + small_recv[4] + small_recv[5]
    small_ref[1] = small[3]
    arrived(gm_x, gm_ref.at[by_x], to_x)
    arrived(gm_across, gm_ref.at[across], to_across)
    arrived(gm_core, gm_ref.at[by_core], to_core)
    own_rows.wait()
    for copy in sent.values():
        copy.wait_send()


def finish_kernel(
    gf_ref, gx_ref, gs_ref, small_ref, onehot_ref, out_ref, gt_ref, gm_ref,
    out_o, gt_o, gm_o, sq_o, sk_o, sv_o, so_o, cq_o, ck_o, cv_o, co_o, gg_o, gu_o, gd_o,
    gain_self_o, gain_cross_o, gain_ffn_o, bias_o,
):
    part, share = sq_o.shape[1], sq_o.shape[0]
    width = small_ref.shape[2]
    out_o[...], gt_o[...], gm_o[...] = out_ref[...], gt_ref[...], gm_ref[...]
    gg_o[...], gu_o[...], gd_o[...] = gf_ref[0], gf_ref[1], gf_ref[2]
    for source, refs in ((gx_ref, (ck_o, cv_o, cq_o, co_o)), (gs_ref, (sk_o, sv_o, sq_o, so_o))):
        value = jnp.concatenate([source[0], source[1], source[2]], 1)
        for i in range(3):
            refs[i][...] = value[:, i * part : (i + 1) * part]
        refs[3][...] = value[:, 3 * part :].T
    shift = width - lax.axis_index("dp") * share
    gains = pltpu.roll(small_ref[0], shift, 1)
    for i, ref in enumerate((gain_self_o, gain_cross_o, gain_ffn_o)):
        ref[...] = gains[i : i + 1, 0:share]
    bias_o[...] = lax.dot_general(
        small_ref[1, 3 : 3 + bias_o.shape[0], 0 : onehot_ref.shape[0]], onehot_ref[...], (((1,), (0,)), ((), ())),
        precision=lax.Precision.HIGHEST, preferred_element_type=F32,
    )


VMEM = pl.BlockSpec(memory_space=pltpu.VMEM)
SMEM = pl.BlockSpec(memory_space=pltpu.SMEM)
ANY = pl.BlockSpec(memory_space=pl.ANY)


def on_device(
    targets,
    memory,
    cotangent,
    target_len,
    memory_len,
    query_self,
    key_self,
    value_self,
    out_self,
    query_cross,
    key_cross,
    value_cross,
    out_cross,
    gate_proj,
    up_proj,
    down_proj,
    gain_self,
    gain_cross,
    gain_ffn,
    pos_bias,
):
    seqs, length, width = targets.shape
    slots = memory.shape[1]
    part = query_self.shape[1]
    units = gate_proj.shape[1]
    heads = part // HEAD_DIM
    blocks = lax.axis_size("mp")
    dp_size = lax.axis_size("dp")
    share = width // dp_size
    quarter = length // blocks
    head_all = heads * blocks

    onehot = jnp.asarray(
        (bucket_table(length)[:, 0][:, None] == np.arange(BUCKETS)[None, :]).astype(np.float32)
    )
    def low(*shape):
        return pltpu.VMEM(shape, BF16)

    def full(*shape):
        return pltpu.VMEM(shape, F32)

    def sums(count, columns):
        return [low(count, 4 * share, columns), low(count, 2 * share, columns), low(count, share, columns)]

    scratch = [
        low(seqs, length, part), low(seqs, length, part), low(seqs, length, part),
        low(seqs, heads, length, length), full(seqs, heads, 1, length),
        full(seqs, heads, HEAD_DIM, length), low(seqs, length, part), full(heads, length, length),
        low(3, length, width), low(3, length, width), low(3, length, width),
        full(length, width),
        low(seqs, length, width), low(part, width), low(part, width), low(part, width),
        low(part, width), low(slots, width), low(seqs, length, width),
        low(width, units), low(width, units), low(units, width), low(blocks, 4 * part, width),
        full(length, width), full(length, width), low(length, width), low(blocks, length, part),
        low(blocks, slots, 2 * part), low(head_all, slots, length), full(head_all, 1, length),
        full(head_all, HEAD_DIM, length), low(blocks, length, part),
        low(seqs, length, width), low(3, seqs * length, units),
        low(2, 2, seqs, quarter, width), low(2, seqs, quarter, width),
        low(seqs, quarter, width), low(seqs, quarter, width),
        low(length, width), low(2, width, seqs * length), low(seqs, length, width),
        low(3, width, units), *sums(3, units),
        low(2, 3, 4 * share, 256), low(2, 3, 2 * share, 256), low(2, 3, share, 256),
        low(2, share, 256), low(2, share, 256), low(4 * share, 256),
        low(3, width, 256), *sums(3, 256)[1:],
        full(4, 8, width), full(6, 8, width),
        pltpu.SemaphoreType.DMA((16,)),
        pltpu.SemaphoreType.DMA((COPIES,)),
        pltpu.SemaphoreType.DMA((COPIES,)),
    ]
    struct = jax.ShapeDtypeStruct
    rows = struct((seqs, quarter, width), BF16)
    out, gt, gm, gf, gx, gs, small = pl.pallas_call(
        layer_kernel,
        out_shape=[
            rows,
            rows,
            struct((seqs, slots // blocks, width), BF16),
            struct((3, share, units), F32),
            struct((3, share, 256), F32),
            struct((3, share, 256), F32),
            struct((2, 8, width), F32),
        ],
        in_specs=[SMEM] * 3 + [VMEM] * 3 + [ANY] * 14,
        out_specs=[VMEM, VMEM, ANY, VMEM, VMEM, VMEM, VMEM],
        scratch_shapes=scratch,
        compiler_params=pltpu.CompilerParams(
            collective_id=0, has_side_effects=True, vmem_limit_bytes=63 * 2**20
        ),
        cost_estimate=pl.CostEstimate(flops=24 * 10**9, bytes_accessed=2**24, transcendentals=0),
        name="layer",
    )(
        target_len, memory_len, pos_bias.T,
        gain_self, gain_cross, gain_ffn, targets,
        query_self.T, key_self.T, value_self.T, out_self, memory, cotangent, query_cross.T, key_cross.T, value_cross.T, out_cross,
        gate_proj, up_proj, down_proj,
    )
    square = struct((share, part), F32)
    turned = struct((part, share), F32)
    (
        out, gt, gm, sq, sk, sv, so, cq, ck, cv, co, gg, gu, gd,
        grad_self, grad_cross, grad_ffn, bias,
    ) = pl.pallas_call(
        finish_kernel,
        out_shape=[
            rows, rows, struct((seqs, slots // blocks, width), BF16),
            square, square, square, turned, square, square, square, turned,
            struct((share, units), F32), struct((share, units), F32), struct((share, units), F32),
            struct((1, share), F32), struct((1, share), F32), struct((1, share), F32),
            struct((heads, BUCKETS), F32),
        ],
        in_specs=[VMEM] * 8,
        out_specs=[VMEM] * 18,
        compiler_params=pltpu.CompilerParams(vmem_limit_bytes=62 * 2**20),
        name="finish",
    )(gf, gx, gs, small, onehot, out, gt, gm)
    return (
        out, gt, gm, sq, sk, sv, so, cq, ck, cv, co, gg, gu, gd.T,
        grad_self[0], grad_cross[0], grad_ffn[0], bias.T,
    )


def project(inputs, weight):
    return jnp.einsum("bld,df->blf", inputs, weight, preferred_element_type=jnp.float32)


def back_project(gradient, weight):
    return jnp.einsum("blf,df->bld", gradient, weight, preferred_element_type=jnp.float32)


def weight_grad(inputs, gradient):
    return jnp.einsum("bld,blf->df", inputs, gradient, preferred_element_type=jnp.float32)


def norm_forward(resid, gain):
    inv_rms = lax.rsqrt(jnp.mean(resid * resid, -1, keepdims=True) + EPS)
    return (resid * inv_rms * gain, inv_rms)


def norm_backward(resid, inv_rms, gain, grad_normed):
    unit_rows = resid * inv_rms
    grad_gain = jnp.sum(grad_normed * unit_rows, axis=(0, 1))
    weighted = grad_normed * gain
    grad_resid = inv_rms * (
        weighted - unit_rows * jnp.mean(weighted * unit_rows, -1, keepdims=True)
    )
    return (grad_resid, grad_gain)


def scores_of(queries, keys, score_bias, valid):
    scores = (
        jnp.einsum("bihe,bjhe->bhij", queries, keys, preferred_element_type=jnp.float32)
        + score_bias
    )
    return jnp.where(valid, scores, NEG)


def attend(queries, keys, values, score_bias, valid):
    scores = scores_of(queries, keys, score_bias, valid)
    row_max = jnp.max(scores, -1, keepdims=True)
    log_total = row_max + jnp.log(jnp.sum(jnp.exp(scores - row_max), -1, keepdims=True))
    attn_probs = jnp.exp(scores - log_total).astype(jnp.bfloat16)
    mixed = jnp.einsum("bhij,bjhe->bihe", attn_probs, values, preferred_element_type=jnp.float32)
    return (mixed, log_total)


def attend_back(queries, keys, values, score_bias, valid, log_total, grad_mixed):
    attn_probs = jnp.exp(scores_of(queries, keys, score_bias, valid) - log_total)
    grad_values = jnp.einsum(
        "bhij,bihe->bjhe",
        attn_probs.astype(jnp.bfloat16),
        grad_mixed,
        preferred_element_type=jnp.float32,
    )
    grad_probs = jnp.einsum(
        "bihe,bjhe->bhij", grad_mixed, values, preferred_element_type=jnp.float32
    )
    grad_scores = attn_probs * (grad_probs - jnp.sum(attn_probs * grad_probs, -1, keepdims=True))
    grad_low = grad_scores.astype(jnp.bfloat16)
    grad_queries = jnp.einsum("bhij,bjhe->bihe", grad_low, keys, preferred_element_type=jnp.float32)
    grad_keys = jnp.einsum("bhij,bihe->bjhe", grad_low, queries, preferred_element_type=jnp.float32)
    return (grad_queries, grad_keys, grad_values, grad_low)


def swap(value, axis, bit):
    return lax.ppermute(value, axis, [(i, i ^ bit) for i in range(lax.axis_size(axis))])


def bits_of(axis):
    return [1 << i for i in range(lax.axis_size(axis).bit_length() - 1)]


def split_bits(value, axis, dim):
    steps = len(bits_of(axis))
    shape = value.shape
    return value.reshape(
        shape[:dim] + (2,) * steps + (shape[dim] >> steps,) + shape[dim + 1 :]
    )


def own_bit(axis, bit):
    return (lax.axis_index(axis) & bit) // bit


def halve(value, axis, bit, dim):
    mine = own_bit(axis, bit)
    kept = lax.dynamic_index_in_dim(value, mine, dim, keepdims=False)
    sent = lax.dynamic_index_in_dim(value, 1 - mine, dim, keepdims=False)
    arrived = swap(sent.astype(jnp.bfloat16), axis, bit)
    return kept + arrived.astype(jnp.float32)


def reduce_scatter(value, axis, dim):
    bits = bits_of(axis)
    value = split_bits(value, axis, dim)
    for at, bit in enumerate(bits):
        value = halve(value, axis, bit, dim + len(bits) - 1 - at)
    return value


def gather_mp(value):
    value = value[None]
    for bit in reversed(bits_of("mp")):
        other = swap(value, "mp", bit)
        first = own_bit("mp", bit) == 0
        low = jnp.where(first, value, other)
        high = jnp.where(first, other, value)
        value = jnp.stack([low, high], 1 if bit == 1 else 0)
        value = value.reshape((-1,) + value.shape[2:])
    return value


def exchange_mp(value):
    count = lax.axis_size("mp")
    value = split_bits(value, "mp", 0)[None]
    steps = len(bits_of("mp"))
    for at, bit in enumerate(bits_of("mp")):
        dim = steps - at
        mine = own_bit("mp", bit)
        kept = lax.dynamic_index_in_dim(value, mine, dim, keepdims=False)
        sent = lax.dynamic_index_in_dim(value, 1 - mine, dim, keepdims=False)
        arrived = swap(sent, "mp", bit)
        first = mine == 0
        low = jnp.where(first, kept, arrived)
        high = jnp.where(first, arrived, kept)
        value = jnp.stack([low, high], 0)
        value = value.reshape((-1,) + value.shape[2:])
    return value.reshape((count,) + value.shape[1:])


def sum_mp(value):
    for bit in bits_of("mp"):
        value = value + swap(value, "mp", bit)
    return value


def on_device_permutes(
    targets,
    memory,
    cotangent,
    target_len,
    memory_len,
    query_self,
    key_self,
    value_self,
    out_self,
    query_cross,
    key_cross,
    value_cross,
    out_cross,
    gate_proj,
    up_proj,
    down_proj,
    gain_self,
    gain_cross,
    gain_ffn,
    pos_bias,
):
    length = targets.shape[1]
    heads_local = query_self.shape[1] // HEAD_DIM
    mp_size = lax.axis_size("mp")
    dp_size = lax.axis_size("dp")
    mp_index = lax.axis_index("mp")
    row_share = length // mp_size
    width = targets.shape[2]

    def split_heads(value):
        return value.reshape(value.shape[0], value.shape[1], -1, HEAD_DIM)

    def merge_heads(value):
        return value.reshape(value.shape[0], value.shape[1], -1)

    def my_rows(value):
        return lax.dynamic_slice_in_dim(value, mp_index * row_share, row_share, 1)

    def mine(value):
        return lax.dynamic_index_in_dim(value, mp_index, 0)

    positions = jnp.arange(length)
    self_valid = (
        (positions[None, :] <= positions[:, None])[None]
        & (positions[None, None, :] < target_len[:, None, None])
    )[:, None]
    mem_positions = jnp.arange(memory.shape[1])
    cross_valid = (mem_positions[None, :] < mine(memory_len)[:, None])[:, None, None, :]
    onehot = (
        jnp.asarray(bucket_table(length)).reshape(-1)[:, None] == jnp.arange(BUCKETS)[None, :]
    ).astype(jnp.float32)
    score_bias = (
        jnp.dot(onehot, pos_bias, precision=lax.Precision.HIGHEST)
        .reshape(length, length, heads_local)
        .transpose(2, 0, 1)[None]
    )
    cross_in = gather_mp(jnp.stack([query_cross, key_cross, value_cross]))
    cross_in = cross_in.transpose(1, 2, 0, 3).reshape(3, width, -1)
    cross_q, cross_k, cross_v = cross_in[0], cross_in[1], cross_in[2]
    cross_o = gather_mp(out_cross).reshape(-1, width)

    resid0 = targets.astype(jnp.float32)
    normed_one, inv_one = norm_forward(resid0, gain_self)
    normed_one = normed_one.astype(jnp.bfloat16)
    queries = split_heads(project(normed_one, query_self).astype(jnp.bfloat16))
    keys = split_heads(project(normed_one, key_self).astype(jnp.bfloat16))
    values = split_heads(project(normed_one, value_self).astype(jnp.bfloat16))
    mixed, log_one = attend(queries, keys, values, score_bias, self_valid)
    mixed = merge_heads(mixed).astype(jnp.bfloat16)
    resid1 = mine(resid0) + reduce_scatter(project(mixed, out_self), "mp", 0)

    mem_own = mine(memory)
    normed_two, inv_two = norm_forward(resid1, gain_cross)
    normed_two = normed_two.astype(jnp.bfloat16)
    queries_two = split_heads(project(normed_two, cross_q).astype(jnp.bfloat16))
    mem_keys = split_heads(project(mem_own, cross_k).astype(jnp.bfloat16))
    mem_values = split_heads(project(mem_own, cross_v).astype(jnp.bfloat16))
    mixed_two, log_two = attend(queries_two, mem_keys, mem_values, 0.0, cross_valid)
    mixed_two = merge_heads(mixed_two).astype(jnp.bfloat16)
    resid2 = resid1 + project(mixed_two, cross_o)
    normed_three, inv_three = norm_forward(resid2, gain_ffn)
    normed_all = gather_mp(normed_three.astype(jnp.bfloat16)[0])

    gate_pre = project(normed_all, gate_proj)
    up_pre = project(normed_all, up_proj)

    def gated(gate_in, up_in):
        return jax.nn.gelu(gate_in, approximate=True) * up_in

    hidden, hidden_pull = jax.vjp(gated, gate_pre, up_pre)
    hidden = hidden.astype(jnp.bfloat16)
    grad_gate_pre, grad_up_pre = hidden_pull(back_project(cotangent, down_proj))
    grad_gate_pre = grad_gate_pre.astype(jnp.bfloat16)
    grad_up_pre = grad_up_pre.astype(jnp.bfloat16)
    grad_normed = reduce_scatter(
        back_project(grad_gate_pre, gate_proj) + back_project(grad_up_pre, up_proj), "mp", 0
    )
    result = project(hidden, down_proj)
    own = (jnp.arange(targets.shape[0]) == mp_index)[:, None, None]
    result = result + jnp.where(own, resid2, 0.0)
    output = reduce_scatter(result, "mp", 1).astype(jnp.bfloat16)
    ffn_grads = jnp.concatenate(
        [
            weight_grad(normed_all, grad_gate_pre),
            weight_grad(normed_all, grad_up_pre),
            weight_grad(cotangent, hidden),
        ],
        1,
    )
    ffn_grads = reduce_scatter(ffn_grads, "dp", 0)
    grad_resid, grad_gain_ffn = norm_backward(resid2, inv_three, gain_ffn, grad_normed)
    grad_two = mine(cotangent).astype(jnp.float32) + grad_resid

    branch_two = grad_two.astype(jnp.bfloat16)
    grad_mixed_two = split_heads(back_project(branch_two, cross_o).astype(jnp.bfloat16))
    grad_q_two, grad_mem_keys, grad_mem_values, _ = attend_back(
        queries_two, mem_keys, mem_values, 0.0, cross_valid, log_two, grad_mixed_two
    )
    grad_q_two = merge_heads(grad_q_two).astype(jnp.bfloat16)
    grad_normed = back_project(grad_q_two, cross_q)
    grad_resid, grad_gain_cross = norm_backward(resid1, inv_two, gain_cross, grad_normed)
    grad_one = grad_two + grad_resid
    branch_one = gather_mp(grad_one.astype(jnp.bfloat16)[0])
    grad_mem_keys = merge_heads(grad_mem_keys).astype(jnp.bfloat16)
    grad_mem_values = merge_heads(grad_mem_values).astype(jnp.bfloat16)
    mem_grad = back_project(grad_mem_keys, cross_k) + back_project(grad_mem_values, cross_v)
    mem_rows = exchange_mp(mem_grad[0].astype(jnp.bfloat16))
    cross_grads = jnp.stack(
        [
            weight_grad(normed_two, grad_q_two),
            weight_grad(mem_own, grad_mem_keys),
            weight_grad(mem_own, grad_mem_values),
            weight_grad(branch_two, mixed_two),
        ],
        1,
    )
    cross_grads = reduce_scatter(cross_grads, "mp", 2)
    cross_grads = reduce_scatter(cross_grads, "dp", 0)

    grad_mixed = split_heads(back_project(branch_one, out_self).astype(jnp.bfloat16))
    grad_q_one, grad_k_one, grad_v_one, grad_scores = attend_back(
        queries, keys, values, score_bias, self_valid, log_one, grad_mixed
    )
    grad_q_one = merge_heads(grad_q_one).astype(jnp.bfloat16)
    grad_k_one = merge_heads(grad_k_one).astype(jnp.bfloat16)
    grad_v_one = merge_heads(grad_v_one).astype(jnp.bfloat16)
    score_total = jnp.sum(grad_scores.astype(jnp.float32), 0).reshape(heads_local, length * length)
    bias_local = jnp.dot(score_total, onehot, precision=lax.Precision.HIGHEST).T
    grad_normed = (
        back_project(grad_q_one, query_self)
        + back_project(grad_k_one, key_self)
        + back_project(grad_v_one, value_self)
    )
    gains = jnp.stack(
        [
            jnp.sum(grad_normed * (resid0 * inv_one), axis=(0, 1)),
            grad_gain_cross,
            grad_gain_ffn,
        ]
    )
    gains = sum_mp(gains)
    share = width // dp_size
    bias_columns = jnp.tile(bias_local.reshape(share, -1), (dp_size, 1))
    self_grads = jnp.concatenate(
        [
            weight_grad(normed_one, grad_q_one),
            weight_grad(normed_one, grad_k_one),
            weight_grad(normed_one, grad_v_one),
            weight_grad(branch_one, mixed),
            gains.T,
            bias_columns,
        ],
        1,
    )
    self_grads = reduce_scatter(self_grads, "dp", 0)
    grad_normed = reduce_scatter(grad_normed, "mp", 1)
    grad_resid, _ = norm_backward(my_rows(resid0), my_rows(inv_one), gain_self, grad_normed)
    grad_targets = (my_rows(branch_one).astype(jnp.float32) + grad_resid).astype(jnp.bfloat16)

    part = query_self.shape[1]
    units = gate_proj.shape[1]
    gains_at = 4 * part
    return (
        output,
        grad_targets,
        mem_rows,
        self_grads[:, :part],
        self_grads[:, part : 2 * part],
        self_grads[:, 2 * part : 3 * part],
        self_grads[:, 3 * part : 4 * part].T,
        cross_grads[:, 0],
        cross_grads[:, 1],
        cross_grads[:, 2],
        cross_grads[:, 3].T,
        ffn_grads[:, :units],
        ffn_grads[:, units : 2 * units],
        ffn_grads[:, 2 * units :].T,
        self_grads[:, gains_at],
        self_grads[:, gains_at + 1],
        self_grads[:, gains_at + 2],
        self_grads[:, gains_at + 3 :].reshape(bias_local.shape),
    )


def solution(mesh):
    fits = mesh.shape["dp"] == 8 and mesh.shape["mp"] == 4
    return jax.shard_map(
        on_device if fits else on_device_permutes,
        mesh=mesh,
        in_specs=(
            P("dp", None, None),
            P("dp", None, None),
            P("dp", None, None),
            P("dp"),
            P("dp"),
            P(None, "mp"),
            P(None, "mp"),
            P(None, "mp"),
            P("mp", None),
            P(None, "mp"),
            P(None, "mp"),
            P(None, "mp"),
            P("mp", None),
            P(None, "mp"),
            P(None, "mp"),
            P("mp", None),
            P(),
            P(),
            P(),
            P(None, "mp"),
        ),
        out_specs=(
            P("dp", "mp", None),
            P("dp", "mp", None),
            P("dp", "mp", None),
            P("dp", "mp"),
            P("dp", "mp"),
            P("dp", "mp"),
            P("mp", "dp"),
            P("dp", "mp"),
            P("dp", "mp"),
            P("dp", "mp"),
            P("mp", "dp"),
            P("dp", "mp"),
            P("dp", "mp"),
            P("mp", "dp"),
            P("dp"),
            P("dp"),
            P("dp"),
            P(None, "mp"),
        ),
        check_vma=False,
    )
```

```python
import jax
import jax.numpy as jnp
import numpy as np
from jax import lax
from jax.experimental import pallas as pl
from jax.experimental.pallas import tpu as pltpu
from jax.sharding import PartitionSpec as P

HEAD_DIM = 64
BUCKETS = 32
MAX_DIST = 128


EPS = 1e-06
NEG = -1000000000.0


def bucket_table(length):
    distance = np.maximum(np.arange(length)[:, None] - np.arange(length)[None, :], 0)
    exact = BUCKETS // 2
    scaled = exact + (
        np.log(np.maximum(distance, 1) / exact) / np.log(MAX_DIST / exact) * (BUCKETS - exact)
    ).astype(np.int32)
    return np.where(distance < exact, distance, np.minimum(scaled, BUCKETS - 1)).astype(np.int32)


F32 = jnp.float32
BF16 = jnp.bfloat16
CHUNK = 256
SPAN = 512
COPIES = 128


def dot(left, right, left_dim, right_dim):
    return lax.dot_general(
        left, right, (((left_dim,), (right_dim,)), ((), ())), preferred_element_type=F32
    )


def dot_nn(left, right):
    return dot(left, right, 1, 0)


def dot_nt(left, right):
    return dot(left, right, 1, 1)


def dot_tn(left, right):
    return dot(left, right, 0, 0)


def unit_rows(resid):
    inv = lax.rsqrt(jnp.mean(resid * resid, -1, keepdims=True) + EPS)
    return inv, resid * inv


def norm_back(resid, gain, grad):
    inv, unit = unit_rows(resid)
    weighted = grad * gain
    grad_resid = inv * (weighted - unit * jnp.mean(weighted * unit, -1, keepdims=True))
    return grad_resid, jnp.sum(grad * unit, 0, keepdims=True)


def bucket_ranges(length):
    of_distance = bucket_table(length)[:, 0]
    ranges = []
    for k in range(BUCKETS):
        inside = np.flatnonzero(of_distance == k)
        ranges.append((int(inside[0]), int(inside[-1]) + 1) if len(inside) else (0, 0))
    return ranges


def place_of(chunk, order):
    y, z1, z2 = chunk % 2, chunk // 2 % 2, chunk // 4
    return 4 * y + 2 * z1 + z2 if order == "y" else 4 * z1 + 2 * y + z2


def layer_kernel(
    tlen_ref, mlen_ref, pos_ref, gain_self_ref, gain_cross_ref, gain_ffn_ref,
    x0_hbm, wq_hbm, wk_hbm, wv_hbm, wo_hbm, mem_hbm, cot_hbm, xq_hbm, xk_hbm, xv_hbm, xo_hbm, wg_hbm, wu_hbm, wd_hbm,
    out_ref, gt_ref, gm_ref, gf_ref, gx_ref, gs_ref, small_ref,
    q1, k1, v1, e1, r1, u1, o1, bias,
    part_send, part_recv, dn_recv, acc,
    x0_ref, wq_ref, wk_ref, wv_ref, wo_ref, mem, cot, wg, wu, wd, cross_w,
    x1, x2, n2, q2, kv2, e2, r2, u2, o2,
    n3, units, rows_low, rows_recv, rows_send_x, rows_recv_x,
    c2, turned, c1, f_low, f_recv0, f_recv1, f_recv2,
    x_recv0, x_recv1, x_recv2, x_send3, x_recv3, x_mid,
    s_low, s_recv1, s_recv2, small, small_recv,
    local_sem, send_sem, recv_sem,
):
    me = lax.axis_index("mp")
    core, chip = lax.rem(me, 2), lax.div(me, 2)
    other_core, other_chip = 1 - core, 1 - chip
    by_core = 2 * chip + other_core
    by_x = 2 * other_chip + core
    across = 2 * other_chip + other_core
    at_dp = lax.axis_index("dp")
    bit_y, bit_z1, bit_z2 = lax.rem(at_dp, 2), lax.rem(lax.div(at_dp, 2), 2), lax.div(at_dp, 4)
    to_core, to_x, to_across = {"mp": by_core}, {"mp": by_x}, {"mp": across}
    to_y = {"dp": at_dp + 1 - 2 * bit_y}
    to_z1 = {"dp": at_dp + 2 - 4 * bit_z1}
    to_z2 = {"dp": at_dp + 4 - 8 * bit_z2}

    seqs, length, width = x0_ref.shape
    part = wq_ref.shape[0]
    heads = part // HEAD_DIM
    slots = mem.shape[0]
    blocks = cross_w.shape[0]
    share = width // 8
    quarter = length // blocks

    gain_self_row, gain_cross_row, gain_ffn_row = (
        ref[...].reshape(1, width) for ref in (gain_self_ref, gain_cross_ref, gain_ffn_ref)
    )
    sent = {}
    names = iter(range(COPIES))

    def fresh(count):
        return [next(names) for _ in range(count)]

    def remote(i, src, dst, device):
        return pltpu.make_async_remote_copy(
            src_ref=src, dst_ref=dst, send_sem=send_sem.at[i], recv_sem=recv_sem.at[i],
            device_id=device, device_id_type=pl.DeviceIdType.MESH,
        )

    def note(i, src, dst, device, waited=False):
        sent[i] = remote(i, src, dst, device)

    def send(i, src, dst, device):
        remote(i, src, dst, device).start()
        note(i, src, dst, device)

    def left(*sends):
        for i in sends:
            sent.pop(i).wait_send()

    def arrived(i, dst, device):
        remote(i, dst, dst, device).wait_recv()

    def add_rows(ref, at, recv, from_at):
        ref[at, :] = (ref[at, :].astype(F32) + recv[from_at, :].astype(F32)).astype(BF16)

    class Sum:
        def __init__(self, low, recvs, order):
            self.low, self.recvs = low, recvs
            bits = (bit_y, bit_z1, bit_z2) if order == "y" else (bit_z1, bit_y, bit_z2)
            self.devices = (to_y, to_z1, to_z2) if order == "y" else (to_z1, to_y, to_z2)
            self.ids = fresh(3)
            self.away, self.kept, self.away_in, self.kept_in = [], [], [], []
            base = 0
            for k, bit in enumerate(bits):
                count = (4 >> k) * share

                def rows(start):
                    return pl.ds(pl.multiple_of(start, share), count)

                self.away.append(rows(base + (1 - bit) * count))
                self.kept.append(rows(base + bit * count))
                self.away_in.append(rows((1 - bit) * count))
                self.kept_in.append(rows(bit * count))
                base = base + bit * count

        def copy(self, k):
            return (self.ids[k], self.low.at[self.away[k]], self.recvs[k], self.devices[k])

        def start(self):
            send(*self.copy(0))

        def start_with(self, landed):
            add_rows(self.low, self.away[0], landed, self.away[0])
            send(*self.copy(0))
            add_rows(self.low, self.kept[0], landed, self.kept[0])

        def step(self, k, in_loop=False):
            recv = self.recvs[k - 1]
            arrived(self.ids[k - 1], recv, self.devices[k - 1])
            add_rows(self.low, self.away[k], recv, self.away_in[k])
            if in_loop:
                remote(*self.copy(k)).start()
            else:
                send(*self.copy(k))
            add_rows(self.low, self.kept[k], recv, self.kept_in[k])

        def total(self):
            arrived(self.ids[2], self.recvs[2], self.devices[2])
            return self.low[self.kept[2], :].astype(F32) + self.recvs[2][...].astype(F32)

    def neighbour(t):
        flip_x, flip_core = lax.div(t, 2), lax.rem(t, 2)
        at_x = chip + flip_x * (other_chip - chip)
        return 2 * at_x + core + flip_core * (other_core - core)

    barrier = pltpu.get_barrier_semaphore()
    partners = (to_core, to_x, to_across, to_y, to_z1, to_z2)
    for device in partners:
        pl.semaphore_signal(barrier, inc=1, device_id=device, device_id_type=pl.DeviceIdType.MESH)

    loads = [
        pltpu.make_async_copy(source, target, local_sem.at[i])
        for i, (source, target) in enumerate((
            (xk_hbm, cross_w.at[me, 0:part]),
            (xv_hbm, cross_w.at[me, part : 2 * part]),
            (xq_hbm, cross_w.at[me, 2 * part : 3 * part]),
            (xo_hbm, cross_w.at[me, 3 * part : 4 * part]),
            (x0_hbm, x0_ref),
            (wq_hbm, wq_ref),
            (wk_hbm, wk_ref),
            (wv_hbm, wv_ref),
            (wo_hbm, wo_ref),
            (mem_hbm.at[me], mem),
            (cot_hbm, cot),
            (wg_hbm, wg),
            (wu_hbm, wu),
            (wd_hbm, wd),
        ))
    ]
    for load in loads[:9]:
        load.start()
    for load in loads[:4]:
        load.wait()
    pl.semaphore_wait(barrier, len(partners))

    def piece(flip_y, flip_z1, p):
        at_y = bit_y + flip_y * (1 - 2 * bit_y)
        at_z1 = bit_z1 + flip_z1 * (1 - 2 * bit_z1)
        start = 2 * part * p + share * (at_y + 2 * at_z1)
        return pl.ds(pl.multiple_of(start, share), share)

    lows, highs = slice(0, 2 * part), slice(2 * part, 4 * part)
    w_core, w_x, w_y, w_z1, w_on = fresh(2), fresh(2), fresh(3), fresh(3), fresh(8)

    def weights_on(i, rows, device, in_loop=False):
        copy = (i, cross_w.at[by_x, rows], cross_w.at[by_x, rows], device)
        if in_loop:
            remote(*copy).start()
        else:
            send(*copy)
        return copy

    def weights_from(i, rows, device):
        arrived(i, cross_w.at[by_x, rows], device)

    def weights_from_x(p, in_loop=False):
        rows = piece(0, 0, p)
        weights_from(w_x[p], rows, to_x)
        return [
            weights_on(w_y[p], rows, to_y, in_loop),
            weights_on(w_z1[p], rows, to_z1, in_loop),
            weights_on(w_on[p], rows, to_core, in_loop),
        ]

    def weights_near(p):
        from_y, from_z1 = piece(1, 0, p), piece(0, 1, p)
        weights_from(w_y[p], from_y, to_y)
        if p == 0:
            weights_on(w_z1[2], from_y, to_z1)
        weights_on(w_on[2 + p], from_y, to_core)
        weights_from(w_z1[p], from_z1, to_z1)
        if p == 1:
            weights_on(w_y[2], from_z1, to_y)
        weights_on(w_on[4 + p], from_z1, to_core)

    def weights_far(p):
        i, device = ((w_z1[2], to_z1), (w_y[2], to_y))[p]
        weights_from(i, piece(1, 1, p), device)
        weights_on(w_on[6 + p], piece(1, 1, p), to_core)

    def weights_from_core(p):
        for i, (flip_y, flip_z1) in enumerate(((0, 0), (1, 0), (0, 1), (1, 1))):
            rows = piece(flip_y, flip_z1, p)
            arrived(w_on[2 * i + p], cross_w.at[across, rows], to_core)

    for p in range(2):
        rows = piece(0, 0, p)
        send(w_x[p], cross_w.at[me, rows], cross_w.at[me, rows], to_x)
    send(w_core[0], cross_w.at[me, lows], cross_w.at[me, lows], to_core)
    send(w_core[1], cross_w.at[me, highs], cross_w.at[me, highs], to_core)
    for load in loads[9:]:
        load.start()

    key_at = lax.broadcasted_iota(jnp.int32, (length, length), 0)
    query_at = lax.broadcasted_iota(jnp.int32, (length, length), 1)
    distance = lax.broadcasted_iota(jnp.int32, (8, length), 1)
    for h in range(heads):
        of_distance = jnp.zeros((8, length), F32)
        for k, (first, last) in enumerate(bucket_ranges(length)):
            inside = (distance >= first) & (distance < last)
            of_distance = jnp.where(inside, pos_ref[h, k], of_distance)
        spread = jnp.broadcast_to(of_distance[0:1], (length, length))
        shifted = pltpu.roll(spread, 0, 1, stride=1, stride_axis=0)
        bias[h] = jnp.where(key_at <= query_at, shifted, NEG)

    for load in loads[4:9]:
        load.wait()

    x1_core0, x1_x, x1_core1 = fresh(3)

    def self_one(t, carry):
        s = neighbour(3 - t)

        @pl.when(t == 3)
        def _():
            weights_from_x(0, True)

        resid = x0_ref[s].astype(F32)
        _, unit = unit_rows(resid)
        n = (unit * gain_self_row).astype(BF16)
        q = dot_nt(n, wq_ref[...]).astype(BF16)
        k = dot_nt(n, wk_ref[...]).astype(BF16)
        v = dot_nt(n, wv_ref[...]).astype(BF16)
        q1[s], k1[s], v1[s] = q, k, v
        mixed = []
        for h in range(heads):
            cols = slice(h * HEAD_DIM, (h + 1) * HEAD_DIM)
            scores = dot_nt(k[:, cols], q[:, cols]) + bias[h]
            scores = jnp.where(key_at < tlen_ref[s], scores, NEG)
            e = jnp.exp(scores - jnp.max(scores, 0, keepdims=True))
            r = 1.0 / jnp.sum(e, 0, keepdims=True)
            e = e.astype(BF16)
            e1[s, h] = e
            r1[s, h] = r
            u = dot_tn(v[:, cols], e)
            u1[s, h] = u
            mixed.append(u * r)
        o = jnp.concatenate(mixed, 0).T.astype(BF16)
        o1[s] = o
        value = dot_nn(o, wo_ref[...])

        @pl.when(t == 0)
        def _():
            part_send[0] = value.astype(BF16)
            remote(x1_core0, part_send.at[0], part_recv.at[0], to_core).start()

        @pl.when(t == 1)
        def _():
            arrived(x1_core0, part_recv.at[0], to_core)
            part_send[1] = (value + part_recv[0].astype(F32)).astype(BF16)
            remote(x1_x, part_send.at[1], part_recv.at[1], to_x).start()

        @pl.when(t == 2)
        def _():
            part_send[2] = value.astype(BF16)
            remote(x1_core1, part_send.at[2], part_recv.at[2], to_core).start()

        @pl.when(t == 3)
        def _():
            x1[...] = resid + value

        return carry

    lax.fori_loop(0, seqs, self_one, 0)
    note(x1_core0, part_send.at[0], part_recv.at[0], to_core, waited=True)
    note(x1_x, part_send.at[1], part_recv.at[1], to_x)
    note(x1_core1, part_send.at[2], part_recv.at[2], to_core)

    first = piece(0, 0, 0)
    for i, device in ((w_y[0], to_y), (w_z1[0], to_z1), (w_on[0], to_core)):
        note(i, cross_w.at[by_x, first], cross_w.at[by_x, first], device)

    def keys_values(b):
        for at in range(0, slots, CHUNK):
            rows = slice(at, at + CHUNK)
            kv2[b, rows, :] = dot_nt(mem[rows, :], cross_w[b, lows, :]).astype(BF16)

    loads[9].wait()
    arrived(w_core[0], cross_w.at[by_core, lows], to_core)

    def near_keys(t, carry):
        keys_values(neighbour(t))
        return carry

    lax.fori_loop(0, 2, near_keys, 0)
    weights_from_x(1)
    weights_near(0)
    arrived(w_core[1], cross_w.at[by_core, highs], to_core)
    weights_near(1)
    arrived(x1_core1, part_recv.at[2], to_core)
    arrived(x1_x, part_recv.at[1], to_x)

    def enter_cross(i, carry):
        rows = pl.ds(pl.multiple_of(i * quarter, quarter), quarter)
        resid = x1[rows, :] + part_recv[1, rows, :].astype(F32) + part_recv[2, rows, :].astype(F32)
        x1[rows, :] = resid
        x2[rows, :] = resid
        n2[rows, :] = (unit_rows(resid)[1] * gain_cross_row).astype(BF16)
        return carry

    lax.fori_loop(0, blocks, enter_cross, 0)
    weights_far(0)
    weights_far(1)
    slot_at = lax.broadcasted_iota(jnp.int32, (CHUNK, length), 0)
    spans = range(0, slots, SPAN)

    def cross_one(t, carry):
        b = neighbour(t)

        @pl.when(t == 2)
        def _():
            keys_values(by_x)

        @pl.when(t == 3)
        def _():
            weights_from_core(0)
            weights_from_core(1)
            keys_values(across)

        q = dot_nt(n2[...], cross_w[b, 2 * part : 3 * part, :]).astype(BF16)
        q2[b] = q
        mixed = []
        for h in range(heads):
            cols = slice(h * HEAD_DIM, (h + 1) * HEAD_DIM)
            cols_v = slice(part + h * HEAD_DIM, part + (h + 1) * HEAD_DIM)

            def scores_at(at):
                scores = dot_nt(kv2[b, at : at + CHUNK, cols], q[:, cols])
                return jnp.where(slot_at < mlen_ref[me] - at, scores, NEG)

            top = jnp.full((1, length), NEG, F32)
            for at in range(0, slots, CHUNK):
                top = jnp.maximum(top, jnp.max(scores_at(at), 0, keepdims=True))
            total = jnp.zeros((1, length), F32)
            u = jnp.zeros((HEAD_DIM, length), F32)
            for at in range(0, slots, CHUNK):
                rows = slice(at, at + CHUNK)
                e = jnp.exp(scores_at(at) - top)
                total = total + jnp.sum(e, 0, keepdims=True)
                e = e.astype(BF16)
                e2[b * heads + h, rows, :] = e
                u = u + dot_tn(kv2[b, rows, cols_v], e)
            r = 1.0 / total
            r2[b * heads + h] = r
            u2[b * heads + h] = u
            mixed.append(u * r)
        o = jnp.concatenate(mixed, 0).T.astype(BF16)
        o2[b] = o
        x2[...] += dot_nn(o, cross_w[b, 3 * part : 4 * part, :])
        return carry

    lax.fori_loop(0, blocks, cross_one, 0)

    n3_x, n3_core, n3_on = fresh(blocks), next(names), fresh(blocks)
    dn_near, dn_core, dn_x = next(names), fresh(blocks), fresh(blocks)

    def quarter_at(i):
        return pl.ds(pl.multiple_of(i * quarter, quarter), quarter)

    def n3_to_x(i):
        return (n3_x[0] + i, n3.at[me, quarter_at(i)], n3.at[me, quarter_at(i)], to_x)

    def n3_to_core(i):
        return (n3_on[0] + i, n3.at[by_x, quarter_at(i)], n3.at[by_x, quarter_at(i)], to_core)

    def dn_to_core(i):
        rows = quarter_at(i)
        return (dn_core[0] + i, part_send.at[1, rows], dn_recv.at[1, rows], to_core)

    def dn_to_x(i):
        return (dn_x[0] + i, part_send.at[2, quarter_at(i)], dn_recv.at[2, quarter_at(i)], to_x)

    def enter_ffn(i, carry):
        rows = quarter_at(i)
        n3[me, rows, :] = (unit_rows(x2[rows, :])[1] * gain_ffn_row).astype(BF16)
        remote(*n3_to_x(i)).start()
        return carry

    lax.fori_loop(0, blocks, enter_ffn, 0)
    for i in range(blocks):
        note(*n3_to_x(i), waited=True)
    send(n3_core, n3.at[me], n3.at[me], to_core)
    for load in loads[10:]:
        load.wait()
    left(x1_core0, x1_x, x1_core1)
    scale, cubic = 0.7978845608028654, 0.044715

    def turn(slot, value, first_col, order=None):
        value = value.T
        cols = pl.ds(first_col, value.shape[1])
        if order is None:
            turned[slot, :, cols] = value
            return
        for j in range(8):
            at = place_of(j, order) * share
            turned[slot, at : at + share, cols] = value[j * share : (j + 1) * share]

    def turn_normed(s):
        turn(0, n3[s], pl.multiple_of(s * length, length), "y")

    def ffn_rows(n, c, at_rows):
        count = n.shape[0] // len(at_rows)
        for at in range(0, wg.shape[1], CHUNK):
            cols = slice(at, at + CHUNK)
            a = dot_nn(n, wg[:, cols])
            b = dot_nn(n, wu[:, cols])
            dh = dot_nt(c, wd[cols, :])
            square = a * a
            slope = jnp.tanh(scale * (a + cubic * (a * square)))
            mid = 0.5 * (1.0 + slope)
            gelu = a * mid
            rise = mid + 0.5 * a * (1.0 - slope * slope) * (scale * (1.0 + 3.0 * cubic * square))
            for i, value in enumerate((dh * b * rise, dh * gelu, gelu * b)):
                value = value.astype(BF16)
                for j, rows in enumerate(at_rows):
                    units[i, rows, cols] = value[j * count : (j + 1) * count]

        def whole(i):
            return jnp.concatenate([units[i, rows, :] for rows in at_rows], 0)

        dn = dot_nt(whole(0), wg[...]) + dot_nt(whole(1), wu[...])
        return dn, lambda: dot_nn(whole(2), wd[...])

    def ffn_near(t, carry):
        s = neighbour(t)

        @pl.when(t == 1)
        def _():
            arrived(n3_core, n3.at[by_core], to_core)

        rows = pl.ds(pl.multiple_of(s * length, length), length)
        dn, result = ffn_rows(n3[s], cot[s], [rows])

        @pl.when(t == 0)
        def _():
            acc[...] = dn

        @pl.when(t == 1)
        def _():
            part_send[0] = dn.astype(BF16)
            remote(dn_near, part_send.at[0], dn_recv.at[0], to_core).start()

        own = jnp.where(t == 0, 1.0, 0.0)
        low = (result() + own * x2[...]).astype(BF16)
        for i in range(blocks):
            rows_low[i % 2, i // 2, s] = low[i * quarter : (i + 1) * quarter]
        return carry

    lax.fori_loop(0, 2, ffn_near, 0)
    note(dn_near, part_send.at[0], dn_recv.at[0], to_core)
    turn_normed(me)
    turn_normed(by_core)

    def pass_dn(i):
        rows = quarter_at(i)
        arrived(dn_core[0] + i, dn_recv.at[1, rows], to_core)
        part_send[2, rows, :] = (
            part_send[2, rows, :].astype(F32) + dn_recv[1, rows, :].astype(F32)
        ).astype(BF16)
        remote(*dn_to_x(i)).start()

    def ffn_far(t, carry):
        rows = quarter_at(t)

        @pl.when(t > 0)
        def _():
            pass_dn(t - 1)

        arrived(n3_x[0] + t, n3.at[by_x, rows], to_x)
        remote(*n3_to_core(t)).start()
        turn(1, cot[t], pl.multiple_of(t * length, length), "z1")
        arrived(n3_on[0] + t, n3.at[across, rows], to_core)
        n = jnp.concatenate([n3[by_x, rows, :], n3[across, rows, :]], 0)
        c = jnp.concatenate([cot[by_x, rows, :], cot[across, rows, :]], 0)
        dn, result = ffn_rows(
            n, c, [
                pl.ds(pl.multiple_of(s * length + t * quarter, quarter), quarter)
                for s in (by_x, across)
            ],
        )
        part_send[1, rows, :] = dn[quarter:].astype(BF16)
        remote(*dn_to_core(t)).start()
        part_send[2, rows, :] = dn[:quarter].astype(BF16)
        low = result().astype(BF16)
        rows_low[lax.rem(t, 2), lax.div(t, 2), by_x] = low[:quarter]
        rows_low[lax.rem(t, 2), lax.div(t, 2), across] = low[quarter:]
        return carry

    lax.fori_loop(0, blocks, ffn_far, 0)
    pass_dn(blocks - 1)
    for i in range(blocks):
        note(*n3_to_core(i), waited=True)
        note(*dn_to_core(i), waited=True)
        note(*dn_to_x(i))
    out_core, out_x = fresh(2)
    send(out_core, rows_low.at[other_core], rows_recv, to_core)
    turn_normed(by_x)
    turn_normed(across)
    orders = ("y", "y", "z1")
    f_sums = [
        Sum(f_low.at[i], [f_recv0.at[i], f_recv1.at[i], f_recv2.at[i]], orders[i]) for i in range(3)
    ]

    def ffn_grad(i, rows):
        f_low[i, rows, :] = dot_nn(turned[i // 2, rows, :], units[i]).astype(BF16)

    for i in (0, 2, 1):
        ffn_grad(i, f_sums[i].away[0])
        f_sums[i].start()
    for i in (0, 2, 1):
        ffn_grad(i, f_sums[i].kept[0])

    arrived(out_core, rows_recv, to_core)
    rows_send_x[...] = (
        rows_low[core, other_chip].astype(F32) + rows_recv[other_chip].astype(F32)
    ).astype(BF16)
    send(out_x, rows_send_x, rows_recv_x, to_x)

    arrived(dn_near, dn_recv.at[0], to_core)
    for i in range(blocks):
        arrived(dn_x[i], dn_recv.at[2, quarter_at(i)], to_x)
    small[...] = jnp.zeros_like(small)

    def enter_back(i, carry):
        rows = pl.ds(pl.multiple_of(i * quarter, quarter), quarter)
        dn3 = acc[rows, :] + dn_recv[0, rows, :].astype(F32) + dn_recv[2, rows, :].astype(F32)
        grad, gain_ffn = norm_back(x2[rows, :], gain_ffn_row, dn3)
        dx2 = cot[me, rows, :].astype(F32) + grad
        acc[rows, :] = dx2
        c2[rows, :] = dx2.astype(BF16)
        small[0, 2:3, :] += gain_ffn
        return carry

    lax.fori_loop(0, blocks, enter_back, 0)

    def cross_back(b, carry):
        @pl.when(b == 2)
        def _():
            f_sums[0].step(1, True)

        @pl.when(b == 3)
        def _():
            f_sums[2].step(1, True)

        do = dot_nt(cross_w[b, 3 * part : 4 * part, :], c2[...])
        q = q2[b]
        dqs = []
        for h in range(heads):
            cols = slice(h * HEAD_DIM, (h + 1) * HEAD_DIM)
            cols_v = slice(part + h * HEAD_DIM, part + (h + 1) * HEAD_DIM)
            r = r2[b * heads + h]
            low = (do[cols] * r).astype(BF16)
            delta = r * jnp.sum(low.astype(F32) * u2[b * heads + h], 0, keepdims=True)
            dq = jnp.zeros((HEAD_DIM, length), F32)
            for at in spans:
                rows = slice(at, at + SPAN)
                e = e2[b * heads + h, rows, :]
                dp = dot_nn(kv2[b, rows, cols_v], low)
                ds = e * (dp - delta).astype(BF16)
                dq = dq + dot_tn(kv2[b, rows, cols], ds)
                kv2[b, rows, cols_v] = dot_nt(e, low).astype(BF16)
                kv2[b, rows, cols] = dot_nn(ds, q[:, cols]).astype(BF16)
            dqs.append(dq)
        q2[b] = jnp.concatenate(dqs, 0).T.astype(BF16)
        return carry

    lax.fori_loop(0, blocks, cross_back, 0)
    for i in (0, 2):
        note(*f_sums[i].copy(1))
    dn2 = dot_nn(q2[0], cross_w[0, 2 * part : 3 * part, :])
    for b in range(1, blocks):
        dn2 = dn2 + dot_nn(q2[b], cross_w[b, 2 * part : 3 * part, :])
    x2[...] = dn2

    def leave_cross(i, carry):
        rows = pl.ds(pl.multiple_of(i * quarter, quarter), quarter)
        grad, gain_cross = norm_back(x1[rows, :], gain_cross_row, x2[rows, :])
        c1[me, rows, :] = (acc[rows, :] + grad).astype(BF16)
        small[0, 1:2, :] += gain_cross
        return carry

    lax.fori_loop(0, blocks, leave_cross, 0)
    arrived(out_x, rows_recv_x, to_x)
    out_ref[...] = (
        rows_low[core, chip].astype(F32)
        + rows_recv[chip].astype(F32)
        + rows_recv_x[...].astype(F32)
    ).astype(BF16)
    left(out_core, out_x)
    c1_x, c1_core, c1_on = fresh(3)
    send(c1_x, c1.at[me], c1.at[me], to_x)
    send(c1_core, c1.at[me], c1.at[me], to_core)
    f_sums[1].step(1)
    turn(0, mem[...], 0)
    turn(1, n2[...], 0)
    turn(1, c2[...], length)

    def put(slabs, first_row, first_col, value):
        at = 0
        while at < value.shape[1]:
            slab, col = divmod(first_col + at, 256)
            count = min(256 - col, value.shape[1] - at)
            for i in range(value.shape[0] // share):
                row = place_of(first_row // share + i, orders[slab]) * share
                slabs[slab][row : row + share, col : col + count] = value[
                    i * share : (i + 1) * share, at : at + count
                ]
            at += count

    def cross_grads(b):
        slabs = [e2.at[3 * b + j] for j in range(3)]
        for at in range(0, width, width // 2):
            rows = slice(at, at + width // 2)
            put(slabs, at, 0, dot_nn(turned[0, rows, :], kv2[b]).astype(BF16))
            put(slabs, at, 2 * part, dot_nn(turned[1, rows, 0:length], q2[b]).astype(BF16))
            put(slabs, at, 3 * part, dot_nn(turned[1, rows, length : 2 * length], o2[b]).astype(BF16))

    def landing(i, j):
        return units.at[j, 0:width, 256 * i : 256 * (i + 1)]

    x_core = [fresh(3) for _ in range(2)]
    x_sums = [
        [
            Sum(
                e2.at[3 * (2 * i + core) + j],
                [x_recv0.at[i, j], x_recv1.at[i, j], x_recv2.at[i, j]],
                orders[j],
            )
            for j in range(3)
        ]
        for i in range(2)
    ]
    mid_sum = Sum(
        e2.at[3 * (2 * chip + core) + 1], [x_mid, x_recv1.at[0, 1], x_recv2.at[0, 1]], "y"
    )
    mid_x = fresh(2)
    mid_halves = [slice(0, 4 * share), slice(4 * share, 8 * share)]

    def cross_away(i):
        b = 2 * i + other_core
        cross_grads(b)
        if i == 0:
            arrived(c1_core, c1.at[by_core], to_core)
        for j in range(3):
            send(x_core[i][j], e2.at[3 * b + j, 0:width], landing(i, j), to_core)

    def cross_start(i):
        for j in (0, 2):
            arrived(x_core[i][j], landing(i, j), to_core)
            x_sums[i][j].start_with(landing(i, j))
        arrived(x_core[i][1], landing(i, 1), to_core)
        for rows in mid_halves:
            add_rows(e2.at[3 * (2 * i + core) + 1], rows, landing(i, 1), rows)

    cross_away(0)
    cross_grads(core)
    cross_away(1)
    cross_start(0)
    for i in (0, 2):
        f_sums[i].step(2)
    cross_grads(2 + core)
    cross_start(1)
    for i in range(2):
        send(
            mid_x[i], e2.at[3 * (2 * other_chip + core) + 1, mid_halves[i]], x_recv0.at[i, 1], to_x
        )

    left(*n3_x, n3_core, *n3_on)
    gm_x, gm_across, gm_core = fresh(3)

    def memory_grad(target):
        rows = pl.ds(pl.multiple_of(target * CHUNK, CHUNK), CHUNK)
        for at in range(0, width, CHUNK):
            cols = slice(at, at + CHUNK)
            total = dot_nn(kv2[0, rows, :], cross_w[0, lows, cols])
            for b in range(1, blocks):
                total = total + dot_nn(kv2[b, rows, :], cross_w[b, lows, cols])
            n3[target, :, cols] = total.astype(BF16)

    memory_grad(by_x)
    send(gm_x, n3.at[by_x], gm_ref.at[me], to_x)
    memory_grad(across)
    send(gm_across, n3.at[across], gm_ref.at[me], to_across)

    bias[...] = jnp.zeros_like(bias)

    def self_back(t, carry):
        s = neighbour(t)

        @pl.when(t == 2)
        def _():
            arrived(c1_x, c1.at[by_x], to_x)
            remote(c1_on, c1.at[by_x], c1.at[by_x], to_core).start()
            f_sums[1].step(2, True)
            x_sums[0][0].step(1, True)
            x_sums[0][2].step(1, True)

        @pl.when(t == 3)
        def _():
            arrived(c1_on, c1.at[across], to_core)
            x_sums[1][0].step(1, True)
            x_sums[1][2].step(1, True)

        do = dot_nt(wo_ref[...], c1[s])
        dqs = []
        for h in range(heads):
            cols = slice(h * HEAD_DIM, (h + 1) * HEAD_DIM)
            r = r1[s, h]
            low = (do[cols] * r).astype(BF16)
            delta = r * jnp.sum(low.astype(F32) * u1[s, h], 0, keepdims=True)
            e = e1[s, h]
            dp = dot_nn(v1[s, :, cols], low)
            ds = e * (dp - delta).astype(BF16)
            bias[h] += ds.astype(F32)
            dqs.append(dot_tn(k1[s, :, cols], ds))
            v1[s, :, cols] = dot_nt(e, low).astype(BF16)
            k1[s, :, cols] = dot_nn(ds, q1[s, :, cols]).astype(BF16)
        q1[s] = jnp.concatenate(dqs, 0).T.astype(BF16)
        dn = dot_nn(q1[s], wq_ref[...]) + dot_nn(k1[s], wk_ref[...]) + dot_nn(v1[s], wv_ref[...])
        acc[...] = dn
        for i in range(blocks):
            rows = slice(i * quarter, (i + 1) * quarter)
            unit = unit_rows(x0_ref[s, rows, :].astype(F32))[1]
            small[0, 0:1, :] += jnp.sum(acc[rows, :] * unit, 0, keepdims=True)
            rows_low[i % 2, i // 2, s] = acc[rows, :].astype(BF16)
        return carry

    lax.fori_loop(0, seqs, self_back, 0)
    note(c1_on, c1.at[by_x], c1.at[by_x], to_core, waited=True)
    note(*f_sums[1].copy(2))
    for i in range(2):
        note(*x_sums[i][2].copy(1))
        note(*x_sums[i][0].copy(1))
    dn1_core, dn1_x, small_y, small_z1, small_z2 = fresh(5)
    small_mp = fresh(3)
    send(dn1_core, rows_low.at[other_core], rows_recv, to_core)
    for h in range(heads):
        total = bias[h]
        step = 1
        while step < length:
            total = jnp.where((key_at & step) != 0, pltpu.roll(total, length - step, 1), total)
            step *= 2
        small[0, 3 + h : 4 + h, 0:length] = jnp.sum(total, 0, keepdims=True)
    send(small_y, small.at[0], small_recv.at[0], to_y)
    for i in range(2):
        arrived(mid_x[i], x_recv0.at[i, 1], to_x)
        add_rows(e2.at[3 * (2 * chip + core) + 1], mid_halves[i], x_recv0.at[i, 1], slice(None))
    mid_sum.start()

    for s in range(seqs):
        _, unit = unit_rows(x0_ref[s].astype(F32))
        turn(0, (unit * gain_self_row).astype(BF16), s * length)
        turn(1, c1[s], s * length)
    slabs = [s_low.at[j] for j in range(3)]
    s_sums = [
        Sum(s_low.at[j], [f_recv0.at[j, :, 0:256], s_recv1.at[j], s_recv2.at[j]], orders[j]) for j in range(3)
    ]
    for i, ref in ((2, q1), (3, o1), (0, k1), (1, v1)):
        right = ref[...].reshape(seqs * length, part)
        for at in range(0, width, width // 2):
            value = dot_nn(turned[i // 3, at : at + width // 2, :], right).astype(BF16)
            put(slabs, at, i * part, value)
        if i == 3:
            s_sums[2].start()
            x_sums[0][0].step(2)
            x_sums[1][0].step(2)
    s_sums[0].start()
    s_sums[1].start()

    arrived(dn1_core, rows_recv, to_core)
    rows_send_x[...] = (
        rows_low[core, other_chip].astype(F32) + rows_recv[other_chip].astype(F32)
    ).astype(BF16)
    send(dn1_x, rows_send_x, rows_recv_x, to_x)

    def pass_small(i, came, device, goes, onward):
        arrived(came, small_recv.at[i], device)
        small[i + 1] = small[i] + small_recv[i]
        if goes is not None:
            send(goes, small.at[i + 1], small_recv.at[i + 1], onward)

    mid_sum.step(1)
    memory_grad(by_core)
    send(gm_core, n3.at[by_core], gm_ref.at[me], to_core)
    memory_grad(me)
    own_rows = pltpu.make_async_copy(n3.at[me], gm_ref.at[me], local_sem.at[15])
    own_rows.start()
    pass_small(0, small_y, to_y, small_z1, to_z1)

    s_sums[2].step(1)
    for i in range(2):
        x_sums[i][2].step(2)
    mid_sum.step(2)
    s_sums[0].step(1)
    pass_small(1, small_z1, to_z1, small_z2, to_z2)
    s_sums[1].step(1)
    s_sums[2].step(2)
    s_sums[0].step(2)
    for i in range(3):
        gf_ref[i] = f_sums[i].total()

    s_sums[1].step(2)

    last_x = next(names)
    for i in range(2):
        for j in (0, 2):
            arrived(x_sums[i][j].ids[2], x_recv2.at[i, j], to_z2)

    def cross_total(at, j):
        rows = x_sums[0][j].kept[2]
        return e2[3 * (2 * at + core) + j, rows, :].astype(F32) + x_recv2[at, j].astype(F32)

    for i, j in enumerate((0, 2)):
        x_send3[i] = cross_total(other_chip, j).astype(BF16)
    send(last_x, x_send3, x_recv3, to_x)
    pass_small(2, small_z2, to_z2, None, None)
    mp_peers = (to_core, to_x, to_across)
    for i, device in enumerate(mp_peers):
        send(small_mp[i], small.at[3], small_recv.at[3 + i], device)
    arrived(dn1_x, rows_recv_x, to_x)
    my_rows = pl.ds(pl.multiple_of(me * quarter, quarter), quarter)
    for s in range(seqs):
        dn = (
            rows_low[core, chip, s].astype(F32)
            + rows_recv[chip, s].astype(F32)
            + rows_recv_x[s].astype(F32)
        )
        grad, _ = norm_back(x0_ref[s, my_rows, :].astype(F32), gain_self_row, dn)
        gt_ref[s] = (c1[s, my_rows, :].astype(F32) + grad).astype(BF16)
    for j in range(3):
        gs_ref[j] = s_sums[j].total()
    arrived(last_x, x_recv3, to_x)
    for i, j in enumerate((0, 2)):
        gx_ref[j] = cross_total(chip, j) + x_recv3[i].astype(F32)
    gx_ref[1] = mid_sum.total()
    for i, device in enumerate(mp_peers):
        arrived(small_mp[i], small_recv.at[3 + i], device)
    small_ref[0] = small[3] + small_recv[3] + small_recv[4] + small_recv[5]
    small_ref[1] = small[3]
    arrived(gm_x, gm_ref.at[by_x], to_x)
    arrived(gm_across, gm_ref.at[across], to_across)
    arrived(gm_core, gm_ref.at[by_core], to_core)
    own_rows.wait()
    for copy in sent.values():
        copy.wait_send()


def finish_kernel(
    gf_ref, gx_ref, gs_ref, small_ref, onehot_ref, out_ref, gt_ref, gm_ref,
    out_o, gt_o, gm_o, sq_o, sk_o, sv_o, so_o, cq_o, ck_o, cv_o, co_o, gg_o, gu_o, gd_o,
    gain_self_o, gain_cross_o, gain_ffn_o, bias_o,
):
    part, share = sq_o.shape[1], sq_o.shape[0]
    width = small_ref.shape[2]
    out_o[...], gt_o[...], gm_o[...] = out_ref[...], gt_ref[...], gm_ref[...]
    gg_o[...], gu_o[...], gd_o[...] = gf_ref[0], gf_ref[1], gf_ref[2]
    for source, refs in ((gx_ref, (ck_o, cv_o, cq_o, co_o)), (gs_ref, (sk_o, sv_o, sq_o, so_o))):
        value = jnp.concatenate([source[0], source[1], source[2]], 1)
        for i in range(3):
            refs[i][...] = value[:, i * part : (i + 1) * part]
        refs[3][...] = value[:, 3 * part :].T
    shift = width - lax.axis_index("dp") * share
    gains = pltpu.roll(small_ref[0], shift, 1)
    for i, ref in enumerate((gain_self_o, gain_cross_o, gain_ffn_o)):
        ref[...] = gains[i : i + 1, 0:share]
    bias_o[...] = lax.dot_general(
        small_ref[1, 3 : 3 + bias_o.shape[0], 0 : onehot_ref.shape[0]], onehot_ref[...], (((1,), (0,)), ((), ())),
        precision=lax.Precision.HIGHEST, preferred_element_type=F32,
    )


VMEM = pl.BlockSpec(memory_space=pltpu.VMEM)
SMEM = pl.BlockSpec(memory_space=pltpu.SMEM)
ANY = pl.BlockSpec(memory_space=pl.ANY)


def on_device(
    targets,
    memory,
    cotangent,
    target_len,
    memory_len,
    query_self,
    key_self,
    value_self,
    out_self,
    query_cross,
    key_cross,
    value_cross,
    out_cross,
    gate_proj,
    up_proj,
    down_proj,
    gain_self,
    gain_cross,
    gain_ffn,
    pos_bias,
):
    seqs, length, width = targets.shape
    slots = memory.shape[1]
    part = query_self.shape[1]
    units = gate_proj.shape[1]
    heads = part // HEAD_DIM
    blocks = lax.axis_size("mp")
    dp_size = lax.axis_size("dp")
    share = width // dp_size
    quarter = length // blocks
    head_all = heads * blocks

    onehot = jnp.asarray(
        (bucket_table(length)[:, 0][:, None] == np.arange(BUCKETS)[None, :]).astype(np.float32)
    )
    def low(*shape):
        return pltpu.VMEM(shape, BF16)

    def full(*shape):
        return pltpu.VMEM(shape, F32)

    def sums(count, columns):
        return [low(count, 4 * share, columns), low(count, 2 * share, columns), low(count, share, columns)]

    scratch = [
        low(seqs, length, part), low(seqs, length, part), low(seqs, length, part),
        low(seqs, heads, length, length), full(seqs, heads, 1, length),
        full(seqs, heads, HEAD_DIM, length), low(seqs, length, part), full(heads, length, length),
        low(3, length, width), low(3, length, width), low(3, length, width),
        full(length, width),
        low(seqs, length, width), low(part, width), low(part, width), low(part, width),
        low(part, width), low(slots, width), low(seqs, length, width),
        low(width, units), low(width, units), low(units, width), low(blocks, 4 * part, width),
        full(length, width), full(length, width), low(length, width), low(blocks, length, part),
        low(blocks, slots, 2 * part), low(head_all, slots, length), full(head_all, 1, length),
        full(head_all, HEAD_DIM, length), low(blocks, length, part),
        low(seqs, length, width), low(3, seqs * length, units),
        low(2, 2, seqs, quarter, width), low(2, seqs, quarter, width),
        low(seqs, quarter, width), low(seqs, quarter, width),
        low(length, width), low(2, width, seqs * length), low(seqs, length, width),
        low(3, width, units), *sums(3, units),
        low(2, 3, 4 * share, 256), low(2, 3, 2 * share, 256), low(2, 3, share, 256),
        low(2, share, 256), low(2, share, 256), low(4 * share, 256),
        low(3, width, 256), *sums(3, 256)[1:],
        full(4, 8, width), full(6, 8, width),
        pltpu.SemaphoreType.DMA((16,)),
        pltpu.SemaphoreType.DMA((COPIES,)),
        pltpu.SemaphoreType.DMA((COPIES,)),
    ]
    struct = jax.ShapeDtypeStruct
    rows = struct((seqs, quarter, width), BF16)
    out, gt, gm, gf, gx, gs, small = pl.pallas_call(
        layer_kernel,
        out_shape=[
            rows,
            rows,
            struct((seqs, slots // blocks, width), BF16),
            struct((3, share, units), F32),
            struct((3, share, 256), F32),
            struct((3, share, 256), F32),
            struct((2, 8, width), F32),
        ],
        in_specs=[SMEM] * 3 + [VMEM] * 3 + [ANY] * 14,
        out_specs=[VMEM, VMEM, ANY, VMEM, VMEM, VMEM, VMEM],
        scratch_shapes=scratch,
        compiler_params=pltpu.CompilerParams(
            collective_id=0, has_side_effects=True, vmem_limit_bytes=63 * 2**20
        ),
        cost_estimate=pl.CostEstimate(flops=24 * 10**9, bytes_accessed=2**24, transcendentals=0),
        name="layer",
    )(
        target_len, memory_len, pos_bias.T,
        gain_self, gain_cross, gain_ffn, targets,
        query_self.T, key_self.T, value_self.T, out_self, memory, cotangent, query_cross.T, key_cross.T, value_cross.T, out_cross,
        gate_proj, up_proj, down_proj,
    )
    square = struct((share, part), F32)
    turned = struct((part, share), F32)
    (
        out, gt, gm, sq, sk, sv, so, cq, ck, cv, co, gg, gu, gd,
        grad_self, grad_cross, grad_ffn, bias,
    ) = pl.pallas_call(
        finish_kernel,
        out_shape=[
            rows, rows, struct((seqs, slots // blocks, width), BF16),
            square, square, square, turned, square, square, square, turned,
            struct((share, units), F32), struct((share, units), F32), struct((share, units), F32),
            struct((1, share), F32), struct((1, share), F32), struct((1, share), F32),
            struct((heads, BUCKETS), F32),
        ],
        in_specs=[VMEM] * 8,
        out_specs=[VMEM] * 18,
        compiler_params=pltpu.CompilerParams(vmem_limit_bytes=62 * 2**20),
        name="finish",
    )(gf, gx, gs, small, onehot, out, gt, gm)
    return (
        out, gt, gm, sq, sk, sv, so, cq, ck, cv, co, gg, gu, gd.T,
        grad_self[0], grad_cross[0], grad_ffn[0], bias.T,
    )


def project(inputs, weight):
    return jnp.einsum("bld,df->blf", inputs, weight, preferred_element_type=jnp.float32)


def back_project(gradient, weight):
    return jnp.einsum("blf,df->bld", gradient, weight, preferred_element_type=jnp.float32)


def weight_grad(inputs, gradient):
    return jnp.einsum("bld,blf->df", inputs, gradient, preferred_element_type=jnp.float32)


def norm_forward(resid, gain):
    inv_rms = lax.rsqrt(jnp.mean(resid * resid, -1, keepdims=True) + EPS)
    return (resid * inv_rms * gain, inv_rms)


def norm_backward(resid, inv_rms, gain, grad_normed):
    unit_rows = resid * inv_rms
    grad_gain = jnp.sum(grad_normed * unit_rows, axis=(0, 1))
    weighted = grad_normed * gain
    grad_resid = inv_rms * (
        weighted - unit_rows * jnp.mean(weighted * unit_rows, -1, keepdims=True)
    )
    return (grad_resid, grad_gain)


def scores_of(queries, keys, score_bias, valid):
    scores = (
        jnp.einsum("bihe,bjhe->bhij", queries, keys, preferred_element_type=jnp.float32)
        + score_bias
    )
    return jnp.where(valid, scores, NEG)


def attend(queries, keys, values, score_bias, valid):
    scores = scores_of(queries, keys, score_bias, valid)
    row_max = jnp.max(scores, -1, keepdims=True)
    log_total = row_max + jnp.log(jnp.sum(jnp.exp(scores - row_max), -1, keepdims=True))
    attn_probs = jnp.exp(scores - log_total).astype(jnp.bfloat16)
    mixed = jnp.einsum("bhij,bjhe->bihe", attn_probs, values, preferred_element_type=jnp.float32)
    return (mixed, log_total)


def attend_back(queries, keys, values, score_bias, valid, log_total, grad_mixed):
    attn_probs = jnp.exp(scores_of(queries, keys, score_bias, valid) - log_total)
    grad_values = jnp.einsum(
        "bhij,bihe->bjhe",
        attn_probs.astype(jnp.bfloat16),
        grad_mixed,
        preferred_element_type=jnp.float32,
    )
    grad_probs = jnp.einsum(
        "bihe,bjhe->bhij", grad_mixed, values, preferred_element_type=jnp.float32
    )
    grad_scores = attn_probs * (grad_probs - jnp.sum(attn_probs * grad_probs, -1, keepdims=True))
    grad_low = grad_scores.astype(jnp.bfloat16)
    grad_queries = jnp.einsum("bhij,bjhe->bihe", grad_low, keys, preferred_element_type=jnp.float32)
    grad_keys = jnp.einsum("bhij,bihe->bjhe", grad_low, queries, preferred_element_type=jnp.float32)
    return (grad_queries, grad_keys, grad_values, grad_low)


def swap(value, axis, bit):
    return lax.ppermute(value, axis, [(i, i ^ bit) for i in range(lax.axis_size(axis))])


def bits_of(axis):
    return [1 << i for i in range(lax.axis_size(axis).bit_length() - 1)]


def split_bits(value, axis, dim):
    steps = len(bits_of(axis))
    shape = value.shape
    return value.reshape(
        shape[:dim] + (2,) * steps + (shape[dim] >> steps,) + shape[dim + 1 :]
    )


def own_bit(axis, bit):
    return (lax.axis_index(axis) & bit) // bit


def halve(value, axis, bit, dim):
    mine = own_bit(axis, bit)
    kept = lax.dynamic_index_in_dim(value, mine, dim, keepdims=False)
    sent = lax.dynamic_index_in_dim(value, 1 - mine, dim, keepdims=False)
    arrived = swap(sent.astype(jnp.bfloat16), axis, bit)
    return kept + arrived.astype(jnp.float32)


def reduce_scatter(value, axis, dim):
    bits = bits_of(axis)
    value = split_bits(value, axis, dim)
    for at, bit in enumerate(bits):
        value = halve(value, axis, bit, dim + len(bits) - 1 - at)
    return value


def gather_mp(value):
    value = value[None]
    for bit in reversed(bits_of("mp")):
        other = swap(value, "mp", bit)
        first = own_bit("mp", bit) == 0
        low = jnp.where(first, value, other)
        high = jnp.where(first, other, value)
        value = jnp.stack([low, high], 1 if bit == 1 else 0)
        value = value.reshape((-1,) + value.shape[2:])
    return value


def exchange_mp(value):
    count = lax.axis_size("mp")
    value = split_bits(value, "mp", 0)[None]
    steps = len(bits_of("mp"))
    for at, bit in enumerate(bits_of("mp")):
        dim = steps - at
        mine = own_bit("mp", bit)
        kept = lax.dynamic_index_in_dim(value, mine, dim, keepdims=False)
        sent = lax.dynamic_index_in_dim(value, 1 - mine, dim, keepdims=False)
        arrived = swap(sent, "mp", bit)
        first = mine == 0
        low = jnp.where(first, kept, arrived)
        high = jnp.where(first, arrived, kept)
        value = jnp.stack([low, high], 0)
        value = value.reshape((-1,) + value.shape[2:])
    return value.reshape((count,) + value.shape[1:])


def sum_mp(value):
    for bit in bits_of("mp"):
        value = value + swap(value, "mp", bit)
    return value


def on_device_permutes(
    targets,
    memory,
    cotangent,
    target_len,
    memory_len,
    query_self,
    key_self,
    value_self,
    out_self,
    query_cross,
    key_cross,
    value_cross,
    out_cross,
    gate_proj,
    up_proj,
    down_proj,
    gain_self,
    gain_cross,
    gain_ffn,
    pos_bias,
):
    length = targets.shape[1]
    heads_local = query_self.shape[1] // HEAD_DIM
    mp_size = lax.axis_size("mp")
    dp_size = lax.axis_size("dp")
    mp_index = lax.axis_index("mp")
    row_share = length // mp_size
    width = targets.shape[2]

    def split_heads(value):
        return value.reshape(value.shape[0], value.shape[1], -1, HEAD_DIM)

    def merge_heads(value):
        return value.reshape(value.shape[0], value.shape[1], -1)

    def my_rows(value):
        return lax.dynamic_slice_in_dim(value, mp_index * row_share, row_share, 1)

    def mine(value):
        return lax.dynamic_index_in_dim(value, mp_index, 0)

    positions = jnp.arange(length)
    self_valid = (
        (positions[None, :] <= positions[:, None])[None]
        & (positions[None, None, :] < target_len[:, None, None])
    )[:, None]
    mem_positions = jnp.arange(memory.shape[1])
    cross_valid = (mem_positions[None, :] < mine(memory_len)[:, None])[:, None, None, :]
    onehot = (
        jnp.asarray(bucket_table(length)).reshape(-1)[:, None] == jnp.arange(BUCKETS)[None, :]
    ).astype(jnp.float32)
    score_bias = (
        jnp.dot(onehot, pos_bias, precision=lax.Precision.HIGHEST)
        .reshape(length, length, heads_local)
        .transpose(2, 0, 1)[None]
    )
    cross_in = gather_mp(jnp.stack([query_cross, key_cross, value_cross]))
    cross_in = cross_in.transpose(1, 2, 0, 3).reshape(3, width, -1)
    cross_q, cross_k, cross_v = cross_in[0], cross_in[1], cross_in[2]
    cross_o = gather_mp(out_cross).reshape(-1, width)

    resid0 = targets.astype(jnp.float32)
    normed_one, inv_one = norm_forward(resid0, gain_self)
    normed_one = normed_one.astype(jnp.bfloat16)
    queries = split_heads(project(normed_one, query_self).astype(jnp.bfloat16))
    keys = split_heads(project(normed_one, key_self).astype(jnp.bfloat16))
    values = split_heads(project(normed_one, value_self).astype(jnp.bfloat16))
    mixed, log_one = attend(queries, keys, values, score_bias, self_valid)
    mixed = merge_heads(mixed).astype(jnp.bfloat16)
    resid1 = mine(resid0) + reduce_scatter(project(mixed, out_self), "mp", 0)

    mem_own = mine(memory)
    normed_two, inv_two = norm_forward(resid1, gain_cross)
    normed_two = normed_two.astype(jnp.bfloat16)
    queries_two = split_heads(project(normed_two, cross_q).astype(jnp.bfloat16))
    mem_keys = split_heads(project(mem_own, cross_k).astype(jnp.bfloat16))
    mem_values = split_heads(project(mem_own, cross_v).astype(jnp.bfloat16))
    mixed_two, log_two = attend(queries_two, mem_keys, mem_values, 0.0, cross_valid)
    mixed_two = merge_heads(mixed_two).astype(jnp.bfloat16)
    resid2 = resid1 + project(mixed_two, cross_o)
    normed_three, inv_three = norm_forward(resid2, gain_ffn)
    normed_all = gather_mp(normed_three.astype(jnp.bfloat16)[0])

    gate_pre = project(normed_all, gate_proj)
    up_pre = project(normed_all, up_proj)

    def gated(gate_in, up_in):
        return jax.nn.gelu(gate_in, approximate=True) * up_in

    hidden, hidden_pull = jax.vjp(gated, gate_pre, up_pre)
    hidden = hidden.astype(jnp.bfloat16)
    grad_gate_pre, grad_up_pre = hidden_pull(back_project(cotangent, down_proj))
    grad_gate_pre = grad_gate_pre.astype(jnp.bfloat16)
    grad_up_pre = grad_up_pre.astype(jnp.bfloat16)
    grad_normed = reduce_scatter(
        back_project(grad_gate_pre, gate_proj) + back_project(grad_up_pre, up_proj), "mp", 0
    )
    result = project(hidden, down_proj)
    own = (jnp.arange(targets.shape[0]) == mp_index)[:, None, None]
    result = result + jnp.where(own, resid2, 0.0)
    output = reduce_scatter(result, "mp", 1).astype(jnp.bfloat16)
    ffn_grads = jnp.concatenate(
        [
            weight_grad(normed_all, grad_gate_pre),
            weight_grad(normed_all, grad_up_pre),
            weight_grad(cotangent, hidden),
        ],
        1,
    )
    ffn_grads = reduce_scatter(ffn_grads, "dp", 0)
    grad_resid, grad_gain_ffn = norm_backward(resid2, inv_three, gain_ffn, grad_normed)
    grad_two = mine(cotangent).astype(jnp.float32) + grad_resid

    branch_two = grad_two.astype(jnp.bfloat16)
    grad_mixed_two = split_heads(back_project(branch_two, cross_o).astype(jnp.bfloat16))
    grad_q_two, grad_mem_keys, grad_mem_values, _ = attend_back(
        queries_two, mem_keys, mem_values, 0.0, cross_valid, log_two, grad_mixed_two
    )
    grad_q_two = merge_heads(grad_q_two).astype(jnp.bfloat16)
    grad_normed = back_project(grad_q_two, cross_q)
    grad_resid, grad_gain_cross = norm_backward(resid1, inv_two, gain_cross, grad_normed)
    grad_one = grad_two + grad_resid
    branch_one = gather_mp(grad_one.astype(jnp.bfloat16)[0])
    grad_mem_keys = merge_heads(grad_mem_keys).astype(jnp.bfloat16)
    grad_mem_values = merge_heads(grad_mem_values).astype(jnp.bfloat16)
    mem_grad = back_project(grad_mem_keys, cross_k) + back_project(grad_mem_values, cross_v)
    mem_rows = exchange_mp(mem_grad[0].astype(jnp.bfloat16))
    cross_grads = jnp.stack(
        [
            weight_grad(normed_two, grad_q_two),
            weight_grad(mem_own, grad_mem_keys),
            weight_grad(mem_own, grad_mem_values),
            weight_grad(branch_two, mixed_two),
        ],
        1,
    )
    cross_grads = reduce_scatter(cross_grads, "mp", 2)
    cross_grads = reduce_scatter(cross_grads, "dp", 0)

    grad_mixed = split_heads(back_project(branch_one, out_self).astype(jnp.bfloat16))
    grad_q_one, grad_k_one, grad_v_one, grad_scores = attend_back(
        queries, keys, values, score_bias, self_valid, log_one, grad_mixed
    )
    grad_q_one = merge_heads(grad_q_one).astype(jnp.bfloat16)
    grad_k_one = merge_heads(grad_k_one).astype(jnp.bfloat16)
    grad_v_one = merge_heads(grad_v_one).astype(jnp.bfloat16)
    score_total = jnp.sum(grad_scores.astype(jnp.float32), 0).reshape(heads_local, length * length)
    bias_local = jnp.dot(score_total, onehot, precision=lax.Precision.HIGHEST).T
    grad_normed = (
        back_project(grad_q_one, query_self)
        + back_project(grad_k_one, key_self)
        + back_project(grad_v_one, value_self)
    )
    gains = jnp.stack(
        [
            jnp.sum(grad_normed * (resid0 * inv_one), axis=(0, 1)),
            grad_gain_cross,
            grad_gain_ffn,
        ]
    )
    gains = sum_mp(gains)
    share = width // dp_size
    bias_columns = jnp.tile(bias_local.reshape(share, -1), (dp_size, 1))
    self_grads = jnp.concatenate(
        [
            weight_grad(normed_one, grad_q_one),
            weight_grad(normed_one, grad_k_one),
            weight_grad(normed_one, grad_v_one),
            weight_grad(branch_one, mixed),
            gains.T,
            bias_columns,
        ],
        1,
    )
    self_grads = reduce_scatter(self_grads, "dp", 0)
    grad_normed = reduce_scatter(grad_normed, "mp", 1)
    grad_resid, _ = norm_backward(my_rows(resid0), my_rows(inv_one), gain_self, grad_normed)
    grad_targets = (my_rows(branch_one).astype(jnp.float32) + grad_resid).astype(jnp.bfloat16)

    part = query_self.shape[1]
    units = gate_proj.shape[1]
    gains_at = 4 * part
    return (
        output,
        grad_targets,
        mem_rows,
        self_grads[:, :part],
        self_grads[:, part : 2 * part],
        self_grads[:, 2 * part : 3 * part],
        self_grads[:, 3 * part : 4 * part].T,
        cross_grads[:, 0],
        cross_grads[:, 1],
        cross_grads[:, 2],
        cross_grads[:, 3].T,
        ffn_grads[:, :units],
        ffn_grads[:, units : 2 * units],
        ffn_grads[:, 2 * units :].T,
        self_grads[:, gains_at],
        self_grads[:, gains_at + 1],
        self_grads[:, gains_at + 2],
        self_grads[:, gains_at + 3 :].reshape(bias_local.shape),
    )


def solution(mesh):
    fits = mesh.shape["dp"] == 8 and mesh.shape["mp"] == 4
    return jax.shard_map(
        on_device if fits else on_device_permutes,
        mesh=mesh,
        in_specs=(
            P("dp", None, None),
            P("dp", None, None),
            P("dp", None, None),
            P("dp"),
            P("dp"),
            P(None, "mp"),
            P(None, "mp"),
            P(None, "mp"),
            P("mp", None),
            P(None, "mp"),
            P(None, "mp"),
            P(None, "mp"),
            P("mp", None),
            P(None, "mp"),
            P(None, "mp"),
            P("mp", None),
            P(),
            P(),
            P(),
            P(None, "mp"),
        ),
        out_specs=(
            P("dp", "mp", None),
            P("dp", "mp", None),
            P("dp", "mp", None),
            P("dp", "mp"),
            P("dp", "mp"),
            P("dp", "mp"),
            P("mp", "dp"),
            P("dp", "mp"),
            P("dp", "mp"),
            P("dp", "mp"),
            P("mp", "dp"),
            P("dp", "mp"),
            P("dp", "mp"),
            P("mp", "dp"),
            P("dp"),
            P("dp"),
            P("dp"),
            P(None, "mp"),
        ),
        check_vma=False,
    )
```
